32 devices in a mesh: groups: 2 (over y), seq: 4 (over z), mp: 2 (over x), rep: 2 (over core).
Axes of the slice: x: 2, y: 2, z: 4, core: 2. Of those that a mesh axis runs over, the one named last changes fastest.
Arguments:
- query_states: bfloat16 [8, 512, 2048], P(('groups', 'mp', 'rep'), 'seq'), parts along dimension 0, may hold values from -10 to 10
- key_states: bfloat16 [8, 512, 2048], P(('groups', 'mp', 'rep'), 'seq'), parts along dimension 0, may hold values from -10 to 10
- value_states: bfloat16 [8, 512, 2048], P(('groups', 'mp', 'rep'), 'seq'), parts along dimension 0, may hold values from -6 to 6
- out_grad: bfloat16 [8, 512, 2048], P(('groups', 'mp', 'rep'), 'seq'), parts along dimension 0, may hold values from -12 to 12
- pattern: int32 [16, 4, 6], P('seq'), may hold values from 0 to 3, as said below
- counts: int32 [16, 4], P('seq'), may hold values from 1 to 6, as said below
Outputs:
- query_grad: bfloat16 [8, 512, 2048], P(('groups', 'mp', 'rep'), 'seq'), parts along dimension 0
- key_grad: bfloat16 [8, 512, 2048], P(('groups', 'mp', 'rep'), 'seq'), parts along dimension 0
- value_grad: bfloat16 [8, 512, 2048], P(('groups', 'mp', 'rep'), 'seq'), parts along dimension 0
The draws below stay inside these ranges and needn't reach their ends.
There are 2 independent parts, one for each index of `groups`. The reference program is written for one: setup_inputs(seed, part) draws one part's arguments, and reference() takes and returns one part's arrays. A program takes and returns all parts, laid end to end along the dimension named above; an argument that names none is the same for every part. Nothing has to cross between parts.
Inputs may be any that keep to these rules, and one draw needn't show every extreme that they name: pattern[h, i, 0] = i; only the first counts[h, i] entries of a row are used, and a row may name a block more than once. `counts`: the number of used entries of each row of pattern.
All inputs are finite; a program needn't handle non-finite values.
Results may differ from the reference program's by a relative error of at most 0.012.
Values may be sent and summed in bfloat16 or wider, within the bound.
No kernel may reach another device: no remote copies, remote signals or barrier semaphores. Data moves between devices by JAX's collectives and lax.ppermute only.
A program may use at most 64 MiB of HBM per device.

```python
import jax
import jax.numpy as jnp
from jax import lax

HEADS = 16
MAXK = 6
SEQ = 512
NBLK = 4
HF = 2048
WINDOWS = 4


def draw_query_states(key, part):
    key = jax.random.fold_in(key, 1)
    return jax.random.truncated_normal(key, -6.0, 6.0, (WINDOWS, SEQ, HF), jnp.float32).astype(jnp.bfloat16)


def draw_key_states(key, part):
    key = jax.random.fold_in(key, 2)
    return jax.random.truncated_normal(key, -6.0, 6.0, (WINDOWS, SEQ, HF), jnp.float32).astype(jnp.bfloat16)


def draw_pattern(key, part):
    key = jax.random.fold_in(key, 3)
    others = jax.random.randint(key, (HEADS, NBLK, MAXK - 1), 0, NBLK)
    itself = jnp.broadcast_to(jnp.arange(NBLK, dtype=jnp.int32)[None, :, None], (HEADS, NBLK, 1))
    return jnp.concatenate([itself, others.astype(jnp.int32)], axis=2)


def draw_counts(key, part):
    key = jax.random.fold_in(key, 4)
    subkeys = jax.random.split(key, 3)
    ceiling = jax.random.randint(subkeys[0], (HEADS, 1), 1, MAXK + 1)
    tallies = jax.random.randint(subkeys[1], (HEADS, NBLK), 0, 1 << 20) % ceiling + 1
    flattened = tallies.reshape(-1)
    position = jax.random.randint(subkeys[2], (), 0, HEADS * NBLK)
    flattened = flattened.at[position].set(MAXK)
    flattened = flattened.at[(position + 1) % (HEADS * NBLK)].set(1)
    return flattened.reshape(HEADS, NBLK).astype(jnp.int32)


def levels(key, extent, shards, low, high):
    factor_of = 1.0
    for dim, blocks in shards:
        draws = jax.random.uniform(jax.random.fold_in(jax.random.fold_in(key, 6), dim), (blocks,), jnp.float32, low / len(shards), high / len(shards))
        factor_of = factor_of * jnp.repeat(jnp.exp(draws), extent[dim] // blocks).reshape((-1,) + (1,) * (len(extent) - 1 - dim))
    return factor_of


def scatter_about(own_key, extent, width, bound, cuts=(), kind=jnp.bfloat16):
    array = width * jax.random.normal(own_key, extent, jnp.float32)
    if cuts:
        array = array * levels(own_key, extent, cuts, -0.22, 0.18)
    return jnp.clip(array, -bound, bound).astype(kind)


def setup_inputs(seed: int = 0, part: int = 0) -> dict:
    arg_keys = jax.random.split(jax.random.key(seed), 7)
    part_splits = jax.random.split(jax.random.fold_in(arg_keys[6], part), 7)
    query_states = draw_query_states(jax.random.fold_in(jax.random.fold_in(arg_keys[6], part), 71), part)
    key_states = draw_key_states(jax.random.fold_in(jax.random.fold_in(arg_keys[6], part), 71), part)
    value_states = scatter_about(part_splits[2], (WINDOWS, SEQ, HF), 1.0, 6.0, ((0, 4), (1, 4)))
    out_grad = scatter_about(part_splits[3], (WINDOWS, SEQ, HF), 2.0, 12.0, ((0, 4), (1, 4)))
    pattern = draw_pattern(jax.random.fold_in(arg_keys[6], 71), part)
    counts = draw_counts(jax.random.fold_in(arg_keys[6], 71), part)
    return {"query_states": query_states, "key_states": key_states, "value_states": value_states, "out_grad": out_grad, "pattern": pattern, "counts": counts}


def head_backward(operands):
    query_head, key_head, value_head, grad_head, pattern_head, count_head = operands
    number_blocks, slot_count = pattern_head.shape
    features = query_head.shape[1]
    factor = features ** -0.5
    query_blk = query_head.astype(jnp.float32).reshape(number_blocks, -1, features)
    key_blk = key_head.astype(jnp.float32).reshape(number_blocks, -1, features)
    value_blk = value_head.astype(jnp.float32).reshape(number_blocks, -1, features)
    grad_blk = grad_head.astype(jnp.float32).reshape(number_blocks, -1, features)
    key_sets = key_blk[pattern_head]
    value_sets = value_blk[pattern_head]
    active = jnp.arange(slot_count, dtype=jnp.int32)[None, :] < count_head[:, None]
    scores = jnp.einsum("iqd,ijkd->iqjk", query_blk, key_sets) * factor
    scores = jnp.where(active[:, None, :, None], scores, -jnp.inf)
    row_max = jnp.max(scores, axis=(2, 3), keepdims=True)
    exponent = jnp.exp(scores - row_max)
    probabilities = exponent / jnp.sum(exponent, axis=(2, 3), keepdims=True)
    weights = lax.optimization_barrier(probabilities.astype(jnp.bfloat16)).astype(jnp.float32)
    attended = jnp.einsum("iqjk,ijkd->iqd", weights, value_sets)
    row_delta = jnp.sum(grad_blk * attended, axis=2)
    prob_grad = jnp.einsum("iqd,ijkd->iqjk", grad_blk, value_sets)
    score_grad = probabilities * (prob_grad - row_delta[:, :, None, None])
    score_grad = lax.optimization_barrier(score_grad.astype(jnp.bfloat16)).astype(jnp.float32)
    query_sum = jnp.einsum("iqjk,ijkd->iqd", score_grad, key_sets)
    key_terms = jnp.einsum("iqjk,iqd->ijkd", score_grad, query_blk)
    value_terms = jnp.einsum("iqjk,iqd->ijkd", weights, grad_blk)
    empty_grad = jnp.zeros(query_blk.shape, jnp.float32)
    key_sum = empty_grad.at[pattern_head].add(key_terms)
    value_sum = empty_grad.at[pattern_head].add(value_terms)
    head_shape = query_head.shape
    return ((factor * query_sum).reshape(head_shape).astype(jnp.bfloat16),
            (factor * key_sum).reshape(head_shape).astype(jnp.bfloat16),
            value_sum.reshape(head_shape).astype(jnp.bfloat16))


def reference(query_states, key_states, value_states, out_grad, pattern, counts):
    windows, length, feature_total = query_states.shape
    head_count = pattern.shape[0]
    features = feature_total // head_count

    def to_heads(tensor):
        tensor = tensor.reshape(windows, length, head_count, features).transpose(0, 2, 1, 3)
        return tensor.reshape(windows * head_count, length, features)

    def to_tokens(tensor):
        tensor = tensor.reshape(windows, head_count, length, features).transpose(0, 2, 1, 3)
        return tensor.reshape(windows, length, feature_total)

    patterns = jnp.tile(pattern, (windows, 1, 1))
    tallies = jnp.tile(counts, (windows, 1))
    gradients = lax.map(head_backward, (to_heads(query_states), to_heads(key_states),
                                        to_heads(value_states), to_heads(out_grad), patterns, tallies))
    return to_tokens(gradients[0]), to_tokens(gradients[1]), to_tokens(gradients[2])
```

```python
import functools
import math

import jax
import jax.numpy as jnp
from jax import lax
from jax.experimental import pallas as pl
from jax.experimental.pallas import tpu as pltpu
from jax.sharding import PartitionSpec as P

LOG2E = math.log2(math.e)
NT = (((1,), (1,)), ((), ()))
NN = (((1,), (0,)), ((), ()))
VMEM_LIMIT = 48 * 1024 * 1024


def dot(left, right, dims=NN):
    return lax.dot_general(left, right, dims, preferred_element_type=jnp.float32)


def pack_kernel(size, width, offset, place, *refs):
    sources, outs, (held, in_sems, out_sems) = refs[:4], refs[4:-3], refs[-3:]
    position = place[0]
    total = sources[0].shape[2]
    reads, writes = [], []
    for step in range(1, size):
        start = lax.rem(position + step, size) * (total // size) + offset
        columns = pl.ds(pl.multiple_of(start, 128), width)
        reads.append(
            [
                pltpu.make_async_copy(
                    source.at[0, :, columns], held.at[step - 1, index], in_sems.at[step - 1, index]
                )
                for index, source in enumerate(sources)
            ]
        )
        writes.append(pltpu.make_async_copy(held.at[step - 1], outs[step - 1], out_sems.at[step - 1]))
    for read in sum(reads, []):
        read.start()
    for read, write in zip(reads, writes):
        for one in read:
            one.wait()
        write.start()
    for write in writes:
        write.wait()


def pack(size, width, offset, place, sources):
    tokens = sources[0].shape[1]
    return pl.pallas_call(
        functools.partial(pack_kernel, size, width, offset),
        out_shape=[jax.ShapeDtypeStruct((4, tokens, width), jnp.bfloat16)] * (size - 1),
        in_specs=[pl.BlockSpec(memory_space=pltpu.SMEM)] + [pl.BlockSpec(memory_space=pl.ANY)] * 4,
        out_specs=[pl.BlockSpec(memory_space=pl.ANY)] * (size - 1),
        scratch_shapes=[
            pltpu.VMEM((size - 1, 4, tokens, width), jnp.bfloat16),
            pltpu.SemaphoreType.DMA((size - 1, 4)),
            pltpu.SemaphoreType.DMA((size - 1,)),
        ],
        compiler_params=pltpu.CompilerParams(vmem_limit_bytes=VMEM_LIMIT),
        name="pack",
    )(place, *sources)


def heads_kernel(size, heads, first, block, place, uses, *refs):
    own_refs, far_refs = refs[:4], refs[4 : 3 + size]
    out_refs = refs[3 + size : 3 + 2 * size]
    joined, key_flip, key_sum, value_sum = refs[3 + 2 * size :]
    position = place[0]
    tokens, features = own_refs[0].shape[1], joined.shape[2]
    length = size * tokens
    blocks = length // block
    local = tokens // block
    chunk = min(length, max(2 * block, 256))
    factor = features**-0.5

    def origin(index):
        return lax.rem(position + size - index // local, size) * local + index % local

    def one_chunk(head, number):
        start = pl.multiple_of(number * chunk, chunk)
        rows = pl.ds(start, chunk)
        query, grad = joined[0, rows, :], joined[3, rows, :]
        scores = dot(joined[1], query, NT)
        prob_grad = dot(joined[2], grad, NT)
        weight_parts, score_parts = [], []
        for part in range(chunk // block):
            row = origin(number * (chunk // block) + part)
            columns = slice(part * block, (part + 1) * block)
            counts = [uses[first + head, row, origin(j)] for j in range(blocks)]
            terms = []
            for j in range(blocks):
                term = scores[j * block : (j + 1) * block, columns] * (factor * LOG2E)
                terms.append(term + jnp.where(counts[j] > 0, 0.0, -jnp.inf))
            top = functools.reduce(jnp.maximum, terms)
            top = jnp.max(top, axis=0, keepdims=True)
            exps = [jnp.exp2(term - top) for term in terms]
            grads = [prob_grad[j * block : (j + 1) * block, columns] for j in range(blocks)]
            total = sum(count * e for count, e in zip(counts, exps))
            moment = sum(count * (e * g) for count, e, g in zip(counts, exps, grads))
            inverse = 1.0 / jnp.sum(total, axis=0, keepdims=True)
            delta = jnp.sum(moment, axis=0, keepdims=True) * inverse
            probs = [e * (inverse * count) for count, e in zip(counts, exps)]
            weight_parts.append(jnp.concatenate([p.astype(jnp.bfloat16) for p in probs], axis=0))
            score_parts.append(
                jnp.concatenate(
                    [(p * (g - delta)).astype(jnp.bfloat16) for p, g in zip(probs, grads)], axis=0
                )
            )
        weights = jnp.concatenate(weight_parts, axis=1)
        score_grad = jnp.concatenate(score_parts, axis=1)
        key_sum[...] += dot(score_grad, query)
        value_sum[...] += dot(weights, grad)
        flipped = dot(key_flip[...], score_grad)
        return (flipped.T * factor).astype(jnp.bfloat16)

    for head in range(heads):
        features_at = pl.ds(head * features, features)
        for index in range(4):
            joined[index, pl.ds(0, tokens), :] = own_refs[index][0, :, features_at]
            for step in range(1, size):
                joined[index, pl.ds(step * tokens, tokens), :] = far_refs[step - 1][index, :, features_at]
        key_flip[...] = joined[1].T
        key_sum[...] = jnp.zeros_like(key_sum)
        value_sum[...] = jnp.zeros_like(value_sum)

        for number in range(length // chunk):
            query_grad = one_chunk(head, number)
            for part in range(max(1, chunk // tokens)):
                step, within = divmod(number * chunk + part * tokens, tokens)
                span = min(chunk, tokens)
                out_refs[step][0, pl.ds(within, span), features_at] = query_grad[part * span : (part + 1) * span]
        for step in range(size):
            rows = pl.ds(step * tokens, tokens)
            out_refs[step][1, :, features_at] = (factor * key_sum[rows, :]).astype(jnp.bfloat16)
            out_refs[step][2, :, features_at] = value_sum[rows, :].astype(jnp.bfloat16)


def run_heads(size, heads, first, block, place, uses, owns, fars):
    tokens = owns[0].shape[1]
    features = fars[0].shape[2] // heads
    width = heads * features
    length = size * tokens
    per_device = owns[0].shape[2] // size // width

    def own_map(place):
        return (0, 0, place[0] * per_device + first // heads)

    own_spec = pl.BlockSpec((1, tokens, width), lambda i, place: own_map(place))
    far_spec = pl.BlockSpec((4, tokens, width), lambda i, place: (0, 0, 0))
    out_spec = pl.BlockSpec((3, tokens, width), lambda i, place: (0, 0, 0))
    return pl.pallas_call(
        functools.partial(heads_kernel, size, heads, first, block),
        grid_spec=pltpu.PrefetchScalarGridSpec(
            num_scalar_prefetch=1,
            grid=(1,),
            in_specs=[pl.BlockSpec(memory_space=pltpu.SMEM)] + [own_spec] * 4 + [far_spec] * (size - 1),
            out_specs=[out_spec] * size,
            scratch_shapes=[
                pltpu.VMEM((4, length, features), jnp.bfloat16),
                pltpu.VMEM((features, length), jnp.bfloat16),
                pltpu.VMEM((length, features), jnp.float32),
                pltpu.VMEM((length, features), jnp.float32),
            ],
        ),
        out_shape=[jax.ShapeDtypeStruct((3, tokens, width), jnp.bfloat16)] * size,
        compiler_params=pltpu.CompilerParams(vmem_limit_bytes=VMEM_LIMIT),
        cost_estimate=pl.CostEstimate(
            flops=heads * 10 * length * length * features,
            bytes_accessed=heads * 14 * length * features,
            transcendentals=heads * length * length,
        ),
        name="heads",
    )(place, uses, *owns, *fars)


def place_kernel(size, groups, width, place, *refs):
    parts, outs = refs[: size * groups], refs[size * groups : -3]
    held, in_sems, out_sems = refs[-3:]
    position = place[0]
    total = outs[0].shape[2]
    reads, writes = [], []
    for step in range(size):
        start = pl.multiple_of(lax.rem(position + step, size) * (total // size), 128)
        reads.append(
            [
                pltpu.make_async_copy(
                    parts[group * size + step],
                    held.at[step, :, :, pl.ds(group * width, width)],
                    in_sems.at[step, group],
                )
                for group in range(groups)
            ]
        )
        writes.append(
            [
                pltpu.make_async_copy(
                    held.at[step, index],
                    out.at[0, :, pl.ds(start, total // size)],
                    out_sems.at[step, index],
                )
                for index, out in enumerate(outs)
            ]
        )
    for read in sum(reads, []):
        read.start()
    for read, write in zip(reads, writes):
        for one in read:
            one.wait()
        for one in write:
            one.start()
    for one in sum(writes, []):
        one.wait()


def put_in_place(size, groups, width, place, parts, shape):
    return pl.pallas_call(
        functools.partial(place_kernel, size, groups, width),
        out_shape=[jax.ShapeDtypeStruct(shape, jnp.bfloat16)] * 3,
        in_specs=[pl.BlockSpec(memory_space=pltpu.SMEM)] + [pl.BlockSpec(memory_space=pl.ANY)] * len(parts),
        out_specs=[pl.BlockSpec(memory_space=pl.ANY)] * 3,
        scratch_shapes=[
            pltpu.VMEM((size, 3, shape[1], groups * width), jnp.bfloat16),
            pltpu.SemaphoreType.DMA((size, groups)),
            pltpu.SemaphoreType.DMA((size, 3)),
        ],
        compiler_params=pltpu.CompilerParams(vmem_limit_bytes=VMEM_LIMIT),
        name="put_in_place",
    )(place, *parts)


def shards(query_states, key_states, value_states, out_grad, pattern, counts):
    size = lax.axis_size("seq")
    place = lax.axis_index("seq").astype(jnp.int32).reshape(1)
    local_heads, blocks, slots = pattern.shape
    tokens, total = query_states.shape[1:]
    features = total // (local_heads * size)
    block = tokens * size // blocks
    sources = (query_states, key_states, value_states, out_grad)

    used = jnp.arange(slots, dtype=jnp.int32) < counts[:, :, None]
    named = pattern[..., None] == jnp.arange(blocks, dtype=jnp.int32)
    uses = jnp.sum(jnp.where(used[..., None] & named, 1.0, 0.0), axis=2, dtype=jnp.float32)

    heads = 2 if local_heads % 2 == 0 else 1
    groups = local_heads // heads
    width = heads * features
    parts = []
    for group in range(groups):
        packed = pack(size, width, group * width, place, sources)
        fars = [
            lax.ppermute(packed[s - 1], "seq", [(j, (j + s) % size) for j in range(size)])
            for s in range(1, size)
        ]
        outs = run_heads(size, heads, group * heads, block, place, uses, sources, fars)
        parts.append(outs[0])
        parts += [
            lax.ppermute(outs[s], "seq", [(j, (j - s) % size) for j in range(size)])
            for s in range(1, size)
        ]
    return tuple(put_in_place(size, groups, width, place, parts, query_states.shape))


def solution(mesh):
    tokens = P(("groups", "mp", "rep"), "seq", None)
    return jax.shard_map(
        shards,
        mesh=mesh,
        in_specs=(tokens, tokens, tokens, tokens, P("seq", None, None), P("seq", None)),
        out_specs=(tokens, tokens, tokens),
        check_vma=False,
    )
```

```python
import functools
import math

import jax
import jax.numpy as jnp
from jax import lax
from jax.experimental import pallas as pl
from jax.experimental.pallas import tpu as pltpu
from jax.sharding import PartitionSpec as P

LOG2E = math.log2(math.e)
NT = (((1,), (1,)), ((), ()))
NN = (((1,), (0,)), ((), ()))
TN = (((0,), (0,)), ((), ()))
VMEM_LIMIT = 32 * 1024 * 1024
SMEM = pl.BlockSpec(memory_space=pltpu.SMEM)
ANY = pl.BlockSpec(memory_space=pl.ANY)
VMEM = pl.BlockSpec(memory_space=pltpu.VMEM)
PARAMS = pltpu.CompilerParams(vmem_limit_bytes=VMEM_LIMIT)
SIZES = ((2, 2), (3, 2), (3, 3), (4, 3), (3, 4), (4, 4), (5, 4), (5, 5), (7, 6))


def dot(left, right, dims=NN):
    return lax.dot_general(left, right, dims, preferred_element_type=jnp.float32)


def shift(array, step):
    size = lax.axis_size("seq")
    return lax.ppermute(array, "seq", [(j, (j + step) % size) for j in range(size)])


def table_kernel(heads, blocks, slots, pattern, counts, table):
    def one_row(index, carry):
        head, row = index // blocks, index % blocks
        count = counts[head, row]
        named = [jnp.where(slot < count, pattern[head, row, slot], blocks) for slot in range(slots)]
        for column in range(blocks):
            table[head, row * blocks + column] = sum((n == column).astype(jnp.int32) for n in named)
        return carry

    if heads * blocks > 16:
        lax.fori_loop(0, heads * blocks, one_row, 0)
    else:
        for index in range(heads * blocks):
            one_row(index, 0)


def count_uses(pattern, counts):
    heads, blocks, slots = pattern.shape
    return pl.pallas_call(
        functools.partial(table_kernel, heads, blocks, slots),
        out_shape=jax.ShapeDtypeStruct((heads, blocks * blocks), jnp.int32),
        in_specs=[SMEM] * 2,
        out_specs=SMEM,
        name="count_uses",
    )(pattern, counts)


class Rows:
    def __init__(self, total):
        self.slots = total
        self.lists = 2 * total
        self.tallies = self.lists + max(max(pair) for pair in SIZES)
        self.shared = self.tallies + 1
        self.spot = self.shared + 1
        self.count = -(-(self.spot + 1) // 8) * 8


def plan_kernel(size, heads, place, *refs):
    parts, (plan, choice, arrived, held, sems) = refs[:size], refs[size:]
    position = place[0]
    total, pairs = size * heads, size * size
    rows = Rows(total)
    copies = [
        pltpu.make_async_copy(part, arrived.at[step], sems.at[step]) for step, part in enumerate(parts)
    ]
    for copy in copies:
        copy.start()
    for copy in copies:
        copy.wait()
    count = arrived.shape[-1]
    for step in range(size):
        for row in range(size):
            named = arrived[step, :, row, :].astype(jnp.float32)
            held[pl.ds(step * heads, heads), pl.ds(row * count, count)] = named
    head = lax.broadcasted_iota(jnp.int32, (total, total), 0)
    place_of = lax.broadcasted_iota(jnp.int32, (total, total), 1)
    step = sum((place_of >= heads * k).astype(jnp.int32) for k in range(1, size))
    owner = position - step
    owner += jnp.where(owner < 0, size, 0)
    order = (head == owner * heads + place_of - step * heads).astype(jnp.float32)
    named = dot(order, held[...])
    head = lax.broadcasted_iota(jnp.int32, (total, pairs), 0)
    pair = lax.broadcasted_iota(jnp.int32, (total, pairs), 1)
    table = jnp.zeros((total, pairs), jnp.float32)
    for row in range(size):
        column = (pair - row * size).astype(jnp.float32)
        for slot in range(row * count, (row + 1) * count):
            table += jnp.where(column == named[:, slot : slot + 1], 1.0, 0.0)
    plan[pl.ds(0, total), :] = table.astype(jnp.int32)

    uses = (table > 0).astype(jnp.float32)
    for block in range(size):
        uses = jnp.where(pair == block * (size + 1), 0.0, uses)
    lane = lax.broadcasted_iota(jnp.int32, (1, pairs), 1)
    shared, mine = jnp.zeros((1, pairs), jnp.int32), jnp.zeros((1, 1), jnp.int32)
    number = head[:, :1].astype(jnp.float32)
    free = number >= 0
    for index in range(size):
        load = jnp.sum(uses, axis=0, keepdims=True)
        score = jnp.sum(uses * (load * load * load), axis=1, keepdims=True)
        score = jnp.where(free, score * total + number, -1.0)
        top = jnp.max(score, axis=0, keepdims=True)
        uses = jnp.where(score == top, 0.0, uses)
        free = free & (score != top)
        name = (top - total * jnp.floor(top * (1.0 / total))).astype(jnp.int32)
        shared = jnp.where(lane == index, name, shared)
        mine = jnp.where(index == position, name, mine)
    earlier = lax.broadcasted_iota(jnp.int32, (total, total), 1) < lax.broadcasted_iota(jnp.int32, (total, total), 0)
    slots = dot(earlier.astype(jnp.float32), uses)
    tallies = jnp.sum(uses, axis=0, keepdims=True)
    plan[pl.ds(rows.slots, total), :] = slots.astype(jnp.int32)
    for slot in range(rows.tallies - rows.lists):
        hit = jnp.where(slots == slot, uses * head.astype(jnp.float32), 0.0)
        plan[pl.ds(rows.lists + slot, 1), :] = jnp.sum(hit, axis=0, keepdims=True).astype(jnp.int32)
    plan[pl.ds(rows.tallies, 1), :] = tallies.astype(jnp.int32)
    plan[pl.ds(rows.shared, 1), :] = shared
    plan[pl.ds(rows.spot, 1), :] = jnp.where(lane == 0, position, mine)

    odd = functools.reduce(
        jnp.logical_or, [lane == i * size + j for i in range(size) for j in range(size) if (i - j) % 2]
    )
    most_odd = jnp.max(jnp.where(odd, tallies, 0.0)).astype(jnp.int32)
    most_even = jnp.max(jnp.where(odd, 0.0, tallies)).astype(jnp.int32)
    chosen = jnp.int32(len(SIZES))
    for index in reversed(range(len(SIZES))):
        fits = (most_odd <= SIZES[index][0]) & (most_even <= SIZES[index][1])
        chosen = jnp.where(fits, index, chosen)
    choice[0] = chosen


def make_plan(size, heads, place, parts):
    total, pairs = size * heads, size * size
    return pl.pallas_call(
        functools.partial(plan_kernel, size, heads),
        out_shape=[
            jax.ShapeDtypeStruct((Rows(total).count, pairs), jnp.int32),
            jax.ShapeDtypeStruct((1,), jnp.int32),
        ],
        in_specs=[SMEM] + [ANY] * size,
        out_specs=[VMEM, SMEM],
        scratch_shapes=[
            pltpu.VMEM((size, *parts[0].shape), jnp.int32),
            pltpu.VMEM((total, size * parts[0].shape[2]), jnp.float32),
            pltpu.SemaphoreType.DMA((size,)),
        ],
        name="make_plan",
    )(place, *parts)


def pack_kernel(size, width, row, place, starts, *refs):
    sources, outs, (held, in_sems, out_sems) = refs[:4], refs[-2 - size : -3], refs[-3:]
    position = place[0]
    reads, writes = [], []
    for step in range(1, size):
        start = starts[row, lax.rem(position + step, size)] * width
        columns = pl.ds(pl.multiple_of(start, 128), width)
        reads.append(
            [
                pltpu.make_async_copy(
                    source.at[0, :, columns], held.at[step - 1, index], in_sems.at[step - 1, index]
                )
                for index, source in enumerate(sources)
            ]
        )
        writes.append(pltpu.make_async_copy(held.at[step - 1], outs[step - 1], out_sems.at[step - 1]))
    for read in sum(reads, []):
        read.start()
    for read, write in zip(reads, writes):
        for one in read:
            one.wait()
        write.start()
    for write in writes:
        write.wait()


def pack(size, width, row, place, starts, sources, after):
    tokens = sources[0].shape[1]
    return pl.pallas_call(
        functools.partial(pack_kernel, size, width, row),
        out_shape=[jax.ShapeDtypeStruct((4, tokens, width), jnp.bfloat16)] * (size - 1),
        in_specs=[SMEM] * 2 + [ANY] * (4 + len(after)),
        out_specs=[ANY] * (size - 1),
        scratch_shapes=[
            pltpu.VMEM((size - 1, 4, tokens, width), jnp.bfloat16),
            pltpu.SemaphoreType.DMA((size - 1, 4)),
            pltpu.SemaphoreType.DMA((size - 1,)),
        ],
        compiler_params=PARAMS,
        name="pack",
    )(place, starts, *sources, *after)


def heads_kernel(size, heads, block, spot, uses, *refs):
    own_refs, far_refs = refs[:4], refs[4 : 3 + size]
    out_refs = refs[-4 - size : -4]
    joined, key_flip, key_sum, value_sum = refs[-4:]
    position, first = spot[0], spot[2]
    tokens, features = own_refs[0].shape[1], joined.shape[2]
    length = size * tokens
    blocks = length // block
    local = tokens // block
    chunk = min(length, max(2 * block, 256))
    factor = features**-0.5

    def origin(index):
        return lax.rem(position + size - index // local, size) * local + index % local

    def one_chunk(head, number):
        start = pl.multiple_of(number * chunk, chunk)
        rows = pl.ds(start, chunk)
        query, grad = joined[0, rows, :], joined[3, rows, :]
        scores = dot(joined[1], query, NT)
        prob_grad = dot(joined[2], grad, NT)
        weight_parts, score_parts = [], []
        for part in range(chunk // block):
            row = origin(number * (chunk // block) + part)
            columns = slice(part * block, (part + 1) * block)
            counts = [
                uses[first + head, row * blocks + origin(j)].astype(jnp.float32) for j in range(blocks)
            ]
            terms = []
            for j in range(blocks):
                term = scores[j * block : (j + 1) * block, columns] * (factor * LOG2E)
                terms.append(term + jnp.where(counts[j] > 0, 0.0, -jnp.inf))
            top = functools.reduce(jnp.maximum, terms)
            top = jnp.max(top, axis=0, keepdims=True)
            exps = [jnp.exp2(term - top) for term in terms]
            grads = [prob_grad[j * block : (j + 1) * block, columns] for j in range(blocks)]
            total = sum(count * e for count, e in zip(counts, exps))
            moment = sum(count * (e * g) for count, e, g in zip(counts, exps, grads))
            inverse = 1.0 / jnp.sum(total, axis=0, keepdims=True)
            delta = jnp.sum(moment, axis=0, keepdims=True) * inverse
            probs = [e * (inverse * count) for count, e in zip(counts, exps)]
            weight_parts.append(jnp.concatenate([p.astype(jnp.bfloat16) for p in probs], axis=0))
            score_parts.append(
                jnp.concatenate(
                    [(p * (g - delta)).astype(jnp.bfloat16) for p, g in zip(probs, grads)], axis=0
                )
            )
        weights = jnp.concatenate(weight_parts, axis=1)
        score_grad = jnp.concatenate(score_parts, axis=1)
        key_sum[...] += dot(score_grad, query)
        value_sum[...] += dot(weights, grad)
        flipped = dot(key_flip[...], score_grad)
        return (flipped.T * factor).astype(jnp.bfloat16)

    for head in range(heads):
        features_at = pl.ds(head * features, features)
        for index in range(4):
            joined[index, pl.ds(0, tokens), :] = own_refs[index][0, :, features_at]
            for step in range(1, size):
                joined[index, pl.ds(step * tokens, tokens), :] = far_refs[step - 1][index, :, features_at]
        key_flip[...] = joined[1].T
        key_sum[...] = jnp.zeros_like(key_sum)
        value_sum[...] = jnp.zeros_like(value_sum)

        for number in range(length // chunk):
            query_grad = one_chunk(head, number)
            for part in range(max(1, chunk // tokens)):
                step, within = divmod(number * chunk + part * tokens, tokens)
                span = min(chunk, tokens)
                out_refs[step][0, pl.ds(within, span), features_at] = query_grad[part * span : (part + 1) * span]
        for step in range(size):
            rows = pl.ds(step * tokens, tokens)
            out_refs[step][1, :, features_at] = (factor * key_sum[rows, :]).astype(jnp.bfloat16)
            out_refs[step][2, :, features_at] = value_sum[rows, :].astype(jnp.bfloat16)


def run_heads(size, heads, block, spot, uses, owns, fars, after=()):
    tokens = owns[0].shape[1]
    features = fars[0].shape[2] // heads
    width = heads * features
    length = size * tokens
    own_spec = pl.BlockSpec((1, tokens, width), lambda i, spot: (0, 0, spot[1]))
    far_spec = pl.BlockSpec((4, tokens, width), lambda i, spot: (0, 0, 0))
    out_spec = pl.BlockSpec((3, tokens, width), lambda i, spot: (0, 0, 0))
    return pl.pallas_call(
        functools.partial(heads_kernel, size, heads, block),
        grid_spec=pltpu.PrefetchScalarGridSpec(
            num_scalar_prefetch=1,
            grid=(1,),
            in_specs=[SMEM] + [own_spec] * 4 + [far_spec] * (size - 1) + [ANY] * len(after),
            out_specs=[out_spec] * size,
            scratch_shapes=[
                pltpu.VMEM((4, length, features), jnp.bfloat16),
                pltpu.VMEM((features, length), jnp.bfloat16),
                pltpu.VMEM((length, features), jnp.float32),
                pltpu.VMEM((length, features), jnp.float32),
            ],
        ),
        out_shape=[jax.ShapeDtypeStruct((3, tokens, width), jnp.bfloat16)] * size,
        compiler_params=PARAMS,
        cost_estimate=pl.CostEstimate(
            flops=heads * 10 * length * length * features,
            bytes_accessed=heads * 14 * length * features,
            transcendentals=heads * length * length,
        ),
        name="heads",
    )(spot, uses, *owns, *fars, *after)


def place_kernel(size, groups, width, place, *refs):
    parts, outs = refs[: size * groups], refs[size * groups : -3]
    held, in_sems, out_sems = refs[-3:]
    position = place[0]
    total = outs[0].shape[2]
    reads, writes = [], []
    for step in range(size):
        start = pl.multiple_of(lax.rem(position + step, size) * (total // size), 128)
        reads.append(
            [
                pltpu.make_async_copy(
                    parts[group * size + step],
                    held.at[step, :, :, pl.ds(group * width, width)],
                    in_sems.at[step, group],
                )
                for group in range(groups)
            ]
        )
        writes.append(
            [
                pltpu.make_async_copy(
                    held.at[step, index],
                    out.at[0, :, pl.ds(start, total // size)],
                    out_sems.at[step, index],
                )
                for index, out in enumerate(outs)
            ]
        )
    for read in sum(reads, []):
        read.start()
    for read, write in zip(reads, writes):
        for one in read:
            one.wait()
        for one in write:
            one.start()
    for one in sum(writes, []):
        one.wait()


def put_in_place(size, groups, width, place, parts, shape):
    return pl.pallas_call(
        functools.partial(place_kernel, size, groups, width),
        out_shape=[jax.ShapeDtypeStruct(shape, jnp.bfloat16)] * 3,
        in_specs=[SMEM] + [ANY] * len(parts),
        out_specs=[ANY] * 3,
        scratch_shapes=[
            pltpu.VMEM((size, 3, shape[1], groups * width), jnp.bfloat16),
            pltpu.SemaphoreType.DMA((size, groups)),
            pltpu.SemaphoreType.DMA((size, 3)),
        ],
        compiler_params=PARAMS,
        name="put_in_place",
    )(place, *parts)


def send_group(size, width, row, place, starts, sources, after=()):
    packed = pack(size, width, row, place, starts, sources, after)
    return [shift(packed[step - 1], step) for step in range(1, size)]


def dense_plan(size, heads, groups, block, place, uses, sources):
    features = sources[0].shape[2] // (uses.shape[0] * size)
    width = heads * features
    parts = []
    for group in range(groups):
        starts = jnp.arange(size, dtype=jnp.int32)[None] * groups + group
        spot = jnp.concatenate([place, place * groups + group, jnp.full(1, group * heads, jnp.int32)])
        fars = send_group(size, width, 0, place, starts, sources)
        outs = run_heads(size, heads, block, spot, uses, sources, fars)
        parts.append(outs[0])
        parts += [shift(outs[step], -step) for step in range(1, size)]
    return tuple(put_in_place(size, groups, width, place, parts, sources[0].shape))


class Items:
    def __init__(self, size, total, odd, even):
        self.size, self.total, self.at = size, total, Rows(total)
        self.slots = {step: odd if step % 2 else even for step in range(1, size)}
        self.first = {}
        row = self.total
        for step in range(1, size):
            self.first[step] = row
            row += self.slots[step]
        self.count = row - self.total
        self.rows = -(-row // 8) * 8


def item_pack_kernel(items, place, plan, query, grad, *outs):
    size = items.size
    position = place[0]
    features = outs[0].shape[-1]
    for step in range(1, size):
        pair = position * size + lax.rem(position + step, size)
        tally = plan[items.at.tallies, pair]
        for slot in range(items.slots[step]):
            head = jnp.where(slot < tally, plan[items.at.lists + slot, pair], 0)
            columns = columns_of(head, features)
            outs[step - 1][slot, 0] = query[0, :, columns]
            outs[step - 1][slot, 1] = grad[0, :, columns]


def item_pack(items, place, plan, query, grad):
    tokens = query.shape[1]
    features = query.shape[2] // items.total
    return pl.pallas_call(
        functools.partial(item_pack_kernel, items),
        out_shape=[
            jax.ShapeDtypeStruct((items.slots[step], 2, tokens, features), jnp.bfloat16)
            for step in range(1, items.size)
        ],
        in_specs=[SMEM] * 2 + [VMEM] * 2,
        out_specs=[VMEM] * (items.size - 1),
        compiler_params=PARAMS,
        name="item_pack",
    )(place, plan, query, grad)


def each_item(items, position, plan):
    for step in range(1, items.size):
        origin = lax.rem(position + items.size - step, items.size)
        pair = origin * items.size + position
        tally = plan[items.at.tallies, pair]
        for slot in range(items.slots[step]):
            real = slot < tally
            head = jnp.where(real, plan[items.at.lists + slot, pair], 0)
            weight = jnp.where(real, plan[head, pair], 0).astype(jnp.float32)
            yield step, slot, head, weight


def columns_of(head, features):
    if isinstance(head, int):
        return pl.ds(head * features, features)
    return pl.ds(pl.multiple_of(head * features, features), features)


def cost(blocks, products, side):
    return pl.CostEstimate(
        flops=2 * blocks * products * side**3,
        bytes_accessed=8 * blocks * side * side,
        transcendentals=blocks * side * side,
    )


def products(keys, values, queries, grads):
    factor = keys.shape[1] ** -0.5
    return dot(keys, queries, NT) * (factor * LOG2E), dot(values, grads, NT)


def one_total(scores, prob_grad):
    top = jnp.max(scores, axis=0, keepdims=True)
    exps = jnp.exp2(scores - top)
    total = jnp.sum(exps, axis=0, keepdims=True)
    moment = jnp.sum(exps * prob_grad, axis=0, keepdims=True)
    return top + jnp.log2(total), moment / total


def one_weight(scores, prob_grad, weight, log, delta):
    probs = jnp.exp2(scores - log) * weight
    return probs.astype(jnp.bfloat16), (probs * (prob_grad - delta)).astype(jnp.bfloat16)


def own_totals_kernel(items, query, key, value, grad, out, kept):
    features = query.shape[2] // items.total
    out[...] = jnp.zeros_like(out)
    for head in range(items.total):
        columns = columns_of(head, features)
        block = [ref[0, :, columns] for ref in (key, value, query, grad)]
        scores, prob_grad = products(*block)
        kept[head, 0], kept[head, 1] = scores, prob_grad
        out[0, pl.ds(head, 1), :], out[1, pl.ds(head, 1), :] = one_total(scores, prob_grad)


def run_own_totals(items, sources):
    tokens = sources[0].shape[1]
    return pl.pallas_call(
        functools.partial(own_totals_kernel, items),
        out_shape=[
            jax.ShapeDtypeStruct((2, items.total, tokens), jnp.float32),
            jax.ShapeDtypeStruct((items.total, 2, tokens, tokens), jnp.float32),
        ],
        in_specs=[VMEM] * 4,
        out_specs=[VMEM] * 2,
        compiler_params=PARAMS,
        cost_estimate=cost(items.total, 2, tokens),
        name="own_totals",
    )(*sources)


def totals_kernel(items, place, plan, key, value, own, *refs):
    far_refs, (out, kept) = refs[:-2], refs[-2:]
    features = key.shape[2] // items.total
    out[:, pl.ds(0, items.total), :] = own[...]
    index = 0
    for step, slot, head, _ in each_item(items, place[0], plan):
        columns = columns_of(head, features)
        far = far_refs[step - 1]
        row = pl.ds(items.first[step] + slot, 1)
        scores, prob_grad = products(key[0, :, columns], value[0, :, columns], far[slot, 0], far[slot, 1])
        kept[index, 0], kept[index, 1] = scores, prob_grad
        out[0, row, :], out[1, row, :] = one_total(scores, prob_grad)
        index += 1


def run_totals(items, place, plan, sources, own, fars):
    tokens = sources[0].shape[1]
    return pl.pallas_call(
        functools.partial(totals_kernel, items),
        out_shape=[
            jax.ShapeDtypeStruct((2, items.rows, tokens), jnp.float32),
            jax.ShapeDtypeStruct((items.count, 2, tokens, tokens), jnp.float32),
        ],
        in_specs=[SMEM] * 2 + [VMEM] * (2 + items.size),
        out_specs=[VMEM] * 2,
        compiler_params=PARAMS,
        cost_estimate=cost(items.count, 2, tokens),
        name="totals",
    )(place, plan, *sources[1:3], own, *fars)


def far_part(items, position, plan, back, head, origin, gap):
    column = lax.rem(position + items.size - back, items.size)
    entry = origin * items.size + column
    weight = plan[head, entry].astype(jnp.float32)
    if gap == 0:
        return weight, back, head
    return weight, back, items.first[gap] + jnp.minimum(plan[items.at.slots + head, entry], items.slots[gap] - 1)


def join(rows, totals, logs, means, shares, joined):
    for index, parts in enumerate(rows):
        at = pl.ds(index, 1)
        for part, (weight, back, row) in enumerate(parts):
            log = totals[back][0, pl.ds(row, 1), :]
            logs[part, at, :] = jnp.where(weight > 0, log, -jnp.inf)
            means[part, at, :] = totals[back][1, pl.ds(row, 1), :]
            shares[part, at, :] = jnp.broadcast_to(weight, log.shape)
    count = logs.shape[0]
    top = functools.reduce(jnp.maximum, [logs[part] for part in range(count)])
    weights = [shares[part] * jnp.exp2(logs[part] - top) for part in range(count)]
    total = sum(weights)
    joined[0] = top + jnp.log2(total)
    joined[1] = sum(weight * means[part] for part, weight in enumerate(weights)) / total


def join_scratch(items, count, tokens):
    rows = -(-count // 8) * 8
    part = pltpu.VMEM((items.size, rows, tokens), jnp.float32)
    return [part, part, part, pltpu.VMEM((2, rows, tokens), jnp.float32)]


def items_kernel(items, place, plan, key, kept, *refs):
    size = items.size
    totals, refs = refs[:size], refs[-4 - size :]
    made, item_outs, scratch = refs[0], refs[1:size], refs[size:]
    position = place[0]
    features = key.shape[2] // items.total
    factor = features**-0.5
    arrived = list(each_item(items, position, plan))
    rows = []
    for step, slot, head, weight in arrived:
        origin = lax.rem(position + size - step, size)
        parts = [(weight, 0, items.first[step] + slot)]
        for back in range(1, size):
            gap = (step - back) % size
            parts.append(far_part(items, position, plan, back, head, origin, gap))
        rows.append(parts)
    join(rows, totals, *scratch)
    joined = scratch[-1]
    for index, (step, slot, head, weight) in enumerate(arrived):
        log, delta = joined[0, pl.ds(index, 1), :], joined[1, pl.ds(index, 1), :]
        log = jnp.where(weight > 0, log, jnp.inf)
        probs, score_grad = one_weight(kept[index, 0], kept[index, 1], weight, log, delta)
        made[index, 0], made[index, 1] = probs, score_grad
        query_term = dot(score_grad, key[0, :, columns_of(head, features)], TN) * factor
        item_outs[step - 1][slot] = query_term.astype(jnp.bfloat16)


def run_items(items, place, plan, sources, kept, totals, after):
    _, tokens, width = sources[0].shape
    features = width // items.total
    outs = [jax.ShapeDtypeStruct(kept.shape, jnp.bfloat16)]
    for step in range(1, items.size):
        outs.append(jax.ShapeDtypeStruct((items.slots[step], tokens, features), jnp.bfloat16))
    return pl.pallas_call(
        functools.partial(items_kernel, items),
        out_shape=outs,
        in_specs=[SMEM] * 2 + [VMEM] * (2 + items.size) + [ANY] * len(after),
        out_specs=[VMEM] * len(outs),
        scratch_shapes=join_scratch(items, items.count, tokens),
        compiler_params=PARAMS,
        cost_estimate=cost(items.count, 5, tokens),
        name="items",
    )(place, plan, sources[1], kept, *totals, *after)


def own_kernel(items, place, plan, query, key, grad, kept, *refs):
    size = items.size
    totals, fars, made = refs[:size], refs[size : 2 * size - 1], refs[2 * size - 1]
    query_out, key_out, value_out = refs[2 * size : 2 * size + 3]
    key_sum, value_sum, own_made, *scratch = refs[2 * size + 3 :]
    position = place[0]
    features = query.shape[2] // items.total
    factor = features**-0.5
    rows = []
    for head in range(items.total):
        parts = [(plan[head, position * size + position].astype(jnp.float32), 0, head)]
        for back in range(1, size):
            parts.append(far_part(items, position, plan, back, head, position, size - back))
        rows.append(parts)
    join(rows, totals, *scratch)
    joined = scratch[-1]
    for head in range(items.total):
        log, delta = joined[0, pl.ds(head, 1), :], joined[1, pl.ds(head, 1), :]
        own_made[head, 0], own_made[head, 1] = one_weight(
            kept[head, 0], kept[head, 1], rows[head][0][0], log, delta
        )
    for head in range(items.total):
        columns = columns_of(head, features)
        key_sum[head] = dot(own_made[head, 1], query[0, :, columns])
        value_sum[head] = dot(own_made[head, 0], grad[0, :, columns])
        query_out[head] = dot(own_made[head, 1], key[0, :, columns], TN) * factor
    for index, (step, slot, head, weight) in enumerate(each_item(items, position, plan)):
        far = fars[step - 1]
        key_sum[head] += dot(made[index, 1], far[slot, 0])
        value_sum[head] += dot(made[index, 0], far[slot, 1])
    for head in range(items.total):
        columns = columns_of(head, features)
        key_out[0, :, columns] = (key_sum[head] * factor).astype(jnp.bfloat16)
        value_out[0, :, columns] = value_sum[head].astype(jnp.bfloat16)


def run_own(items, place, plan, sources, kept, totals, fars, made):
    _, tokens, width = sources[0].shape
    features = width // items.total
    each = (items.total, tokens, features)
    query, key, _, grad = sources
    return pl.pallas_call(
        functools.partial(own_kernel, items),
        out_shape=[
            jax.ShapeDtypeStruct(each, jnp.float32),
            jax.ShapeDtypeStruct(query.shape, jnp.bfloat16),
            jax.ShapeDtypeStruct(query.shape, jnp.bfloat16),
        ],
        in_specs=[SMEM] * 2 + [VMEM] * (4 + 2 * items.size),
        out_specs=[VMEM] * 3,
        scratch_shapes=[pltpu.VMEM(each, jnp.float32)] * 2
        + [pltpu.VMEM((items.total, 2, tokens, tokens), jnp.bfloat16)]
        + join_scratch(items, items.total, tokens),
        compiler_params=PARAMS,
        cost_estimate=cost(items.total + items.count, 5, tokens),
        name="own",
    )(place, plan, query, key, grad, kept, *totals, *fars, made)


def query_kernel(items, place, plan, own_query, *refs):
    size = items.size
    backs, (out, held, sems) = refs[: size - 1], refs[size - 1 :]
    position = place[0]
    features = own_query.shape[2]
    group = 4 if items.total % 4 == 0 else 1
    copies = []
    for head in range(items.total):
        total = own_query[head]
        for step in range(1, size):
            entry = position * size + lax.rem(position + step, size)
            used = plan[head, entry] > 0
            slot = jnp.minimum(plan[items.at.slots + head, entry], items.slots[step] - 1)
            total += jnp.where(used, backs[step - 1][slot].astype(jnp.float32), 0.0)
        held[:, columns_of(head, features)] = total.astype(jnp.bfloat16)
        if (head + 1) % group == 0:
            columns = pl.ds((head + 1 - group) * features, group * features)
            copies.append(
                pltpu.make_async_copy(held.at[:, columns], out.at[0, :, columns], sems.at[head])
            )
            copies[-1].start()
    for copy in copies:
        copy.wait()


def query_gradient(items, place, plan, own_query, backs, shape):
    return pl.pallas_call(
        functools.partial(query_kernel, items),
        out_shape=jax.ShapeDtypeStruct(shape, jnp.bfloat16),
        in_specs=[SMEM] * 2 + [VMEM] * items.size,
        out_specs=ANY,
        scratch_shapes=[
            pltpu.VMEM(shape[1:], jnp.bfloat16),
            pltpu.SemaphoreType.DMA((items.total,)),
        ],
        compiler_params=PARAMS,
        name="query_gradient",
    )(place, plan, own_query, *backs)


def shared_kernel(items, place, plan, *refs):
    size = items.size
    parts, outs, sems = refs[:size], refs[size + 3 : size + 6], refs[-1]
    position = place[0]
    features = parts[0].shape[2]
    copies = []
    for step in range(size):
        columns = columns_of(plan[items.at.shared, lax.rem(position + step, size)], features)
        for index, out in enumerate(outs):
            copies.append(
                pltpu.make_async_copy(
                    parts[step].at[index], out.at[0, :, columns], sems.at[step, index]
                )
            )
    for copy in copies:
        copy.start()
    for copy in copies:
        copy.wait()


def put_shared(items, place, plan, parts, grads):
    first = 2 + len(parts)
    return pl.pallas_call(
        functools.partial(shared_kernel, items),
        out_shape=[jax.ShapeDtypeStruct(grad.shape, jnp.bfloat16) for grad in grads],
        in_specs=[SMEM] * 2 + [VMEM] * len(parts) + [ANY] * 3,
        out_specs=[ANY] * 3,
        scratch_shapes=[pltpu.SemaphoreType.DMA((items.size, 3))],
        input_output_aliases={first + index: index for index in range(3)},
        compiler_params=PARAMS,
        name="put_shared",
    )(place, plan, *parts, *grads)


def items_plan(items, block, place, plan, sources):
    size = items.size
    width = sources[0].shape[2] // items.total
    packed = item_pack(items, place, plan, sources[0], sources[3])
    fars = [shift(packed[step - 1], step) for step in range(1, size)]
    shared_fars = send_group(size, width, items.at.shared, place, plan, sources, packed)
    own_totals, own_kept = run_own_totals(items, sources)
    totals, kept = run_totals(items, place, plan, sources, own_totals, fars)
    all_totals = [totals] + [shift(totals, step) for step in range(1, size)]
    made, *outs = run_items(items, place, plan, sources, kept, all_totals, shared_fars)
    backs = [shift(outs[step - 1], -step) for step in range(1, size)]
    spot = plan[items.at.spot, :3]
    parts = run_heads(size, 1, block, spot, plan, sources, shared_fars, (made,))
    parts = [parts[0]] + [shift(parts[step], -step) for step in range(1, size)]
    own_query, *light = run_own(items, place, plan, sources, own_kept, all_totals, fars, made)
    query_light = query_gradient(items, place, plan, own_query, backs, light[0].shape)
    return tuple(put_shared(items, place, plan, parts, (query_light, *light)))


def shards(query_states, key_states, value_states, out_grad, pattern, counts):
    size = lax.axis_size("seq")
    place = lax.axis_index("seq").astype(jnp.int32).reshape(1)
    heads, blocks, slots = pattern.shape
    block = query_states.shape[1] * size // blocks
    sources = (query_states, key_states, value_states, out_grad)

    def by_heads(*sources):
        uses = count_uses(pattern, counts)
        together = 2 if heads % 2 == 0 else 1
        return dense_plan(size, together, heads // together, block, place, uses, sources)

    if size > 4 or size % 2 or blocks != size or heads == 1:
        return by_heads(*sources)
    used = jnp.arange(slots, dtype=jnp.int32) < counts[:, :, None]
    named = jnp.where(used, pattern, size * blocks)
    parts = [named] + [shift(named, step) for step in range(1, size)]
    plan, choice = make_plan(size, heads, place, parts)

    def by_items(odd, even):
        items = Items(size, size * heads, odd, even)
        return lambda *sources: items_plan(items, block, place, plan, sources)

    branches = [by_items(odd, even) for odd, even in SIZES] + [by_heads]
    return lax.switch(choice[0], branches, *sources)


def solution(mesh):
    tokens = P(("groups", "mp", "rep"), "seq", None)
    return jax.shard_map(
        shards,
        mesh=mesh,
        in_specs=(tokens, tokens, tokens, tokens, P("seq", None, None), P("seq", None)),
        out_specs=(tokens, tokens, tokens),
        check_vma=False,
    )
```

```python
import functools
import math

import jax
import jax.numpy as jnp
from jax import lax
from jax.experimental import pallas as pl
from jax.experimental.pallas import tpu as pltpu
from jax.sharding import PartitionSpec as P

LOG2E = math.log2(math.e)
NT = (((1,), (1,)), ((), ()))
NN = (((1,), (0,)), ((), ()))
TN = (((0,), (0,)), ((), ()))
VMEM_LIMIT = 32 * 1024 * 1024
SMEM = pl.BlockSpec(memory_space=pltpu.SMEM)
ANY = pl.BlockSpec(memory_space=pl.ANY)
VMEM = pl.BlockSpec(memory_space=pltpu.VMEM)
PARAMS = pltpu.CompilerParams(vmem_limit_bytes=VMEM_LIMIT)
SIZES = ((3, 2), (3, 3), (4, 3), (4, 4), (5, 5))


def dot(left, right, dims=NN):
    return lax.dot_general(left, right, dims, preferred_element_type=jnp.float32)


def shift(array, step):
    size = lax.axis_size("seq")
    return lax.ppermute(array, "seq", [(j, (j + step) % size) for j in range(size)])


def table_kernel(heads, blocks, slots, pattern, counts, table):
    def one_row(index, carry):
        head, row = index // blocks, index % blocks
        count = counts[head, row]
        named = [jnp.where(slot < count, pattern[head, row, slot], blocks) for slot in range(slots)]
        for column in range(blocks):
            table[head, row * blocks + column] = sum((n == column).astype(jnp.int32) for n in named)
        return carry

    if heads * blocks > 16:
        lax.fori_loop(0, heads * blocks, one_row, 0)
    else:
        for index in range(heads * blocks):
            one_row(index, 0)


def count_uses(pattern, counts):
    heads, blocks, slots = pattern.shape
    return pl.pallas_call(
        functools.partial(table_kernel, heads, blocks, slots),
        out_shape=jax.ShapeDtypeStruct((heads, blocks * blocks), jnp.int32),
        in_specs=[SMEM] * 2,
        out_specs=SMEM,
        name="count_uses",
    )(pattern, counts)


class Rows:
    def __init__(self, total):
        self.slots = total
        self.lists = 2 * total
        self.tallies = self.lists + max(max(pair) for pair in SIZES)
        self.shared = self.tallies + 1
        self.spot = self.shared + 1
        self.count = -(-(self.spot + 1) // 8) * 8


def plan_kernel(size, heads, place, *refs):
    parts, (plan, choice, arrived, held, sems) = refs[:size], refs[size:]
    position = place[0]
    total, pairs = size * heads, size * size
    rows = Rows(total)
    copies = [
        pltpu.make_async_copy(part, arrived.at[step], sems.at[step]) for step, part in enumerate(parts)
    ]
    for copy in copies:
        copy.start()
    for copy in copies:
        copy.wait()
    count = arrived.shape[-1]
    for step in range(size):
        for row in range(size):
            named = arrived[step, :, row, :].astype(jnp.float32)
            held[pl.ds(step * heads, heads), pl.ds(row * count, count)] = named
    head = lax.broadcasted_iota(jnp.int32, (total, total), 0)
    place_of = lax.broadcasted_iota(jnp.int32, (total, total), 1)
    step = sum((place_of >= heads * k).astype(jnp.int32) for k in range(1, size))
    owner = position - step
    owner += jnp.where(owner < 0, size, 0)
    order = (head == owner * heads + place_of - step * heads).astype(jnp.float32)
    named = dot(order, held[...])
    head = lax.broadcasted_iota(jnp.int32, (total, pairs), 0)
    pair = lax.broadcasted_iota(jnp.int32, (total, pairs), 1)
    table = jnp.zeros((total, pairs), jnp.float32)
    for row in range(size):
        column = (pair - row * size).astype(jnp.float32)
        for slot in range(row * count, (row + 1) * count):
            table += jnp.where(column == named[:, slot : slot + 1], 1.0, 0.0)
    plan[pl.ds(0, total), :] = table.astype(jnp.int32)

    uses = (table > 0).astype(jnp.float32)
    for block in range(size):
        uses = jnp.where(pair == block * (size + 1), 0.0, uses)
    lane = lax.broadcasted_iota(jnp.int32, (1, pairs), 1)
    shared, mine = jnp.zeros((1, pairs), jnp.int32), jnp.zeros((1, 1), jnp.int32)
    number = head[:, :1].astype(jnp.float32)
    free = number >= 0
    for index in range(size):
        load = jnp.sum(uses, axis=0, keepdims=True)
        score = jnp.sum(uses * (load * load * load), axis=1, keepdims=True)
        score = jnp.where(free, score * total + number, -1.0)
        top = jnp.max(score, axis=0, keepdims=True)
        uses = jnp.where(score == top, 0.0, uses)
        free = free & (score != top)
        name = (top - total * jnp.floor(top * (1.0 / total))).astype(jnp.int32)
        shared = jnp.where(lane == index, name, shared)
        mine = jnp.where(index == position, name, mine)
    earlier = lax.broadcasted_iota(jnp.int32, (total, total), 1) < lax.broadcasted_iota(jnp.int32, (total, total), 0)
    slots = dot(earlier.astype(jnp.float32), uses)
    tallies = jnp.sum(uses, axis=0, keepdims=True)
    plan[pl.ds(rows.slots, total), :] = slots.astype(jnp.int32)
    for slot in range(rows.tallies - rows.lists):
        hit = jnp.where(slots == slot, uses * head.astype(jnp.float32), 0.0)
        plan[pl.ds(rows.lists + slot, 1), :] = jnp.sum(hit, axis=0, keepdims=True).astype(jnp.int32)
    plan[pl.ds(rows.tallies, 1), :] = tallies.astype(jnp.int32)
    plan[pl.ds(rows.shared, 1), :] = shared
    plan[pl.ds(rows.spot, 1), :] = jnp.where(lane == 0, position, mine)

    odd = functools.reduce(
        jnp.logical_or, [lane == i * size + j for i in range(size) for j in range(size) if (i - j) % 2]
    )
    most_odd = jnp.max(jnp.where(odd, tallies, 0.0)).astype(jnp.int32)
    most_even = jnp.max(jnp.where(odd, 0.0, tallies)).astype(jnp.int32)
    chosen = jnp.int32(len(SIZES))
    for index in reversed(range(len(SIZES))):
        fits = (most_odd <= SIZES[index][0]) & (most_even <= SIZES[index][1])
        chosen = jnp.where(fits, index, chosen)
    choice[0] = chosen


def make_plan(size, heads, place, parts):
    total, pairs = size * heads, size * size
    return pl.pallas_call(
        functools.partial(plan_kernel, size, heads),
        out_shape=[
            jax.ShapeDtypeStruct((Rows(total).count, pairs), jnp.int32),
            jax.ShapeDtypeStruct((1,), jnp.int32),
        ],
        in_specs=[SMEM] + [ANY] * size,
        out_specs=[VMEM, SMEM],
        scratch_shapes=[
            pltpu.VMEM((size, *parts[0].shape), jnp.int32),
            pltpu.VMEM((total, size * parts[0].shape[2]), jnp.float32),
            pltpu.SemaphoreType.DMA((size,)),
        ],
        name="make_plan",
    )(place, *parts)


def pack_kernel(size, width, row, place, starts, *refs):
    sources, outs, (held, in_sems, out_sems) = refs[:4], refs[-2 - size : -3], refs[-3:]
    position = place[0]
    reads, writes = [], []
    for step in range(1, size):
        start = starts[row, lax.rem(position + step, size)] * width
        columns = pl.ds(pl.multiple_of(start, 128), width)
        reads.append(
            [
                pltpu.make_async_copy(
                    source.at[0, :, columns], held.at[step - 1, index], in_sems.at[step - 1, index]
                )
                for index, source in enumerate(sources)
            ]
        )
        writes.append(pltpu.make_async_copy(held.at[step - 1], outs[step - 1], out_sems.at[step - 1]))
    for read in sum(reads, []):
        read.start()
    for read, write in zip(reads, writes):
        for one in read:
            one.wait()
        write.start()
    for write in writes:
        write.wait()


def pack(size, width, row, place, starts, sources, after):
    tokens = sources[0].shape[1]
    return pl.pallas_call(
        functools.partial(pack_kernel, size, width, row),
        out_shape=[jax.ShapeDtypeStruct((4, tokens, width), jnp.bfloat16)] * (size - 1),
        in_specs=[SMEM] * 2 + [ANY] * (4 + len(after)),
        out_specs=[ANY] * (size - 1),
        scratch_shapes=[
            pltpu.VMEM((size - 1, 4, tokens, width), jnp.bfloat16),
            pltpu.SemaphoreType.DMA((size - 1, 4)),
            pltpu.SemaphoreType.DMA((size - 1,)),
        ],
        compiler_params=PARAMS,
        name="pack",
    )(place, starts, *sources, *after)


def heads_kernel(size, heads, block, spot, uses, *refs):
    own_refs, far_refs = refs[:4], refs[4 : 3 + size]
    out_refs = refs[-4 - size : -4]
    joined, key_flip, key_sum, value_sum = refs[-4:]
    position, first = spot[0], spot[2]
    tokens, features = own_refs[0].shape[1], joined.shape[2]
    length = size * tokens
    blocks = length // block
    local = tokens // block
    chunk = min(length, max(2 * block, 256))
    factor = features**-0.5

    def origin(index):
        return lax.rem(position + size - index // local, size) * local + index % local

    def one_chunk(head, number):
        start = pl.multiple_of(number * chunk, chunk)
        rows = pl.ds(start, chunk)
        query, grad = joined[0, rows, :], joined[3, rows, :]
        scores = dot(joined[1], query, NT)
        prob_grad = dot(joined[2], grad, NT)
        weight_parts, score_parts = [], []
        for part in range(chunk // block):
            row = origin(number * (chunk // block) + part)
            columns = slice(part * block, (part + 1) * block)
            counts = [
                uses[first + head, row * blocks + origin(j)].astype(jnp.float32) for j in range(blocks)
            ]
            terms = []
            for j in range(blocks):
                term = scores[j * block : (j + 1) * block, columns] * (factor * LOG2E)
                terms.append(term + jnp.where(counts[j] > 0, 0.0, -jnp.inf))
            top = functools.reduce(jnp.maximum, terms)
            top = jnp.max(top, axis=0, keepdims=True)
            exps = [jnp.exp2(term - top) for term in terms]
            grads = [prob_grad[j * block : (j + 1) * block, columns] for j in range(blocks)]
            total = sum(count * e for count, e in zip(counts, exps))
            moment = sum(count * (e * g) for count, e, g in zip(counts, exps, grads))
            inverse = 1.0 / jnp.sum(total, axis=0, keepdims=True)
            delta = jnp.sum(moment, axis=0, keepdims=True) * inverse
            probs = [e * (inverse * count) for count, e in zip(counts, exps)]
            weight_parts.append(jnp.concatenate([p.astype(jnp.bfloat16) for p in probs], axis=0))
            score_parts.append(
                jnp.concatenate(
                    [(p * (g - delta)).astype(jnp.bfloat16) for p, g in zip(probs, grads)], axis=0
                )
            )
        weights = jnp.concatenate(weight_parts, axis=1)
        score_grad = jnp.concatenate(score_parts, axis=1)
        key_sum[...] += dot(score_grad, query)
        value_sum[...] += dot(weights, grad)
        flipped = dot(key_flip[...], score_grad)
        return (flipped.T * factor).astype(jnp.bfloat16)

    def one_head(head, carry):
        features_at = columns_of(head, features)
        for index in range(4):
            joined[index, pl.ds(0, tokens), :] = own_refs[index][0, :, features_at]
            for step in range(1, size):
                joined[index, pl.ds(step * tokens, tokens), :] = far_refs[step - 1][index, :, features_at]
        key_flip[...] = joined[1].T
        key_sum[...] = jnp.zeros_like(key_sum)
        value_sum[...] = jnp.zeros_like(value_sum)

        for number in range(length // chunk):
            query_grad = one_chunk(head, number)
            for part in range(max(1, chunk // tokens)):
                step, within = divmod(number * chunk + part * tokens, tokens)
                span = min(chunk, tokens)
                out_refs[step][0, pl.ds(within, span), features_at] = query_grad[part * span : (part + 1) * span]
        for step in range(size):
            rows = pl.ds(step * tokens, tokens)
            out_refs[step][1, :, features_at] = (factor * key_sum[rows, :]).astype(jnp.bfloat16)
            out_refs[step][2, :, features_at] = value_sum[rows, :].astype(jnp.bfloat16)
        return carry

    if heads == 1:
        one_head(0, 0)
    else:
        lax.fori_loop(0, heads, one_head, 0)


def run_heads(size, heads, block, spot, uses, owns, fars, after=()):
    tokens = owns[0].shape[1]
    features = fars[0].shape[2] // heads
    width = heads * features
    length = size * tokens
    own_spec = pl.BlockSpec((1, tokens, width), lambda i, spot: (0, 0, spot[1]))
    far_spec = pl.BlockSpec((4, tokens, width), lambda i, spot: (0, 0, 0))
    out_spec = pl.BlockSpec((3, tokens, width), lambda i, spot: (0, 0, 0))
    return pl.pallas_call(
        functools.partial(heads_kernel, size, heads, block),
        grid_spec=pltpu.PrefetchScalarGridSpec(
            num_scalar_prefetch=1,
            grid=(1,),
            in_specs=[SMEM] + [own_spec] * 4 + [far_spec] * (size - 1) + [ANY] * len(after),
            out_specs=[out_spec] * size,
            scratch_shapes=[
                pltpu.VMEM((4, length, features), jnp.bfloat16),
                pltpu.VMEM((features, length), jnp.bfloat16),
                pltpu.VMEM((length, features), jnp.float32),
                pltpu.VMEM((length, features), jnp.float32),
            ],
        ),
        out_shape=[jax.ShapeDtypeStruct((3, tokens, width), jnp.bfloat16)] * size,
        compiler_params=PARAMS,
        cost_estimate=pl.CostEstimate(
            flops=heads * 10 * length * length * features,
            bytes_accessed=heads * 14 * length * features,
            transcendentals=heads * length * length,
        ),
        name="heads",
    )(spot, uses, *owns, *fars, *after)


def place_kernel(size, groups, width, place, *refs):
    parts, outs = refs[: size * groups], refs[size * groups : -3]
    held, in_sems, out_sems = refs[-3:]
    position = place[0]
    total = outs[0].shape[2]
    reads, writes = [], []
    for step in range(size):
        start = pl.multiple_of(lax.rem(position + step, size) * (total // size), 128)
        reads.append(
            [
                pltpu.make_async_copy(
                    parts[group * size + step],
                    held.at[step, :, :, pl.ds(group * width, width)],
                    in_sems.at[step, group],
                )
                for group in range(groups)
            ]
        )
        writes.append(
            [
                pltpu.make_async_copy(
                    held.at[step, index],
                    out.at[0, :, pl.ds(start, total // size)],
                    out_sems.at[step, index],
                )
                for index, out in enumerate(outs)
            ]
        )
    for read in sum(reads, []):
        read.start()
    for read, write in zip(reads, writes):
        for one in read:
            one.wait()
        for one in write:
            one.start()
    for one in sum(writes, []):
        one.wait()


def put_in_place(size, groups, width, place, parts, shape):
    return pl.pallas_call(
        functools.partial(place_kernel, size, groups, width),
        out_shape=[jax.ShapeDtypeStruct(shape, jnp.bfloat16)] * 3,
        in_specs=[SMEM] + [ANY] * len(parts),
        out_specs=[ANY] * 3,
        scratch_shapes=[
            pltpu.VMEM((size, 3, shape[1], groups * width), jnp.bfloat16),
            pltpu.SemaphoreType.DMA((size, groups)),
            pltpu.SemaphoreType.DMA((size, 3)),
        ],
        compiler_params=PARAMS,
        name="put_in_place",
    )(place, *parts)


def send_group(size, width, row, place, starts, sources, after=()):
    packed = pack(size, width, row, place, starts, sources, after)
    return [shift(packed[step - 1], step) for step in range(1, size)]


def dense_plan(size, heads, groups, block, place, uses, sources):
    features = sources[0].shape[2] // (uses.shape[0] * size)
    width = heads * features
    parts = []
    for group in range(groups):
        starts = jnp.arange(size, dtype=jnp.int32)[None] * groups + group
        spot = jnp.concatenate([place, place * groups + group, jnp.full(1, group * heads, jnp.int32)])
        fars = send_group(size, width, 0, place, starts, sources)
        outs = run_heads(size, heads, block, spot, uses, sources, fars)
        parts.append(outs[0])
        parts += [shift(outs[step], -step) for step in range(1, size)]
    return tuple(put_in_place(size, groups, width, place, parts, sources[0].shape))


class Items:
    def __init__(self, size, total, odd, even):
        self.size, self.total, self.at = size, total, Rows(total)
        self.slots = {step: odd if step % 2 else even for step in range(1, size)}
        self.first = {}
        row = self.total
        for step in range(1, size):
            self.first[step] = row
            row += self.slots[step]
        self.count = row - self.total
        self.rows = -(-row // 8) * 8


def item_pack_kernel(items, place, plan, query, grad, *outs):
    size = items.size
    position = place[0]
    features = outs[0].shape[-1]
    for step in range(1, size):
        pair = position * size + lax.rem(position + step, size)
        tally = plan[items.at.tallies, pair]
        for slot in range(items.slots[step]):
            head = jnp.where(slot < tally, plan[items.at.lists + slot, pair], 0)
            columns = columns_of(head, features)
            outs[step - 1][slot, 0] = query[0, :, columns]
            outs[step - 1][slot, 1] = grad[0, :, columns]


def item_pack(items, place, plan, query, grad):
    tokens = query.shape[1]
    features = query.shape[2] // items.total
    return pl.pallas_call(
        functools.partial(item_pack_kernel, items),
        out_shape=[
            jax.ShapeDtypeStruct((items.slots[step], 2, tokens, features), jnp.bfloat16)
            for step in range(1, items.size)
        ],
        in_specs=[SMEM] * 2 + [VMEM] * 2,
        out_specs=[VMEM] * (items.size - 1),
        compiler_params=PARAMS,
        name="item_pack",
    )(place, plan, query, grad)


def each_item(items, position, plan):
    for step in range(1, items.size):
        origin = lax.rem(position + items.size - step, items.size)
        pair = origin * items.size + position
        tally = plan[items.at.tallies, pair]
        for slot in range(items.slots[step]):
            real = slot < tally
            head = jnp.where(real, plan[items.at.lists + slot, pair], 0)
            weight = jnp.where(real, plan[head, pair], 0).astype(jnp.float32)
            yield step, slot, head, weight


def columns_of(head, features):
    if isinstance(head, int):
        return pl.ds(head * features, features)
    return pl.ds(pl.multiple_of(head * features, features), features)


def by_groups(count, one, straight=8):
    straight = math.gcd(count, straight)

    def some(index, carry):
        for part in range(straight):
            one(index * straight + part)
        return carry

    lax.fori_loop(0, count // straight, some, 0)


def cost(blocks, products, side):
    return pl.CostEstimate(
        flops=2 * blocks * products * side**3,
        bytes_accessed=8 * blocks * side * side,
        transcendentals=blocks * side * side,
    )


def products(keys, values, queries, grads):
    factor = keys.shape[1] ** -0.5
    return dot(keys, queries, NT) * (factor * LOG2E), dot(values, grads, NT)


def one_total(scores, prob_grad):
    top = jnp.max(scores, axis=0, keepdims=True)
    exps = jnp.exp2(scores - top)
    total = jnp.sum(exps, axis=0, keepdims=True)
    moment = jnp.sum(exps * prob_grad, axis=0, keepdims=True)
    return top + jnp.log2(total), moment / total


def one_weight(scores, prob_grad, weight, log, delta):
    probs = jnp.exp2(scores - log) * weight
    return probs.astype(jnp.bfloat16), (probs * (prob_grad - delta)).astype(jnp.bfloat16)


def own_totals_kernel(total, query, key, value, grad, out, kept):
    features = query.shape[2] // total

    def one_head(head):
        columns = columns_of(head, features)
        block = [ref[0, :, columns] for ref in (key, value, query, grad)]
        scores, prob_grad = products(*block)
        kept[head, 0], kept[head, 1] = scores, prob_grad
        out[0, pl.ds(head, 1), :], out[1, pl.ds(head, 1), :] = one_total(scores, prob_grad)

    by_groups(total, one_head)


def run_own_totals(total, sources):
    tokens = sources[0].shape[1]
    return pl.pallas_call(
        functools.partial(own_totals_kernel, total),
        out_shape=[
            jax.ShapeDtypeStruct((2, total, tokens), jnp.float32),
            jax.ShapeDtypeStruct((total, 2, tokens, tokens), jnp.float32),
        ],
        in_specs=[VMEM] * 4,
        out_specs=[VMEM] * 2,
        compiler_params=PARAMS,
        cost_estimate=cost(total, 2, tokens),
        name="own_totals",
    )(*sources)


def totals_kernel(items, place, plan, key, value, own, *refs):
    far_refs, (out, kept) = refs[:-2], refs[-2:]
    features = key.shape[2] // items.total
    out[:, pl.ds(0, items.total), :] = own[...]
    index = 0
    for step, slot, head, _ in each_item(items, place[0], plan):
        columns = columns_of(head, features)
        far = far_refs[step - 1]
        row = pl.ds(items.first[step] + slot, 1)
        scores, prob_grad = products(key[0, :, columns], value[0, :, columns], far[slot, 0], far[slot, 1])
        kept[index, 0], kept[index, 1] = scores, prob_grad
        out[0, row, :], out[1, row, :] = one_total(scores, prob_grad)
        index += 1


def run_totals(items, place, plan, sources, own, fars):
    tokens = sources[0].shape[1]
    return pl.pallas_call(
        functools.partial(totals_kernel, items),
        out_shape=[
            jax.ShapeDtypeStruct((2, items.rows, tokens), jnp.float32),
            jax.ShapeDtypeStruct((items.count, 2, tokens, tokens), jnp.float32),
        ],
        in_specs=[SMEM] * 2 + [VMEM] * (2 + items.size),
        out_specs=[VMEM] * 2,
        compiler_params=PARAMS,
        cost_estimate=cost(items.count, 2, tokens),
        name="totals",
    )(place, plan, *sources[1:3], own, *fars)


def far_part(items, position, plan, back, head, origin, gap):
    column = lax.rem(position + items.size - back, items.size)
    entry = origin * items.size + column
    weight = plan[head, entry].astype(jnp.float32)
    if gap == 0:
        return weight, back, head
    return weight, back, items.first[gap] + jnp.minimum(plan[items.at.slots + head, entry], items.slots[gap] - 1)


def join(rows, totals, logs, means, shares, joined):
    for index, parts in enumerate(rows):
        at = pl.ds(index, 1)
        for part, (weight, back, row) in enumerate(parts):
            log = totals[back][0, pl.ds(row, 1), :]
            logs[part, at, :] = jnp.where(weight > 0, log, -jnp.inf)
            means[part, at, :] = totals[back][1, pl.ds(row, 1), :]
            shares[part, at, :] = jnp.broadcast_to(weight, log.shape)
    count = logs.shape[0]
    top = functools.reduce(jnp.maximum, [logs[part] for part in range(count)])
    weights = [shares[part] * jnp.exp2(logs[part] - top) for part in range(count)]
    total = sum(weights)
    joined[0] = top + jnp.log2(total)
    joined[1] = sum(weight * means[part] for part, weight in enumerate(weights)) / total


def join_scratch(items, count, tokens):
    rows = -(-count // 8) * 8
    part = pltpu.VMEM((items.size, rows, tokens), jnp.float32)
    return [part, part, part, pltpu.VMEM((2, rows, tokens), jnp.float32)]


def items_kernel(items, place, plan, key, kept, *refs):
    size = items.size
    totals, refs = refs[:size], refs[-4 - size :]
    made, item_outs, scratch = refs[0], refs[1:size], refs[size:]
    position = place[0]
    features = key.shape[2] // items.total
    factor = features**-0.5
    arrived = list(each_item(items, position, plan))
    rows = []
    for step, slot, head, weight in arrived:
        origin = lax.rem(position + size - step, size)
        parts = [(weight, 0, items.first[step] + slot)]
        for back in range(1, size):
            gap = (step - back) % size
            parts.append(far_part(items, position, plan, back, head, origin, gap))
        rows.append(parts)
    join(rows, totals, *scratch)
    joined = scratch[-1]
    for index, (step, slot, head, weight) in enumerate(arrived):
        log, delta = joined[0, pl.ds(index, 1), :], joined[1, pl.ds(index, 1), :]
        log = jnp.where(weight > 0, log, jnp.inf)
        probs, score_grad = one_weight(kept[index, 0], kept[index, 1], weight, log, delta)
        made[index, 0], made[index, 1] = probs, score_grad
        query_term = dot(score_grad, key[0, :, columns_of(head, features)], TN) * factor
        item_outs[step - 1][slot] = query_term.astype(jnp.bfloat16)


def run_items(items, place, plan, sources, kept, totals, after):
    _, tokens, width = sources[0].shape
    features = width // items.total
    outs = [jax.ShapeDtypeStruct(kept.shape, jnp.bfloat16)]
    for step in range(1, items.size):
        outs.append(jax.ShapeDtypeStruct((items.slots[step], tokens, features), jnp.bfloat16))
    return pl.pallas_call(
        functools.partial(items_kernel, items),
        out_shape=outs,
        in_specs=[SMEM] * 2 + [VMEM] * (2 + items.size) + [ANY] * len(after),
        out_specs=[VMEM] * len(outs),
        scratch_shapes=join_scratch(items, items.count, tokens),
        compiler_params=PARAMS,
        cost_estimate=cost(items.count, 5, tokens),
        name="items",
    )(place, plan, sources[1], kept, *totals, *after)


def own_kernel(items, place, plan, query, key, grad, kept, *refs):
    size = items.size
    totals, fars, made = refs[:size], refs[size : 2 * size - 1], refs[2 * size - 1]
    query_out, key_out, value_out = refs[2 * size : 2 * size + 3]
    key_sum, value_sum, *scratch = refs[2 * size + 3 :]
    position = place[0]
    features = query.shape[2] // items.total
    factor = features**-0.5
    rows = []
    for head in range(items.total):
        parts = [(plan[head, position * size + position].astype(jnp.float32), 0, head)]
        for back in range(1, size):
            parts.append(far_part(items, position, plan, back, head, position, size - back))
        rows.append(parts)
    join(rows, totals, *scratch)
    joined = scratch[-1]

    def one_head(head):
        log, delta = joined[0, pl.ds(head, 1), :], joined[1, pl.ds(head, 1), :]
        weight = plan[head, position * size + position].astype(jnp.float32)
        probs, score_grad = one_weight(kept[head, 0], kept[head, 1], weight, log, delta)
        columns = columns_of(head, features)
        key_sum[head] = dot(score_grad, query[0, :, columns])
        value_sum[head] = dot(probs, grad[0, :, columns])
        query_out[head] = dot(score_grad, key[0, :, columns], TN) * factor

    by_groups(items.total, one_head)
    for index, (step, slot, head, weight) in enumerate(each_item(items, position, plan)):
        far = fars[step - 1]
        key_sum[head] += dot(made[index, 1], far[slot, 0])
        value_sum[head] += dot(made[index, 0], far[slot, 1])

    def one_sum(head):
        columns = columns_of(head, features)
        key_out[0, :, columns] = (key_sum[head] * factor).astype(jnp.bfloat16)
        value_out[0, :, columns] = value_sum[head].astype(jnp.bfloat16)

    by_groups(items.total, one_sum)


def run_own(items, place, plan, sources, kept, totals, fars, made):
    _, tokens, width = sources[0].shape
    features = width // items.total
    each = (items.total, tokens, features)
    query, key, _, grad = sources
    return pl.pallas_call(
        functools.partial(own_kernel, items),
        out_shape=[
            jax.ShapeDtypeStruct(each, jnp.float32),
            jax.ShapeDtypeStruct(query.shape, jnp.bfloat16),
            jax.ShapeDtypeStruct(query.shape, jnp.bfloat16),
        ],
        in_specs=[SMEM] * 2 + [VMEM] * (4 + 2 * items.size),
        out_specs=[VMEM] * 3,
        scratch_shapes=[pltpu.VMEM(each, jnp.float32)] * 2
        + join_scratch(items, items.total, tokens),
        compiler_params=PARAMS,
        cost_estimate=cost(items.total + items.count, 5, tokens),
        name="own",
    )(place, plan, query, key, grad, kept, *totals, *fars, made)


def query_kernel(items, place, plan, own_query, *refs):
    size = items.size
    backs, (out, held, sems) = refs[: size - 1], refs[size - 1 :]
    position = place[0]
    features = own_query.shape[2]
    group = math.gcd(items.total, 4)

    def copy(first):
        columns = pl.ds(pl.multiple_of(first * features, 128), group * features)
        return pltpu.make_async_copy(held.at[:, columns], out.at[0, :, columns], sems.at[first // group])

    def some(index, carry):
        for part in range(group):
            head = index * group + part
            total = own_query[head]
            for step in range(1, size):
                entry = position * size + lax.rem(position + step, size)
                used = plan[head, entry] > 0
                slot = jnp.minimum(plan[items.at.slots + head, entry], items.slots[step] - 1)
                total += jnp.where(used, backs[step - 1][slot].astype(jnp.float32), 0.0)
            held[:, columns_of(head, features)] = total.astype(jnp.bfloat16)
        copy(index * group).start()
        return carry

    lax.fori_loop(0, items.total // group, some, 0)
    for first in range(0, items.total, group):
        copy(first).wait()


def query_gradient(items, place, plan, own_query, backs, shape):
    return pl.pallas_call(
        functools.partial(query_kernel, items),
        out_shape=jax.ShapeDtypeStruct(shape, jnp.bfloat16),
        in_specs=[SMEM] * 2 + [VMEM] * items.size,
        out_specs=ANY,
        scratch_shapes=[
            pltpu.VMEM(shape[1:], jnp.bfloat16),
            pltpu.SemaphoreType.DMA((items.total // math.gcd(items.total, 4),)),
        ],
        compiler_params=PARAMS,
        name="query_gradient",
    )(place, plan, own_query, *backs)


def shared_kernel(items, place, plan, *refs):
    size = items.size
    parts, outs, sems = refs[:size], refs[size + 3 : size + 6], refs[-1]
    position = place[0]
    features = parts[0].shape[2]
    copies = []
    for step in range(size):
        columns = columns_of(plan[items.at.shared, lax.rem(position + step, size)], features)
        for index, out in enumerate(outs):
            copies.append(
                pltpu.make_async_copy(
                    parts[step].at[index], out.at[0, :, columns], sems.at[step, index]
                )
            )
    for copy in copies:
        copy.start()
    for copy in copies:
        copy.wait()


def put_shared(items, place, plan, parts, grads):
    first = 2 + len(parts)
    return pl.pallas_call(
        functools.partial(shared_kernel, items),
        out_shape=[jax.ShapeDtypeStruct(grad.shape, jnp.bfloat16) for grad in grads],
        in_specs=[SMEM] * 2 + [VMEM] * len(parts) + [ANY] * 3,
        out_specs=[ANY] * 3,
        scratch_shapes=[pltpu.SemaphoreType.DMA((items.size, 3))],
        input_output_aliases={first + index: index for index in range(3)},
        compiler_params=PARAMS,
        name="put_shared",
    )(place, plan, *parts, *grads)


def items_plan(items, block, place, plan, sources):
    size = items.size
    width = sources[0].shape[2] // items.total
    packed = item_pack(items, place, plan, sources[0], sources[3])
    fars = [shift(packed[step - 1], step) for step in range(1, size)]
    shared_fars = send_group(size, width, items.at.shared, place, plan, sources, packed)
    own_totals, own_kept = run_own_totals(items.total, sources)
    totals, kept = run_totals(items, place, plan, sources, own_totals, fars)
    all_totals = [totals] + [shift(totals, step) for step in range(1, size)]
    made, *outs = run_items(items, place, plan, sources, kept, all_totals, shared_fars)
    backs = [shift(outs[step - 1], -step) for step in range(1, size)]
    spot = plan[items.at.spot, :3]
    parts = run_heads(size, 1, block, spot, plan, sources, shared_fars, (made,))
    parts = [parts[0]] + [shift(parts[step], -step) for step in range(1, size)]
    own_query, *light = run_own(items, place, plan, sources, own_kept, all_totals, fars, made)
    query_light = query_gradient(items, place, plan, own_query, backs, light[0].shape)
    return tuple(put_shared(items, place, plan, parts, (query_light, *light)))


def shards(query_states, key_states, value_states, out_grad, pattern, counts):
    size = lax.axis_size("seq")
    place = lax.axis_index("seq").astype(jnp.int32).reshape(1)
    heads, blocks, slots = pattern.shape
    block = query_states.shape[1] * size // blocks
    sources = (query_states, key_states, value_states, out_grad)

    def by_heads(*sources):
        uses = count_uses(pattern, counts)
        return dense_plan(size, heads, 1, block, place, uses, sources)

    if size > 4 or size % 2 or blocks != size or heads == 1:
        return by_heads(*sources)
    used = jnp.arange(slots, dtype=jnp.int32) < counts[:, :, None]
    named = jnp.where(used, pattern, size * blocks)
    parts = [named] + [shift(named, step) for step in range(1, size)]
    plan, choice = make_plan(size, heads, place, parts)

    def by_items(odd, even):
        items = Items(size, size * heads, odd, even)
        return lambda *sources: items_plan(items, block, place, plan, sources)

    branches = [by_items(odd, even) for odd, even in SIZES] + [by_heads]
    return lax.switch(choice[0], branches, *sources)


def solution(mesh):
    tokens = P(("groups", "mp", "rep"), "seq", None)
    return jax.shard_map(
        shards,
        mesh=mesh,
        in_specs=(tokens, tokens, tokens, tokens, P("seq", None, None), P("seq", None)),
        out_specs=(tokens, tokens, tokens),
        check_vma=False,
    )
```

```python
import functools
import math

import jax
import jax.numpy as jnp
from jax import lax
from jax.experimental import pallas as pl
from jax.experimental.pallas import tpu as pltpu
from jax.sharding import PartitionSpec as P

LOG2E = math.log2(math.e)
NT = (((1,), (1,)), ((), ()))
NN = (((1,), (0,)), ((), ()))
TN = (((0,), (0,)), ((), ()))
VMEM_LIMIT = 32 * 1024 * 1024
SMEM = pl.BlockSpec(memory_space=pltpu.SMEM)
ANY = pl.BlockSpec(memory_space=pl.ANY)
VMEM = pl.BlockSpec(memory_space=pltpu.VMEM)
PARAMS = pltpu.CompilerParams(vmem_limit_bytes=VMEM_LIMIT)
SIZES = ((3, 2), (3, 3), (4, 3), (4, 4), (5, 5))


def dot(left, right, dims=NN):
    return lax.dot_general(left, right, dims, preferred_element_type=jnp.float32)


def shift(array, step):
    size = lax.axis_size("seq")
    return lax.ppermute(array, "seq", [(j, (j + step) % size) for j in range(size)])


def table_kernel(heads, blocks, slots, pattern, counts, table):
    def one_row(index, carry):
        head, row = index // blocks, index % blocks
        count = counts[head, row]
        named = [jnp.where(slot < count, pattern[head, row, slot], blocks) for slot in range(slots)]
        for column in range(blocks):
            table[head, row * blocks + column] = sum((n == column).astype(jnp.int32) for n in named)
        return carry

    if heads * blocks > 16:
        lax.fori_loop(0, heads * blocks, one_row, 0)
    else:
        for index in range(heads * blocks):
            one_row(index, 0)


def count_uses(pattern, counts):
    heads, blocks, slots = pattern.shape
    return pl.pallas_call(
        functools.partial(table_kernel, heads, blocks, slots),
        out_shape=jax.ShapeDtypeStruct((heads, blocks * blocks), jnp.int32),
        in_specs=[SMEM] * 2,
        out_specs=SMEM,
        name="count_uses",
    )(pattern, counts)


class Rows:
    def __init__(self, total):
        self.slots = total
        self.lists = 2 * total
        self.tallies = self.lists + max(max(pair) for pair in SIZES)
        self.shared = self.tallies + 1
        self.spot = self.shared + 1
        self.count = -(-(self.spot + 1) // 8) * 8


def plan_kernel(size, heads, place, *refs):
    parts, (plan, choice, held) = refs[:size], refs[size:]
    position = place[0]
    total, pairs = size * heads, size * size
    rows = Rows(total)
    count = parts[0].shape[-1]
    for step in range(size):
        for row in range(size):
            named = parts[step][:, row, :].astype(jnp.float32)
            held[pl.ds(step * heads, heads), pl.ds(row * count, count)] = named
    head = lax.broadcasted_iota(jnp.int32, (total, total), 0)
    place_of = lax.broadcasted_iota(jnp.int32, (total, total), 1)
    step = sum((place_of >= heads * k).astype(jnp.int32) for k in range(1, size))
    owner = position - step
    owner += jnp.where(owner < 0, size, 0)
    order = (head == owner * heads + place_of - step * heads).astype(jnp.float32)
    named = dot(order, held[...])
    head = lax.broadcasted_iota(jnp.int32, (total, pairs), 0)
    pair = lax.broadcasted_iota(jnp.int32, (total, pairs), 1)
    table = jnp.zeros((total, pairs), jnp.float32)
    for row in range(size):
        column = (pair - row * size).astype(jnp.float32)
        for slot in range(row * count, (row + 1) * count):
            table += jnp.where(column == named[:, slot : slot + 1], 1.0, 0.0)
    plan[pl.ds(0, total), :] = table.astype(jnp.int32)

    uses = (table > 0).astype(jnp.float32)
    for block in range(size):
        uses = jnp.where(pair == block * (size + 1), 0.0, uses)
    lane = lax.broadcasted_iota(jnp.int32, (1, pairs), 1)
    shared, mine = jnp.zeros((1, pairs), jnp.int32), jnp.zeros((1, 1), jnp.int32)
    number = head[:, :1].astype(jnp.float32)
    free = number >= 0
    for index in range(size):
        load = jnp.sum(uses, axis=0, keepdims=True)
        score = jnp.sum(uses * (load * load * load), axis=1, keepdims=True)
        score = jnp.where(free, score * total + number, -1.0)
        top = jnp.max(score, axis=0, keepdims=True)
        uses = jnp.where(score == top, 0.0, uses)
        free = free & (score != top)
        name = (top - total * jnp.floor(top * (1.0 / total))).astype(jnp.int32)
        shared = jnp.where(lane == index, name, shared)
        mine = jnp.where(index == position, name, mine)
    earlier = lax.broadcasted_iota(jnp.int32, (total, total), 1) < lax.broadcasted_iota(jnp.int32, (total, total), 0)
    slots = dot(earlier.astype(jnp.float32), uses)
    tallies = jnp.sum(uses, axis=0, keepdims=True)
    plan[pl.ds(rows.slots, total), :] = slots.astype(jnp.int32)
    for slot in range(rows.tallies - rows.lists):
        hit = jnp.where(slots == slot, uses * head.astype(jnp.float32), 0.0)
        plan[pl.ds(rows.lists + slot, 1), :] = jnp.sum(hit, axis=0, keepdims=True).astype(jnp.int32)
    plan[pl.ds(rows.tallies, 1), :] = tallies.astype(jnp.int32)
    plan[pl.ds(rows.shared, 1), :] = shared
    plan[pl.ds(rows.spot, 1), :] = jnp.where(lane == 0, position, mine)

    odd = functools.reduce(
        jnp.logical_or, [lane == i * size + j for i in range(size) for j in range(size) if (i - j) % 2]
    )
    most_odd = jnp.max(jnp.where(odd, tallies, 0.0)).astype(jnp.int32)
    most_even = jnp.max(jnp.where(odd, 0.0, tallies)).astype(jnp.int32)
    chosen = jnp.int32(len(SIZES))
    for index in reversed(range(len(SIZES))):
        fits = (most_odd <= SIZES[index][0]) & (most_even <= SIZES[index][1])
        chosen = jnp.where(fits, index, chosen)
    choice[0] = chosen


def make_plan(size, heads, place, parts):
    total, pairs = size * heads, size * size
    return pl.pallas_call(
        functools.partial(plan_kernel, size, heads),
        out_shape=[
            jax.ShapeDtypeStruct((Rows(total).count, pairs), jnp.int32),
            jax.ShapeDtypeStruct((1,), jnp.int32),
        ],
        in_specs=[SMEM] + [VMEM] * size,
        out_specs=[VMEM, SMEM],
        scratch_shapes=[pltpu.VMEM((total, size * parts[0].shape[2]), jnp.float32)],
        name="make_plan",
    )(place, *parts)


def pack_kernel(size, width, row, place, starts, *refs):
    sources, outs, (held, in_sems, out_sems) = refs[:4], refs[-2 - size : -3], refs[-3:]
    position = place[0]
    reads, writes = [], []
    for step in range(1, size):
        start = starts[row, lax.rem(position + step, size)] * width
        columns = pl.ds(pl.multiple_of(start, 128), width)
        reads.append(
            [
                pltpu.make_async_copy(
                    source.at[0, :, columns], held.at[step - 1, index], in_sems.at[step - 1, index]
                )
                for index, source in enumerate(sources)
            ]
        )
        writes.append(pltpu.make_async_copy(held.at[step - 1], outs[step - 1], out_sems.at[step - 1]))
    for read in sum(reads, []):
        read.start()
    for read, write in zip(reads, writes):
        for one in read:
            one.wait()
        write.start()
    for write in writes:
        write.wait()


def pack(size, width, row, place, starts, sources, after):
    tokens = sources[0].shape[1]
    return pl.pallas_call(
        functools.partial(pack_kernel, size, width, row),
        out_shape=[jax.ShapeDtypeStruct((4, tokens, width), jnp.bfloat16)] * (size - 1),
        in_specs=[SMEM] * 2 + [ANY] * (4 + len(after)),
        out_specs=[ANY] * (size - 1),
        scratch_shapes=[
            pltpu.VMEM((size - 1, 4, tokens, width), jnp.bfloat16),
            pltpu.SemaphoreType.DMA((size - 1, 4)),
            pltpu.SemaphoreType.DMA((size - 1,)),
        ],
        compiler_params=PARAMS,
        name="pack",
    )(place, starts, *sources, *after)


def heads_kernel(size, heads, block, spot, uses, *refs):
    own_refs, far_refs = refs[:4], refs[4 : 3 + size]
    out_refs = refs[-4 - size : -4]
    joined, key_flip, key_sum, value_sum = refs[-4:]
    position, first = spot[0], spot[2]
    tokens, features = own_refs[0].shape[1], joined.shape[2]
    length = size * tokens
    blocks = length // block
    local = tokens // block
    chunk = min(length, max(2 * block, 256))
    factor = features**-0.5

    def origin(index):
        return lax.rem(position + size - index // local, size) * local + index % local

    def one_chunk(head, number):
        start = pl.multiple_of(number * chunk, chunk)
        rows = pl.ds(start, chunk)
        query, grad = joined[0, rows, :], joined[3, rows, :]
        scores = dot(joined[1], query, NT)
        prob_grad = dot(joined[2], grad, NT)
        weight_parts, score_parts = [], []
        for part in range(chunk // block):
            row = origin(number * (chunk // block) + part)
            columns = slice(part * block, (part + 1) * block)
            counts = [
                uses[first + head, row * blocks + origin(j)].astype(jnp.float32) for j in range(blocks)
            ]
            terms = []
            for j in range(blocks):
                term = scores[j * block : (j + 1) * block, columns] * (factor * LOG2E)
                terms.append(term + jnp.where(counts[j] > 0, 0.0, -jnp.inf))
            top = functools.reduce(jnp.maximum, terms)
            top = jnp.max(top, axis=0, keepdims=True)
            exps = [jnp.exp2(term - top) for term in terms]
            grads = [prob_grad[j * block : (j + 1) * block, columns] for j in range(blocks)]
            total = sum(count * e for count, e in zip(counts, exps))
            moment = sum(count * (e * g) for count, e, g in zip(counts, exps, grads))
            inverse = 1.0 / jnp.sum(total, axis=0, keepdims=True)
            delta = jnp.sum(moment, axis=0, keepdims=True) * inverse
            probs = [e * (inverse * count) for count, e in zip(counts, exps)]
            weight_parts.append(jnp.concatenate([p.astype(jnp.bfloat16) for p in probs], axis=0))
            score_parts.append(
                jnp.concatenate(
                    [(p * (g - delta)).astype(jnp.bfloat16) for p, g in zip(probs, grads)], axis=0
                )
            )
        weights = jnp.concatenate(weight_parts, axis=1)
        score_grad = jnp.concatenate(score_parts, axis=1)
        key_sum[...] += dot(score_grad, query)
        value_sum[...] += dot(weights, grad)
        flipped = dot(key_flip[...], score_grad)
        return (flipped.T * factor).astype(jnp.bfloat16)

    def one_head(head, carry):
        features_at = columns_of(head, features)
        for index in range(4):
            joined[index, pl.ds(0, tokens), :] = own_refs[index][0, :, features_at]
            for step in range(1, size):
                joined[index, pl.ds(step * tokens, tokens), :] = far_refs[step - 1][index, :, features_at]
        key_flip[...] = joined[1].T
        key_sum[...] = jnp.zeros_like(key_sum)
        value_sum[...] = jnp.zeros_like(value_sum)

        for number in range(length // chunk):
            query_grad = one_chunk(head, number)
            for part in range(max(1, chunk // tokens)):
                step, within = divmod(number * chunk + part * tokens, tokens)
                span = min(chunk, tokens)
                out_refs[step][0, pl.ds(within, span), features_at] = query_grad[part * span : (part + 1) * span]
        for step in range(size):
            rows = pl.ds(step * tokens, tokens)
            out_refs[step][1, :, features_at] = (factor * key_sum[rows, :]).astype(jnp.bfloat16)
            out_refs[step][2, :, features_at] = value_sum[rows, :].astype(jnp.bfloat16)
        return carry

    if heads == 1:
        one_head(0, 0)
    else:
        lax.fori_loop(0, heads, one_head, 0)


def run_heads(size, heads, block, spot, uses, owns, fars, after=()):
    tokens = owns[0].shape[1]
    features = fars[0].shape[2] // heads
    width = heads * features
    length = size * tokens
    own_spec = pl.BlockSpec((1, tokens, width), lambda i, spot: (0, 0, spot[1]))
    far_spec = pl.BlockSpec((4, tokens, width), lambda i, spot: (0, 0, 0))
    out_spec = pl.BlockSpec((3, tokens, width), lambda i, spot: (0, 0, 0))
    return pl.pallas_call(
        functools.partial(heads_kernel, size, heads, block),
        grid_spec=pltpu.PrefetchScalarGridSpec(
            num_scalar_prefetch=1,
            grid=(1,),
            in_specs=[SMEM] + [own_spec] * 4 + [far_spec] * (size - 1) + [ANY] * len(after),
            out_specs=[out_spec] * size,
            scratch_shapes=[
                pltpu.VMEM((4, length, features), jnp.bfloat16),
                pltpu.VMEM((features, length), jnp.bfloat16),
                pltpu.VMEM((length, features), jnp.float32),
                pltpu.VMEM((length, features), jnp.float32),
            ],
        ),
        out_shape=[jax.ShapeDtypeStruct((3, tokens, width), jnp.bfloat16)] * size,
        compiler_params=PARAMS,
        cost_estimate=pl.CostEstimate(
            flops=heads * 10 * length * length * features,
            bytes_accessed=heads * 14 * length * features,
            transcendentals=heads * length * length,
        ),
        name="heads",
    )(spot, uses, *owns, *fars, *after)


def place_kernel(size, groups, width, place, *refs):
    parts, outs = refs[: size * groups], refs[size * groups : -3]
    held, in_sems, out_sems = refs[-3:]
    position = place[0]
    total = outs[0].shape[2]
    reads, writes = [], []
    for step in range(size):
        start = pl.multiple_of(lax.rem(position + step, size) * (total // size), 128)
        reads.append(
            [
                pltpu.make_async_copy(
                    parts[group * size + step],
                    held.at[step, :, :, pl.ds(group * width, width)],
                    in_sems.at[step, group],
                )
                for group in range(groups)
            ]
        )
        writes.append(
            [
                pltpu.make_async_copy(
                    held.at[step, index],
                    out.at[0, :, pl.ds(start, total // size)],
                    out_sems.at[step, index],
                )
                for index, out in enumerate(outs)
            ]
        )
    for read in sum(reads, []):
        read.start()
    for read, write in zip(reads, writes):
        for one in read:
            one.wait()
        for one in write:
            one.start()
    for one in sum(writes, []):
        one.wait()


def put_in_place(size, groups, width, place, parts, shape):
    return pl.pallas_call(
        functools.partial(place_kernel, size, groups, width),
        out_shape=[jax.ShapeDtypeStruct(shape, jnp.bfloat16)] * 3,
        in_specs=[SMEM] + [ANY] * len(parts),
        out_specs=[ANY] * 3,
        scratch_shapes=[
            pltpu.VMEM((size, 3, shape[1], groups * width), jnp.bfloat16),
            pltpu.SemaphoreType.DMA((size, groups)),
            pltpu.SemaphoreType.DMA((size, 3)),
        ],
        compiler_params=PARAMS,
        name="put_in_place",
    )(place, *parts)


def send_group(size, width, row, place, starts, sources, after=()):
    packed = pack(size, width, row, place, starts, sources, after)
    return [shift(packed[step - 1], step) for step in range(1, size)]


def dense_plan(size, heads, groups, block, place, uses, sources):
    features = sources[0].shape[2] // (uses.shape[0] * size)
    width = heads * features
    parts = []
    for group in range(groups):
        starts = jnp.arange(size, dtype=jnp.int32)[None] * groups + group
        spot = jnp.concatenate([place, place * groups + group, jnp.full(1, group * heads, jnp.int32)])
        fars = send_group(size, width, 0, place, starts, sources)
        outs = run_heads(size, heads, block, spot, uses, sources, fars)
        parts.append(outs[0])
        parts += [shift(outs[step], -step) for step in range(1, size)]
    return tuple(put_in_place(size, groups, width, place, parts, sources[0].shape))


class Items:
    def __init__(self, size, total, odd, even):
        self.size, self.total, self.at = size, total, Rows(total)
        self.slots = {step: odd if step % 2 else even for step in range(1, size)}
        self.first, self.count = {}, 0
        for step in range(1, size):
            self.first[step] = self.count
            self.count += self.slots[step]
        self.rows = {step: -(-(self.slots[step] + self.count) // 8) * 8 for step in self.slots}


def item_pack_kernel(items, place, plan, query, grad, *outs):
    size = items.size
    position = place[0]
    features = outs[0].shape[-1]
    for step in range(1, size):
        pair = position * size + lax.rem(position + step, size)
        tally = plan[items.at.tallies, pair]
        for slot in range(items.slots[step]):
            head = jnp.where(slot < tally, plan[items.at.lists + slot, pair], 0)
            columns = columns_of(head, features)
            outs[step - 1][slot, 0] = query[0, :, columns]
            outs[step - 1][slot, 1] = grad[0, :, columns]


def item_pack(items, place, plan, query, grad):
    tokens = query.shape[1]
    features = query.shape[2] // items.total
    return pl.pallas_call(
        functools.partial(item_pack_kernel, items),
        out_shape=[
            jax.ShapeDtypeStruct((items.slots[step], 2, tokens, features), jnp.bfloat16)
            for step in range(1, items.size)
        ],
        in_specs=[SMEM] * 2 + [VMEM] * 2,
        out_specs=[VMEM] * (items.size - 1),
        compiler_params=PARAMS,
        name="item_pack",
    )(place, plan, query, grad)


def each_item(items, position, plan):
    for step in range(1, items.size):
        origin = lax.rem(position + items.size - step, items.size)
        pair = origin * items.size + position
        tally = plan[items.at.tallies, pair]
        for slot in range(items.slots[step]):
            real = slot < tally
            head = jnp.where(real, plan[items.at.lists + slot, pair], 0)
            weight = jnp.where(real, plan[head, pair], 0).astype(jnp.float32)
            yield step, slot, head, weight


def columns_of(head, features):
    if isinstance(head, int):
        return pl.ds(head * features, features)
    return pl.ds(pl.multiple_of(head * features, features), features)


def by_groups(count, one, straight=8):
    straight = math.gcd(count, straight)

    def some(index, carry):
        for part in range(straight):
            one(index * straight + part)
        return carry

    lax.fori_loop(0, count // straight, some, 0)


def cost(blocks, products, side):
    return pl.CostEstimate(
        flops=2 * blocks * products * side**3,
        bytes_accessed=8 * blocks * side * side,
        transcendentals=blocks * side * side,
    )


def products(keys, values, queries, grads):
    factor = keys.shape[1] ** -0.5
    return dot(keys, queries, NT) * (factor * LOG2E), dot(values, grads, NT)


def one_total(scores, prob_grad):
    top = jnp.max(scores, axis=0, keepdims=True)
    exps = jnp.exp2(scores - top)
    total = jnp.sum(exps, axis=0, keepdims=True)
    moment = jnp.sum(exps * prob_grad, axis=0, keepdims=True)
    return top + jnp.log2(total), moment / total


def one_weight(scores, prob_grad, weight, log, delta):
    probs = jnp.exp2(scores - log) * weight
    return probs.astype(jnp.bfloat16), (probs * (prob_grad - delta)).astype(jnp.bfloat16)


def own_totals_kernel(total, query, key, value, grad, out, kept):
    features = query.shape[2] // total

    def one_head(head):
        columns = columns_of(head, features)
        block = [ref[0, :, columns] for ref in (key, value, query, grad)]
        scores, prob_grad = products(*block)
        kept[head, 0], kept[head, 1] = scores, prob_grad
        out[0, pl.ds(head, 1), :], out[1, pl.ds(head, 1), :] = one_total(scores, prob_grad)

    by_groups(total, one_head)


def run_own_totals(total, sources):
    tokens = sources[0].shape[1]
    return pl.pallas_call(
        functools.partial(own_totals_kernel, total),
        out_shape=[
            jax.ShapeDtypeStruct((2, total, tokens), jnp.float32),
            jax.ShapeDtypeStruct((total, 2, tokens, tokens), jnp.float32),
        ],
        in_specs=[VMEM] * 4,
        out_specs=[VMEM] * 2,
        compiler_params=PARAMS,
        cost_estimate=cost(total, 2, tokens),
        name="own_totals",
    )(*sources)


def totals_kernel(items, place, plan, key, value, own, *refs):
    size = items.size
    far_refs, (out, kept, *packets) = refs[: size - 1], refs[size - 1 :]
    position = place[0]
    features = key.shape[2] // items.total
    for step, packet in enumerate(packets, 1):
        pair = position * size + lax.rem(position + step, size)
        tally = plan[items.at.tallies, pair]
        for slot in range(items.slots[step]):
            head = jnp.where(slot < tally, plan[items.at.lists + slot, pair], 0)
            for plane in range(2):
                packet[plane, pl.ds(slot, 1), :] = own[plane, pl.ds(head, 1), :]
    for index, (step, slot, head, _) in enumerate(each_item(items, position, plan)):
        columns = columns_of(head, features)
        far = far_refs[step - 1]
        scores, prob_grad = products(key[0, :, columns], value[0, :, columns], far[slot, 0], far[slot, 1])
        kept[index, 0], kept[index, 1] = scores, prob_grad
        for plane, total in enumerate(one_total(scores, prob_grad)):
            out[plane, pl.ds(index, 1), :] = total
            for back, packet in enumerate(packets, 1):
                packet[plane, pl.ds(items.slots[back] + index, 1), :] = total


def run_totals(items, place, plan, sources, own, fars):
    tokens = sources[0].shape[1]
    rows = [-(-items.count // 8) * 8] + [items.rows[step] for step in range(1, items.size)]
    totals = [jax.ShapeDtypeStruct((2, count, tokens), jnp.float32) for count in rows]
    kept = jax.ShapeDtypeStruct((items.count, 2, tokens, tokens), jnp.float32)
    return pl.pallas_call(
        functools.partial(totals_kernel, items),
        out_shape=[totals[0], kept, *totals[1:]],
        in_specs=[SMEM] * 2 + [VMEM] * (2 + items.size),
        out_specs=[VMEM] * (1 + items.size),
        compiler_params=PARAMS,
        cost_estimate=cost(items.count, 2, tokens),
        name="totals",
    )(place, plan, *sources[1:3], own, *fars)


def far_part(items, position, plan, back, head, origin, gap, slot=None):
    column = lax.rem(position + items.size - back, items.size)
    entry = origin * items.size + column
    weight = plan[head, entry].astype(jnp.float32)
    if gap == 0:
        return weight, back, slot
    row = jnp.minimum(plan[items.at.slots + head, entry], items.slots[gap] - 1)
    return weight, back, items.slots[back] + items.first[gap] + row


def join(rows, totals, logs, means, shares, joined):
    for index, parts in enumerate(rows):
        at = pl.ds(index, 1)
        for part, (weight, back, row) in enumerate(parts):
            log = totals[back][0, pl.ds(row, 1), :]
            logs[part, at, :] = jnp.where(weight > 0, log, -jnp.inf)
            means[part, at, :] = totals[back][1, pl.ds(row, 1), :]
            shares[part, at, :] = jnp.broadcast_to(weight, log.shape)
    count = logs.shape[0]
    top = functools.reduce(jnp.maximum, [logs[part] for part in range(count)])
    weights = [shares[part] * jnp.exp2(logs[part] - top) for part in range(count)]
    total = sum(weights)
    joined[0] = top + jnp.log2(total)
    joined[1] = sum(weight * means[part] for part, weight in enumerate(weights)) / total


def join_scratch(items, count, tokens):
    rows = -(-count // 8) * 8
    part = pltpu.VMEM((items.size, rows, tokens), jnp.float32)
    return [part, part, part, pltpu.VMEM((2, rows, tokens), jnp.float32)]


def items_kernel(items, place, plan, key, kept, *refs):
    size = items.size
    totals, refs = refs[:size], refs[-4 - size :]
    made, item_outs, scratch = refs[0], refs[1:size], refs[size:]
    position = place[0]
    features = key.shape[2] // items.total
    factor = features**-0.5
    arrived = list(each_item(items, position, plan))
    rows = []
    for index, (step, slot, head, weight) in enumerate(arrived):
        origin = lax.rem(position + size - step, size)
        parts = [(weight, 0, index)]
        for back in range(1, size):
            gap = (step - back) % size
            parts.append(far_part(items, position, plan, back, head, origin, gap, slot))
        rows.append(parts)
    join(rows, totals, *scratch)
    joined = scratch[-1]
    for index, (step, slot, head, weight) in enumerate(arrived):
        log, delta = joined[0, pl.ds(index, 1), :], joined[1, pl.ds(index, 1), :]
        log = jnp.where(weight > 0, log, jnp.inf)
        probs, score_grad = one_weight(kept[index, 0], kept[index, 1], weight, log, delta)
        made[index, 0], made[index, 1] = probs, score_grad
        query_term = dot(score_grad, key[0, :, columns_of(head, features)], TN) * factor
        item_outs[step - 1][slot] = query_term.astype(jnp.bfloat16)


def run_items(items, place, plan, sources, kept, totals, after):
    _, tokens, width = sources[0].shape
    features = width // items.total
    outs = [jax.ShapeDtypeStruct(kept.shape, jnp.bfloat16)]
    for step in range(1, items.size):
        outs.append(jax.ShapeDtypeStruct((items.slots[step], tokens, features), jnp.bfloat16))
    return pl.pallas_call(
        functools.partial(items_kernel, items),
        out_shape=outs,
        in_specs=[SMEM] * 2 + [VMEM] * (2 + items.size) + [ANY] * len(after),
        out_specs=[VMEM] * len(outs),
        scratch_shapes=join_scratch(items, items.count, tokens),
        compiler_params=PARAMS,
        cost_estimate=cost(items.count, 5, tokens),
        name="items",
    )(place, plan, sources[1], kept, *totals, *after)


def own_kernel(items, place, plan, query, key, grad, kept, *refs):
    size = items.size
    totals, fars, made = refs[:size], refs[size : 2 * size - 1], refs[2 * size - 1]
    query_out, key_out, value_out = refs[2 * size : 2 * size + 3]
    key_sum, value_sum, *scratch = refs[2 * size + 3 :]
    position = place[0]
    features = query.shape[2] // items.total
    factor = features**-0.5
    rows = []
    for head in range(items.total):
        parts = [(plan[head, position * size + position].astype(jnp.float32), 0, head)]
        for back in range(1, size):
            parts.append(far_part(items, position, plan, back, head, position, size - back))
        rows.append(parts)
    join(rows, totals, *scratch)
    joined = scratch[-1]

    def one_head(head):
        log, delta = joined[0, pl.ds(head, 1), :], joined[1, pl.ds(head, 1), :]
        weight = plan[head, position * size + position].astype(jnp.float32)
        probs, score_grad = one_weight(kept[head, 0], kept[head, 1], weight, log, delta)
        columns = columns_of(head, features)
        key_sum[head] = dot(score_grad, query[0, :, columns])
        value_sum[head] = dot(probs, grad[0, :, columns])
        query_out[head] = dot(score_grad, key[0, :, columns], TN) * factor

    by_groups(items.total, one_head)
    for index, (step, slot, head, weight) in enumerate(each_item(items, position, plan)):
        far = fars[step - 1]
        key_sum[head] += dot(made[index, 1], far[slot, 0])
        value_sum[head] += dot(made[index, 0], far[slot, 1])

    def one_sum(head):
        columns = columns_of(head, features)
        key_out[0, :, columns] = (key_sum[head] * factor).astype(jnp.bfloat16)
        value_out[0, :, columns] = value_sum[head].astype(jnp.bfloat16)

    by_groups(items.total, one_sum)


def run_own(items, place, plan, sources, kept, totals, fars, made):
    _, tokens, width = sources[0].shape
    features = width // items.total
    each = (items.total, tokens, features)
    query, key, _, grad = sources
    return pl.pallas_call(
        functools.partial(own_kernel, items),
        out_shape=[
            jax.ShapeDtypeStruct(each, jnp.float32),
            jax.ShapeDtypeStruct(query.shape, jnp.bfloat16),
            jax.ShapeDtypeStruct(query.shape, jnp.bfloat16),
        ],
        in_specs=[SMEM] * 2 + [VMEM] * (4 + 2 * items.size),
        out_specs=[VMEM] * 3,
        scratch_shapes=[pltpu.VMEM(each, jnp.float32)] * 2
        + join_scratch(items, items.total, tokens),
        compiler_params=PARAMS,
        cost_estimate=cost(items.total + items.count, 5, tokens),
        name="own",
    )(place, plan, query, key, grad, kept, *totals, *fars, made)


def query_kernel(items, place, plan, own_query, *refs):
    size = items.size
    backs, (out, held, sems) = refs[: size - 1], refs[size - 1 :]
    position = place[0]
    features = own_query.shape[2]
    group = math.gcd(items.total, 4)

    def copy(first):
        columns = pl.ds(pl.multiple_of(first * features, 128), group * features)
        return pltpu.make_async_copy(held.at[:, columns], out.at[0, :, columns], sems.at[first // group])

    def some(index, carry):
        for part in range(group):
            head = index * group + part
            total = own_query[head]
            for step in range(1, size):
                entry = position * size + lax.rem(position + step, size)
                used = plan[head, entry] > 0
                slot = jnp.minimum(plan[items.at.slots + head, entry], items.slots[step] - 1)
                total += jnp.where(used, backs[step - 1][slot].astype(jnp.float32), 0.0)
            held[:, columns_of(head, features)] = total.astype(jnp.bfloat16)
        copy(index * group).start()
        return carry

    lax.fori_loop(0, items.total // group, some, 0)
    for first in range(0, items.total, group):
        copy(first).wait()


def query_gradient(items, place, plan, own_query, backs, shape):
    return pl.pallas_call(
        functools.partial(query_kernel, items),
        out_shape=jax.ShapeDtypeStruct(shape, jnp.bfloat16),
        in_specs=[SMEM] * 2 + [VMEM] * items.size,
        out_specs=ANY,
        scratch_shapes=[
            pltpu.VMEM(shape[1:], jnp.bfloat16),
            pltpu.SemaphoreType.DMA((items.total // math.gcd(items.total, 4),)),
        ],
        compiler_params=PARAMS,
        name="query_gradient",
    )(place, plan, own_query, *backs)


def shared_kernel(items, place, plan, *refs):
    size = items.size
    parts, outs, sems = refs[:size], refs[size + 3 : size + 6], refs[-1]
    position = place[0]
    features = parts[0].shape[2]
    copies = []
    for step in range(size):
        columns = columns_of(plan[items.at.shared, lax.rem(position + step, size)], features)
        for index, out in enumerate(outs):
            copies.append(
                pltpu.make_async_copy(
                    parts[step].at[index], out.at[0, :, columns], sems.at[step, index]
                )
            )
    for copy in copies:
        copy.start()
    for copy in copies:
        copy.wait()


def put_shared(items, place, plan, parts, grads):
    first = 2 + len(parts)
    return pl.pallas_call(
        functools.partial(shared_kernel, items),
        out_shape=[jax.ShapeDtypeStruct(grad.shape, jnp.bfloat16) for grad in grads],
        in_specs=[SMEM] * 2 + [VMEM] * len(parts) + [ANY] * 3,
        out_specs=[ANY] * 3,
        scratch_shapes=[pltpu.SemaphoreType.DMA((items.size, 3))],
        input_output_aliases={first + index: index for index in range(3)},
        compiler_params=PARAMS,
        name="put_shared",
    )(place, plan, *parts, *grads)


def items_plan(items, block, place, plan, sources):
    size = items.size
    width = sources[0].shape[2] // items.total
    packed = item_pack(items, place, plan, sources[0], sources[3])
    fars = [shift(packed[step - 1], step) for step in range(1, size)]
    shared_fars = send_group(size, width, items.at.shared, place, plan, sources, packed)
    own_totals, own_kept = run_own_totals(items.total, sources)
    totals, kept, *packets = run_totals(items, place, plan, sources, own_totals, fars)
    packets = [shift(packets[step - 1], step) for step in range(1, size)]
    made, *outs = run_items(items, place, plan, sources, kept, [totals, *packets], shared_fars)
    backs = [shift(outs[step - 1], -step) for step in range(1, size)]
    spot = plan[items.at.spot, :3]
    parts = run_heads(size, 1, block, spot, plan, sources, shared_fars, (made,))
    parts = [parts[0]] + [shift(parts[step], -step) for step in range(1, size)]
    own_query, *light = run_own(items, place, plan, sources, own_kept, [own_totals, *packets], fars, made)
    query_light = query_gradient(items, place, plan, own_query, backs, light[0].shape)
    return tuple(put_shared(items, place, plan, parts, (query_light, *light)))


def shards(query_states, key_states, value_states, out_grad, pattern, counts):
    size = lax.axis_size("seq")
    place = lax.axis_index("seq").astype(jnp.int32).reshape(1)
    heads, blocks, slots = pattern.shape
    block = query_states.shape[1] * size // blocks
    sources = (query_states, key_states, value_states, out_grad)

    def by_heads(*sources):
        uses = count_uses(pattern, counts)
        return dense_plan(size, heads, 1, block, place, uses, sources)

    if size > 4 or size % 2 or blocks != size or heads == 1:
        return by_heads(*sources)
    used = jnp.arange(slots, dtype=jnp.int32) < counts[:, :, None]
    named = jnp.where(used, pattern, size * blocks)
    parts = [named] + [shift(named, step) for step in range(1, size)]
    plan, choice = make_plan(size, heads, place, parts)

    def by_items(odd, even):
        items = Items(size, size * heads, odd, even)
        return lambda *sources: items_plan(items, block, place, plan, sources)

    branches = [by_items(odd, even) for odd, even in SIZES] + [by_heads]
    return lax.switch(choice[0], branches, *sources)


def solution(mesh):
    tokens = P(("groups", "mp", "rep"), "seq", None)
    return jax.shard_map(
        shards,
        mesh=mesh,
        in_specs=(tokens, tokens, tokens, tokens, P("seq", None, None), P("seq", None)),
        out_specs=(tokens, tokens, tokens),
        check_vma=False,
    )
```

```python
import functools
import math

import jax
import jax.numpy as jnp
from jax import lax
from jax.experimental import pallas as pl
from jax.experimental.pallas import tpu as pltpu
from jax.sharding import PartitionSpec as P

LOG2E = math.log2(math.e)
NT = (((1,), (1,)), ((), ()))
NN = (((1,), (0,)), ((), ()))
TN = (((0,), (0,)), ((), ()))
VMEM_LIMIT = 32 * 1024 * 1024
SMEM = pl.BlockSpec(memory_space=pltpu.SMEM)
ANY = pl.BlockSpec(memory_space=pl.ANY)
VMEM = pl.BlockSpec(memory_space=pltpu.VMEM)
PARAMS = pltpu.CompilerParams(vmem_limit_bytes=VMEM_LIMIT)
LITTLE = pltpu.CompilerParams(vmem_limit_bytes=4 * 1024 * 1024)
SIZES = ((3, 2), (3, 3), (4, 3), (4, 4), (5, 5))


def dot(left, right, dims=NN):
    return lax.dot_general(left, right, dims, preferred_element_type=jnp.float32)


def shift(array, step):
    size = lax.axis_size("seq")
    return lax.ppermute(array, "seq", [(j, (j + step) % size) for j in range(size)])


def table_kernel(heads, blocks, slots, pattern, counts, table):
    def one_row(index, carry):
        head, row = index // blocks, index % blocks
        count = counts[head, row]
        named = [jnp.where(slot < count, pattern[head, row, slot], blocks) for slot in range(slots)]
        for column in range(blocks):
            table[head, row * blocks + column] = sum((n == column).astype(jnp.int32) for n in named)
        return carry

    if heads * blocks > 16:
        lax.fori_loop(0, heads * blocks, one_row, 0)
    else:
        for index in range(heads * blocks):
            one_row(index, 0)


def count_uses(pattern, counts):
    heads, blocks, slots = pattern.shape
    return pl.pallas_call(
        functools.partial(table_kernel, heads, blocks, slots),
        out_shape=jax.ShapeDtypeStruct((heads, blocks * blocks), jnp.int32),
        in_specs=[SMEM] * 2,
        out_specs=SMEM,
        name="count_uses",
    )(pattern, counts)


class Rows:
    def __init__(self, total):
        self.slots = total
        self.lists = 2 * total
        self.tallies = self.lists + max(max(pair) for pair in SIZES)
        self.shared = self.tallies + 1
        self.spot = self.shared + 1
        self.count = -(-(self.spot + 1) // 8) * 8


def plan_kernel(size, heads, place, *refs):
    parts, (plan, choice, held) = refs[:size], refs[size:]
    position = place[0]
    total, pairs = size * heads, size * size
    rows = Rows(total)
    count = parts[0].shape[-1]
    for step in range(size):
        for row in range(size):
            named = parts[step][:, row, :].astype(jnp.float32)
            held[pl.ds(step * heads, heads), pl.ds(row * count, count)] = named
    head = lax.broadcasted_iota(jnp.int32, (total, total), 0)
    place_of = lax.broadcasted_iota(jnp.int32, (total, total), 1)
    step = sum((place_of >= heads * k).astype(jnp.int32) for k in range(1, size))
    owner = position - step
    owner += jnp.where(owner < 0, size, 0)
    order = (head == owner * heads + place_of - step * heads).astype(jnp.float32)
    named = dot(order, held[...])
    head = lax.broadcasted_iota(jnp.int32, (total, pairs), 0)
    pair = lax.broadcasted_iota(jnp.int32, (total, pairs), 1)
    table = jnp.zeros((total, pairs), jnp.float32)
    for row in range(size):
        column = (pair - row * size).astype(jnp.float32)
        for slot in range(row * count, (row + 1) * count):
            table += jnp.where(column == named[:, slot : slot + 1], 1.0, 0.0)
    plan[pl.ds(0, total), :] = table.astype(jnp.int32)

    uses = (table > 0).astype(jnp.float32)
    for block in range(size):
        uses = jnp.where(pair == block * (size + 1), 0.0, uses)
    lane = lax.broadcasted_iota(jnp.int32, (1, pairs), 1)
    shared, mine = jnp.zeros((1, pairs), jnp.int32), jnp.zeros((1, 1), jnp.int32)
    number = head[:, :1].astype(jnp.float32)
    free = number >= 0
    for index in range(size):
        load = jnp.sum(uses, axis=0, keepdims=True)
        score = jnp.sum(uses * (load * load * load), axis=1, keepdims=True)
        score = jnp.where(free, score * total + number, -1.0)
        top = jnp.max(score, axis=0, keepdims=True)
        uses = jnp.where(score == top, 0.0, uses)
        free = free & (score != top)
        name = (top - total * jnp.floor(top * (1.0 / total))).astype(jnp.int32)
        shared = jnp.where(lane == index, name, shared)
        mine = jnp.where(index == position, name, mine)
    earlier = lax.broadcasted_iota(jnp.int32, (total, total), 1) < lax.broadcasted_iota(jnp.int32, (total, total), 0)
    slots = dot(earlier.astype(jnp.float32), uses)
    tallies = jnp.sum(uses, axis=0, keepdims=True)
    plan[pl.ds(rows.slots, total), :] = slots.astype(jnp.int32)
    for slot in range(rows.tallies - rows.lists):
        hit = jnp.where(slots == slot, uses * head.astype(jnp.float32), 0.0)
        plan[pl.ds(rows.lists + slot, 1), :] = jnp.sum(hit, axis=0, keepdims=True).astype(jnp.int32)
    plan[pl.ds(rows.tallies, 1), :] = tallies.astype(jnp.int32)
    plan[pl.ds(rows.shared, 1), :] = shared
    plan[pl.ds(rows.spot, 1), :] = jnp.where(lane == 0, position, mine)

    odd = functools.reduce(
        jnp.logical_or, [lane == i * size + j for i in range(size) for j in range(size) if (i - j) % 2]
    )
    most_odd = jnp.max(jnp.where(odd, tallies, 0.0)).astype(jnp.int32)
    most_even = jnp.max(jnp.where(odd, 0.0, tallies)).astype(jnp.int32)
    chosen = jnp.int32(len(SIZES))
    for index in reversed(range(len(SIZES))):
        fits = (most_odd <= SIZES[index][0]) & (most_even <= SIZES[index][1])
        chosen = jnp.where(fits, index, chosen)
    choice[0] = chosen


def make_plan(size, heads, place, parts):
    total, pairs = size * heads, size * size
    return pl.pallas_call(
        functools.partial(plan_kernel, size, heads),
        out_shape=[
            jax.ShapeDtypeStruct((Rows(total).count, pairs), jnp.int32),
            jax.ShapeDtypeStruct((1,), jnp.int32),
        ],
        in_specs=[SMEM] + [VMEM] * size,
        out_specs=[VMEM, SMEM],
        scratch_shapes=[pltpu.VMEM((total, size * parts[0].shape[2]), jnp.float32)],
        compiler_params=LITTLE,
        name="make_plan",
    )(place, *parts)


def pack_kernel(size, width, row, place, starts, *refs):
    sources, outs, (held, in_sems, out_sems) = refs[:4], refs[-2 - size : -3], refs[-3:]
    position = place[0]
    reads, writes = [], []
    for step in range(1, size):
        start = starts[row, lax.rem(position + step, size)] * width
        columns = pl.ds(pl.multiple_of(start, 128), width)
        reads.append(
            [
                pltpu.make_async_copy(
                    source.at[0, :, columns], held.at[step - 1, index], in_sems.at[step - 1, index]
                )
                for index, source in enumerate(sources)
            ]
        )
        writes.append(pltpu.make_async_copy(held.at[step - 1], outs[step - 1], out_sems.at[step - 1]))
    for read in sum(reads, []):
        read.start()
    for read, write in zip(reads, writes):
        for one in read:
            one.wait()
        write.start()
    for write in writes:
        write.wait()


def pack(size, width, row, place, starts, sources, after):
    tokens = sources[0].shape[1]
    return pl.pallas_call(
        functools.partial(pack_kernel, size, width, row),
        out_shape=[jax.ShapeDtypeStruct((4, tokens, width), jnp.bfloat16)] * (size - 1),
        in_specs=[SMEM] * 2 + [ANY] * (4 + len(after)),
        out_specs=[ANY] * (size - 1),
        scratch_shapes=[
            pltpu.VMEM((size - 1, 4, tokens, width), jnp.bfloat16),
            pltpu.SemaphoreType.DMA((size - 1, 4)),
            pltpu.SemaphoreType.DMA((size - 1,)),
        ],
        compiler_params=PARAMS,
        name="pack",
    )(place, starts, *sources, *after)


def heads_kernel(size, heads, block, spot, uses, *refs):
    own_refs, far_refs = refs[:4], refs[4 : 3 + size]
    out_refs = refs[-4 - size : -4]
    joined, key_flip, key_sum, value_sum = refs[-4:]
    position, first = spot[0], spot[2]
    tokens, features = own_refs[0].shape[1], joined.shape[2]
    length = size * tokens
    blocks = length // block
    local = tokens // block
    chunk = min(length, max(2 * block, 256))
    factor = features**-0.5

    def origin(index):
        return lax.rem(position + size - index // local, size) * local + index % local

    def one_chunk(head, number):
        start = pl.multiple_of(number * chunk, chunk)
        rows = pl.ds(start, chunk)
        query, grad = joined[0, rows, :], joined[3, rows, :]
        scores = dot(joined[1], query, NT)
        prob_grad = dot(joined[2], grad, NT)
        weight_parts, score_parts = [], []
        for part in range(chunk // block):
            row = origin(number * (chunk // block) + part)
            columns = slice(part * block, (part + 1) * block)
            counts = [
                uses[first + head, row * blocks + origin(j)].astype(jnp.float32) for j in range(blocks)
            ]
            terms = []
            for j in range(blocks):
                term = scores[j * block : (j + 1) * block, columns] * (factor * LOG2E)
                terms.append(term + jnp.where(counts[j] > 0, 0.0, -jnp.inf))
            top = functools.reduce(jnp.maximum, terms)
            top = jnp.max(top, axis=0, keepdims=True)
            exps = [jnp.exp2(term - top) for term in terms]
            grads = [prob_grad[j * block : (j + 1) * block, columns] for j in range(blocks)]
            total = sum(count * e for count, e in zip(counts, exps))
            moment = sum(count * (e * g) for count, e, g in zip(counts, exps, grads))
            inverse = 1.0 / jnp.sum(total, axis=0, keepdims=True)
            delta = jnp.sum(moment, axis=0, keepdims=True) * inverse
            probs = [e * (inverse * count) for count, e in zip(counts, exps)]
            weight_parts.append(jnp.concatenate([p.astype(jnp.bfloat16) for p in probs], axis=0))
            score_parts.append(
                jnp.concatenate(
                    [(p * (g - delta)).astype(jnp.bfloat16) for p, g in zip(probs, grads)], axis=0
                )
            )
        weights = jnp.concatenate(weight_parts, axis=1)
        score_grad = jnp.concatenate(score_parts, axis=1)
        key_sum[...] += dot(score_grad, query)
        value_sum[...] += dot(weights, grad)
        flipped = dot(key_flip[...], score_grad)
        return (flipped.T * factor).astype(jnp.bfloat16)

    def one_head(head, carry):
        features_at = columns_of(head, features)
        for index in range(4):
            joined[index, pl.ds(0, tokens), :] = own_refs[index][0, :, features_at]
            for step in range(1, size):
                joined[index, pl.ds(step * tokens, tokens), :] = far_refs[step - 1][index, :, features_at]
        key_flip[...] = joined[1].T
        key_sum[...] = jnp.zeros_like(key_sum)
        value_sum[...] = jnp.zeros_like(value_sum)

        for number in range(length // chunk):
            query_grad = one_chunk(head, number)
            for part in range(max(1, chunk // tokens)):
                step, within = divmod(number * chunk + part * tokens, tokens)
                span = min(chunk, tokens)
                out_refs[step][0, pl.ds(within, span), features_at] = query_grad[part * span : (part + 1) * span]
        for step in range(size):
            rows = pl.ds(step * tokens, tokens)
            out_refs[step][1, :, features_at] = (factor * key_sum[rows, :]).astype(jnp.bfloat16)
            out_refs[step][2, :, features_at] = value_sum[rows, :].astype(jnp.bfloat16)
        return carry

    if heads == 1:
        one_head(0, 0)
    else:
        lax.fori_loop(0, heads, one_head, 0)


def run_heads(size, heads, block, spot, uses, owns, fars, after=()):
    tokens = owns[0].shape[1]
    features = fars[0].shape[2] // heads
    width = heads * features
    length = size * tokens
    own_spec = pl.BlockSpec((1, tokens, width), lambda i, spot: (0, 0, spot[1]))
    far_spec = pl.BlockSpec((4, tokens, width), lambda i, spot: (0, 0, 0))
    out_spec = pl.BlockSpec((3, tokens, width), lambda i, spot: (0, 0, 0))
    return pl.pallas_call(
        functools.partial(heads_kernel, size, heads, block),
        grid_spec=pltpu.PrefetchScalarGridSpec(
            num_scalar_prefetch=1,
            grid=(1,),
            in_specs=[SMEM] + [own_spec] * 4 + [far_spec] * (size - 1) + [ANY] * len(after),
            out_specs=[out_spec] * size,
            scratch_shapes=[
                pltpu.VMEM((4, length, features), jnp.bfloat16),
                pltpu.VMEM((features, length), jnp.bfloat16),
                pltpu.VMEM((length, features), jnp.float32),
                pltpu.VMEM((length, features), jnp.float32),
            ],
        ),
        out_shape=[jax.ShapeDtypeStruct((3, tokens, width), jnp.bfloat16)] * size,
        compiler_params=PARAMS,
        cost_estimate=pl.CostEstimate(
            flops=heads * 10 * length * length * features,
            bytes_accessed=heads * 14 * length * features,
            transcendentals=heads * length * length,
        ),
        name="heads",
    )(spot, uses, *owns, *fars, *after)


def place_kernel(size, groups, width, place, *refs):
    parts, outs = refs[: size * groups], refs[size * groups : -3]
    held, in_sems, out_sems = refs[-3:]
    position = place[0]
    total = outs[0].shape[2]
    reads, writes = [], []
    for step in range(size):
        start = pl.multiple_of(lax.rem(position + step, size) * (total // size), 128)
        reads.append(
            [
                pltpu.make_async_copy(
                    parts[group * size + step],
                    held.at[step, :, :, pl.ds(group * width, width)],
                    in_sems.at[step, group],
                )
                for group in range(groups)
            ]
        )
        writes.append(
            [
                pltpu.make_async_copy(
                    held.at[step, index],
                    out.at[0, :, pl.ds(start, total // size)],
                    out_sems.at[step, index],
                )
                for index, out in enumerate(outs)
            ]
        )
    for read in sum(reads, []):
        read.start()
    for read, write in zip(reads, writes):
        for one in read:
            one.wait()
        for one in write:
            one.start()
    for one in sum(writes, []):
        one.wait()


def put_in_place(size, groups, width, place, parts, shape):
    return pl.pallas_call(
        functools.partial(place_kernel, size, groups, width),
        out_shape=[jax.ShapeDtypeStruct(shape, jnp.bfloat16)] * 3,
        in_specs=[SMEM] + [ANY] * len(parts),
        out_specs=[ANY] * 3,
        scratch_shapes=[
            pltpu.VMEM((size, 3, shape[1], groups * width), jnp.bfloat16),
            pltpu.SemaphoreType.DMA((size, groups)),
            pltpu.SemaphoreType.DMA((size, 3)),
        ],
        compiler_params=PARAMS,
        name="put_in_place",
    )(place, *parts)


def send_group(size, width, row, place, starts, sources, after=()):
    packed = pack(size, width, row, place, starts, sources, after)
    return [shift(packed[step - 1], step) for step in range(1, size)]


def dense_plan(size, heads, groups, block, place, uses, sources):
    features = sources[0].shape[2] // (uses.shape[0] * size)
    width = heads * features
    parts = []
    for group in range(groups):
        starts = jnp.arange(size, dtype=jnp.int32)[None] * groups + group
        spot = jnp.concatenate([place, place * groups + group, jnp.full(1, group * heads, jnp.int32)])
        fars = send_group(size, width, 0, place, starts, sources)
        outs = run_heads(size, heads, block, spot, uses, sources, fars)
        parts.append(outs[0])
        parts += [shift(outs[step], -step) for step in range(1, size)]
    return tuple(put_in_place(size, groups, width, place, parts, sources[0].shape))


class Items:
    def __init__(self, size, total, odd, even):
        self.size, self.total, self.at = size, total, Rows(total)
        self.slots = {step: odd if step % 2 else even for step in range(1, size)}
        self.first, self.count = {}, 0
        for step in range(1, size):
            self.first[step] = self.count
            self.count += self.slots[step]
        self.rows = {step: -(-(self.slots[step] + self.count) // 8) * 8 for step in self.slots}


def item_pack_kernel(items, place, plan, query, grad, *outs):
    size = items.size
    position = place[0]
    features = outs[0].shape[-1]
    for step in range(1, size):
        pair = position * size + lax.rem(position + step, size)
        tally = plan[items.at.tallies, pair]
        for slot in range(items.slots[step]):
            head = jnp.where(slot < tally, plan[items.at.lists + slot, pair], 0)
            columns = columns_of(head, features)
            outs[step - 1][slot, 0] = query[0, :, columns]
            outs[step - 1][slot, 1] = grad[0, :, columns]


def item_pack(items, place, plan, query, grad):
    tokens = query.shape[1]
    features = query.shape[2] // items.total
    return pl.pallas_call(
        functools.partial(item_pack_kernel, items),
        out_shape=[
            jax.ShapeDtypeStruct((items.slots[step], 2, tokens, features), jnp.bfloat16)
            for step in range(1, items.size)
        ],
        in_specs=[SMEM] * 2 + [VMEM] * 2,
        out_specs=[VMEM] * (items.size - 1),
        compiler_params=PARAMS,
        name="item_pack",
    )(place, plan, query, grad)


def each_item(items, position, plan):
    for step in range(1, items.size):
        origin = lax.rem(position + items.size - step, items.size)
        pair = origin * items.size + position
        tally = plan[items.at.tallies, pair]
        for slot in range(items.slots[step]):
            real = slot < tally
            head = jnp.where(real, plan[items.at.lists + slot, pair], 0)
            weight = jnp.where(real, plan[head, pair], 0).astype(jnp.float32)
            yield step, slot, head, weight


def columns_of(head, features):
    if isinstance(head, int):
        return pl.ds(head * features, features)
    return pl.ds(pl.multiple_of(head * features, features), features)


def by_groups(count, one, straight=8):
    straight = math.gcd(count, straight)

    def some(index, carry):
        for part in range(straight):
            one(index * straight + part)
        return carry

    lax.fori_loop(0, count // straight, some, 0)


def cost(blocks, products, side):
    return pl.CostEstimate(
        flops=2 * blocks * products * side**3,
        bytes_accessed=8 * blocks * side * side,
        transcendentals=blocks * side * side,
    )


def products(keys, values, queries, grads):
    factor = keys.shape[1] ** -0.5
    return dot(keys, queries, NT) * (factor * LOG2E), dot(values, grads, NT)


def one_total(scores, prob_grad):
    top = jnp.max(scores, axis=0, keepdims=True)
    exps = jnp.exp2(scores - top)
    total = jnp.sum(exps, axis=0, keepdims=True)
    moment = jnp.sum(exps * prob_grad, axis=0, keepdims=True)
    return top + jnp.log2(total), moment / total


def one_weight(scores, prob_grad, weight, log, delta):
    probs = jnp.exp2(scores - log) * weight
    return probs.astype(jnp.bfloat16), (probs * (prob_grad - delta)).astype(jnp.bfloat16)


def own_totals_kernel(total, query, key, value, grad, out, kept):
    features = query.shape[2] // total

    def one_head(head):
        columns = columns_of(head, features)
        block = [ref[0, :, columns] for ref in (key, value, query, grad)]
        scores, prob_grad = products(*block)
        kept[head, 0], kept[head, 1] = scores, prob_grad
        out[0, pl.ds(head, 1), :], out[1, pl.ds(head, 1), :] = one_total(scores, prob_grad)

    by_groups(total, one_head)


def run_own_totals(total, sources):
    tokens = sources[0].shape[1]
    return pl.pallas_call(
        functools.partial(own_totals_kernel, total),
        out_shape=[
            jax.ShapeDtypeStruct((2, total, tokens), jnp.float32),
            jax.ShapeDtypeStruct((total, 2, tokens, tokens), jnp.float32),
        ],
        in_specs=[VMEM] * 4,
        out_specs=[VMEM] * 2,
        compiler_params=PARAMS,
        cost_estimate=cost(total, 2, tokens),
        name="own_totals",
    )(*sources)


def totals_kernel(items, place, plan, key, value, own, *refs):
    size = items.size
    far_refs, (out, kept, *packets) = refs[: size - 1], refs[size - 1 :]
    position = place[0]
    features = key.shape[2] // items.total
    for step, packet in enumerate(packets, 1):
        pair = position * size + lax.rem(position + step, size)
        tally = plan[items.at.tallies, pair]
        for slot in range(items.slots[step]):
            head = jnp.where(slot < tally, plan[items.at.lists + slot, pair], 0)
            for plane in range(2):
                packet[plane, pl.ds(slot, 1), :] = own[plane, pl.ds(head, 1), :]
    for index, (step, slot, head, _) in enumerate(each_item(items, position, plan)):
        columns = columns_of(head, features)
        far = far_refs[step - 1]
        scores, prob_grad = products(key[0, :, columns], value[0, :, columns], far[slot, 0], far[slot, 1])
        kept[index, 0], kept[index, 1] = scores, prob_grad
        for plane, total in enumerate(one_total(scores, prob_grad)):
            out[plane, pl.ds(index, 1), :] = total
            for back, packet in enumerate(packets, 1):
                packet[plane, pl.ds(items.slots[back] + index, 1), :] = total


def run_totals(items, place, plan, sources, own, fars):
    tokens = sources[0].shape[1]
    rows = [-(-items.count // 8) * 8] + [items.rows[step] for step in range(1, items.size)]
    totals = [jax.ShapeDtypeStruct((2, count, tokens), jnp.float32) for count in rows]
    kept = jax.ShapeDtypeStruct((items.count, 2, tokens, tokens), jnp.float32)
    return pl.pallas_call(
        functools.partial(totals_kernel, items),
        out_shape=[totals[0], kept, *totals[1:]],
        in_specs=[SMEM] * 2 + [VMEM] * (2 + items.size),
        out_specs=[VMEM] * (1 + items.size),
        compiler_params=PARAMS,
        cost_estimate=cost(items.count, 2, tokens),
        name="totals",
    )(place, plan, *sources[1:3], own, *fars)


def far_part(items, position, plan, back, head, origin, gap, slot=None):
    column = lax.rem(position + items.size - back, items.size)
    entry = origin * items.size + column
    weight = plan[head, entry].astype(jnp.float32)
    if gap == 0:
        return weight, back, slot
    row = jnp.minimum(plan[items.at.slots + head, entry], items.slots[gap] - 1)
    return weight, back, items.slots[back] + items.first[gap] + row


def join(rows, totals, logs, means, shares, joined):
    for index, parts in enumerate(rows):
        at = pl.ds(index, 1)
        for part, (weight, back, row) in enumerate(parts):
            log = totals[back][0, pl.ds(row, 1), :]
            logs[part, at, :] = jnp.where(weight > 0, log, -jnp.inf)
            means[part, at, :] = totals[back][1, pl.ds(row, 1), :]
            shares[part, at, :] = jnp.broadcast_to(weight, log.shape)
    count = logs.shape[0]
    top = functools.reduce(jnp.maximum, [logs[part] for part in range(count)])
    weights = [shares[part] * jnp.exp2(logs[part] - top) for part in range(count)]
    total = sum(weights)
    joined[0] = top + jnp.log2(total)
    joined[1] = sum(weight * means[part] for part, weight in enumerate(weights)) / total


def join_scratch(items, count, tokens):
    rows = -(-count // 8) * 8
    part = pltpu.VMEM((items.size, rows, tokens), jnp.float32)
    return [part, part, part, pltpu.VMEM((2, rows, tokens), jnp.float32)]


def items_kernel(items, place, plan, key, kept, *refs):
    size = items.size
    totals, refs = refs[:size], refs[-4 - size :]
    made, item_outs, scratch = refs[0], refs[1:size], refs[size:]
    position = place[0]
    features = key.shape[2] // items.total
    factor = features**-0.5
    arrived = list(each_item(items, position, plan))
    rows = []
    for index, (step, slot, head, weight) in enumerate(arrived):
        origin = lax.rem(position + size - step, size)
        parts = [(weight, 0, index)]
        for back in range(1, size):
            gap = (step - back) % size
            parts.append(far_part(items, position, plan, back, head, origin, gap, slot))
        rows.append(parts)
    join(rows, totals, *scratch)
    joined = scratch[-1]
    for index, (step, slot, head, weight) in enumerate(arrived):
        log, delta = joined[0, pl.ds(index, 1), :], joined[1, pl.ds(index, 1), :]
        log = jnp.where(weight > 0, log, jnp.inf)
        probs, score_grad = one_weight(kept[index, 0], kept[index, 1], weight, log, delta)
        made[index, 0], made[index, 1] = probs, score_grad
        query_term = dot(score_grad, key[0, :, columns_of(head, features)], TN) * factor
        item_outs[step - 1][slot] = query_term.astype(jnp.bfloat16)


def run_items(items, place, plan, sources, kept, totals, after):
    _, tokens, width = sources[0].shape
    features = width // items.total
    outs = [jax.ShapeDtypeStruct(kept.shape, jnp.bfloat16)]
    for step in range(1, items.size):
        outs.append(jax.ShapeDtypeStruct((items.slots[step], tokens, features), jnp.bfloat16))
    return pl.pallas_call(
        functools.partial(items_kernel, items),
        out_shape=outs,
        in_specs=[SMEM] * 2 + [VMEM] * (2 + items.size) + [ANY] * len(after),
        out_specs=[VMEM] * len(outs),
        scratch_shapes=join_scratch(items, items.count, tokens),
        compiler_params=PARAMS,
        cost_estimate=cost(items.count, 5, tokens),
        name="items",
    )(place, plan, sources[1], kept, *totals, *after)


def own_kernel(items, place, plan, query, key, grad, kept, *refs):
    size = items.size
    totals, fars, made = refs[:size], refs[size : 2 * size - 1], refs[2 * size - 1]
    query_out, key_out, value_out = refs[2 * size : 2 * size + 3]
    key_sum, value_sum, *scratch = refs[2 * size + 3 :]
    position = place[0]
    features = query.shape[2] // items.total
    factor = features**-0.5
    rows = []
    for head in range(items.total):
        parts = [(plan[head, position * size + position].astype(jnp.float32), 0, head)]
        for back in range(1, size):
            parts.append(far_part(items, position, plan, back, head, position, size - back))
        rows.append(parts)
    join(rows, totals, *scratch)
    joined = scratch[-1]

    def one_head(head):
        log, delta = joined[0, pl.ds(head, 1), :], joined[1, pl.ds(head, 1), :]
        weight = plan[head, position * size + position].astype(jnp.float32)
        probs, score_grad = one_weight(kept[head, 0], kept[head, 1], weight, log, delta)
        columns = columns_of(head, features)
        key_sum[head] = dot(score_grad, query[0, :, columns])
        value_sum[head] = dot(probs, grad[0, :, columns])
        query_out[head] = dot(score_grad, key[0, :, columns], TN) * factor

    by_groups(items.total, one_head)
    for index, (step, slot, head, weight) in enumerate(each_item(items, position, plan)):
        far = fars[step - 1]
        key_sum[head] += dot(made[index, 1], far[slot, 0])
        value_sum[head] += dot(made[index, 0], far[slot, 1])

    def one_sum(head):
        columns = columns_of(head, features)
        key_out[0, :, columns] = (key_sum[head] * factor).astype(jnp.bfloat16)
        value_out[0, :, columns] = value_sum[head].astype(jnp.bfloat16)

    by_groups(items.total, one_sum)


def run_own(items, place, plan, sources, kept, totals, fars, made):
    _, tokens, width = sources[0].shape
    features = width // items.total
    each = (items.total, tokens, features)
    query, key, _, grad = sources
    return pl.pallas_call(
        functools.partial(own_kernel, items),
        out_shape=[
            jax.ShapeDtypeStruct(each, jnp.float32),
            jax.ShapeDtypeStruct(query.shape, jnp.bfloat16),
            jax.ShapeDtypeStruct(query.shape, jnp.bfloat16),
        ],
        in_specs=[SMEM] * 2 + [VMEM] * (4 + 2 * items.size),
        out_specs=[VMEM] * 3,
        scratch_shapes=[pltpu.VMEM(each, jnp.float32)] * 2
        + join_scratch(items, items.total, tokens),
        compiler_params=PARAMS,
        cost_estimate=cost(items.total + items.count, 5, tokens),
        name="own",
    )(place, plan, query, key, grad, kept, *totals, *fars, made)


def query_kernel(items, place, plan, own_query, *refs):
    size = items.size
    backs, (out, held, sems) = refs[: size - 1], refs[size - 1 :]
    position = place[0]
    features = own_query.shape[2]
    group = math.gcd(items.total, 4)

    def copy(first):
        columns = pl.ds(pl.multiple_of(first * features, 128), group * features)
        return pltpu.make_async_copy(held.at[:, columns], out.at[0, :, columns], sems.at[first // group])

    def some(index, carry):
        for part in range(group):
            head = index * group + part
            total = own_query[head]
            for step in range(1, size):
                entry = position * size + lax.rem(position + step, size)
                used = plan[head, entry] > 0
                slot = jnp.minimum(plan[items.at.slots + head, entry], items.slots[step] - 1)
                total += jnp.where(used, backs[step - 1][slot].astype(jnp.float32), 0.0)
            held[:, columns_of(head, features)] = total.astype(jnp.bfloat16)
        copy(index * group).start()
        return carry

    lax.fori_loop(0, items.total // group, some, 0)
    for first in range(0, items.total, group):
        copy(first).wait()


def query_gradient(items, place, plan, own_query, backs, shape):
    return pl.pallas_call(
        functools.partial(query_kernel, items),
        out_shape=jax.ShapeDtypeStruct(shape, jnp.bfloat16),
        in_specs=[SMEM] * 2 + [VMEM] * items.size,
        out_specs=ANY,
        scratch_shapes=[
            pltpu.VMEM(shape[1:], jnp.bfloat16),
            pltpu.SemaphoreType.DMA((items.total // math.gcd(items.total, 4),)),
        ],
        compiler_params=PARAMS,
        name="query_gradient",
    )(place, plan, own_query, *backs)


def shared_kernel(items, place, plan, *refs):
    size = items.size
    parts, outs, sems = refs[:size], refs[size + 3 : size + 6], refs[-1]
    position = place[0]
    features = parts[0].shape[2]
    copies = []
    for step in range(size):
        columns = columns_of(plan[items.at.shared, lax.rem(position + step, size)], features)
        for index, out in enumerate(outs):
            copies.append(
                pltpu.make_async_copy(
                    parts[step].at[index], out.at[0, :, columns], sems.at[step, index]
                )
            )
    for copy in copies:
        copy.start()
    for copy in copies:
        copy.wait()


def put_shared(items, place, plan, parts, grads):
    first = 2 + len(parts)
    return pl.pallas_call(
        functools.partial(shared_kernel, items),
        out_shape=[jax.ShapeDtypeStruct(grad.shape, jnp.bfloat16) for grad in grads],
        in_specs=[SMEM] * 2 + [VMEM] * len(parts) + [ANY] * 3,
        out_specs=[ANY] * 3,
        scratch_shapes=[pltpu.SemaphoreType.DMA((items.size, 3))],
        input_output_aliases={first + index: index for index in range(3)},
        compiler_params=PARAMS,
        name="put_shared",
    )(place, plan, *parts, *grads)


def items_plan(items, block, place, plan, sources):
    size = items.size
    width = sources[0].shape[2] // items.total
    packed = item_pack(items, place, plan, sources[0], sources[3])
    fars = [shift(packed[step - 1], step) for step in range(1, size)]
    shared_fars = send_group(size, width, items.at.shared, place, plan, sources, packed)
    own_totals, own_kept = run_own_totals(items.total, sources)
    totals, kept, *packets = run_totals(items, place, plan, sources, own_totals, fars)
    packets = [shift(packets[step - 1], step) for step in range(1, size)]
    made, *outs = run_items(items, place, plan, sources, kept, [totals, *packets], shared_fars)
    backs = [shift(outs[step - 1], -step) for step in range(1, size)]
    spot = plan[items.at.spot, :3]
    parts = run_heads(size, 1, block, spot, plan, sources, shared_fars, (made,))
    parts = [parts[0]] + [shift(parts[step], -step) for step in range(1, size)]
    own_query, *light = run_own(items, place, plan, sources, own_kept, [own_totals, *packets], fars, made)
    query_light = query_gradient(items, place, plan, own_query, backs, light[0].shape)
    return tuple(put_shared(items, place, plan, parts, (query_light, *light)))


def shards(query_states, key_states, value_states, out_grad, pattern, counts):
    size = lax.axis_size("seq")
    place = lax.axis_index("seq").astype(jnp.int32).reshape(1)
    heads, blocks, slots = pattern.shape
    block = query_states.shape[1] * size // blocks
    sources = (query_states, key_states, value_states, out_grad)

    def by_heads(*sources):
        uses = count_uses(pattern, counts)
        return dense_plan(size, heads, 1, block, place, uses, sources)

    if size > 4 or size % 2 or blocks != size or heads == 1:
        return by_heads(*sources)
    used = jnp.arange(slots, dtype=jnp.int32) < counts[:, :, None]
    named = jnp.where(used, pattern, size * blocks)
    parts = [named] + [shift(named, step) for step in range(1, size)]
    plan, choice = make_plan(size, heads, place, parts)

    def by_items(odd, even):
        items = Items(size, size * heads, odd, even)
        return lambda *sources: items_plan(items, block, place, plan, sources)

    branches = [by_items(odd, even) for odd, even in SIZES] + [by_heads]
    return lax.switch(choice[0], branches, *sources)


def solution(mesh):
    tokens = P(("groups", "mp", "rep"), "seq", None)
    return jax.shard_map(
        shards,
        mesh=mesh,
        in_specs=(tokens, tokens, tokens, tokens, P("seq", None, None), P("seq", None)),
        out_specs=(tokens, tokens, tokens),
        check_vma=False,
    )
```

```python
import functools
import math

import jax
import jax.numpy as jnp
from jax import lax
from jax.experimental import pallas as pl
from jax.experimental.pallas import tpu as pltpu
from jax.sharding import PartitionSpec as P

LOG2E = math.log2(math.e)
NT = (((1,), (1,)), ((), ()))
NN = (((1,), (0,)), ((), ()))
TN = (((0,), (0,)), ((), ()))
VMEM_LIMIT = 32 * 1024 * 1024
SMEM = pl.BlockSpec(memory_space=pltpu.SMEM)
ANY = pl.BlockSpec(memory_space=pl.ANY)
VMEM = pl.BlockSpec(memory_space=pltpu.VMEM)
PARAMS = pltpu.CompilerParams(vmem_limit_bytes=VMEM_LIMIT)
LITTLE = pltpu.CompilerParams(vmem_limit_bytes=4 * 1024 * 1024)
SIZES = ((3, 2), (3, 3), (4, 3), (4, 4), (5, 5))


def dot(left, right, dims=NN):
    return lax.dot_general(left, right, dims, preferred_element_type=jnp.float32)


def shift(array, step):
    size = lax.axis_size("seq")
    return lax.ppermute(array, "seq", [(j, (j + step) % size) for j in range(size)])


def table_kernel(heads, blocks, slots, pattern, counts, table):
    def one_row(index, carry):
        head, row = index // blocks, index % blocks
        count = counts[head, row]
        named = [jnp.where(slot < count, pattern[head, row, slot], blocks) for slot in range(slots)]
        for column in range(blocks):
            table[head, row * blocks + column] = sum((n == column).astype(jnp.int32) for n in named)
        return carry

    if heads * blocks > 16:
        lax.fori_loop(0, heads * blocks, one_row, 0)
    else:
        for index in range(heads * blocks):
            one_row(index, 0)


def count_uses(pattern, counts):
    heads, blocks, slots = pattern.shape
    return pl.pallas_call(
        functools.partial(table_kernel, heads, blocks, slots),
        out_shape=jax.ShapeDtypeStruct((heads, blocks * blocks), jnp.int32),
        in_specs=[SMEM] * 2,
        out_specs=SMEM,
        name="count_uses",
    )(pattern, counts)


class Rows:
    def __init__(self, total):
        self.slots = total
        self.lists = 2 * total
        self.tallies = self.lists + max(max(pair) for pair in SIZES)
        self.shared = self.tallies + 1
        self.spot = self.shared + 1
        self.count = -(-(self.spot + 1) // 8) * 8


def plan_kernel(size, heads, place, *refs):
    parts, (plan, choice, held) = refs[:size], refs[size:]
    position = place[0]
    total, pairs = size * heads, size * size
    rows = Rows(total)
    count = parts[0].shape[-1]
    for step in range(size):
        for row in range(size):
            named = parts[step][:, row, :].astype(jnp.float32)
            held[pl.ds(step * heads, heads), pl.ds(row * count, count)] = named
    head = lax.broadcasted_iota(jnp.int32, (total, total), 0)
    place_of = lax.broadcasted_iota(jnp.int32, (total, total), 1)
    step = sum((place_of >= heads * k).astype(jnp.int32) for k in range(1, size))
    owner = position - step
    owner += jnp.where(owner < 0, size, 0)
    order = (head == owner * heads + place_of - step * heads).astype(jnp.float32)
    named = dot(order, held[...])
    head = lax.broadcasted_iota(jnp.int32, (total, pairs), 0)
    pair = lax.broadcasted_iota(jnp.int32, (total, pairs), 1)
    table = jnp.zeros((total, pairs), jnp.float32)
    for row in range(size):
        column = (pair - row * size).astype(jnp.float32)
        for slot in range(row * count, (row + 1) * count):
            table += jnp.where(column == named[:, slot : slot + 1], 1.0, 0.0)
    plan[pl.ds(0, total), :] = table.astype(jnp.int32)

    uses = (table > 0).astype(jnp.float32)
    for block in range(size):
        uses = jnp.where(pair == block * (size + 1), 0.0, uses)
    lane = lax.broadcasted_iota(jnp.int32, (1, pairs), 1)
    shared, mine = jnp.zeros((1, pairs), jnp.int32), jnp.zeros((1, 1), jnp.int32)
    odd = functools.reduce(
        jnp.logical_or, [lane == i * size + j for i in range(size) for j in range(size) if (i - j) % 2]
    )
    number = head[:, :1].astype(jnp.float32)
    free = number >= 0
    for index in range(size):
        load = jnp.sum(uses, axis=0, keepdims=True) + jnp.where(odd, 0.0, 0.6)
        load = load * load * load
        score = jnp.sum(uses * (load * load), axis=1, keepdims=True)
        score = jnp.where(free, score, -1.0)
        top = jnp.max(score, axis=0, keepdims=True)
        name = jnp.max(jnp.where(score == top, number, -1.0), axis=0, keepdims=True)
        uses = jnp.where(number == name, 0.0, uses)
        free = free & (number != name)
        shared = jnp.where(lane == index, name.astype(jnp.int32), shared)
        mine = jnp.where(index == position, name.astype(jnp.int32), mine)
    earlier = lax.broadcasted_iota(jnp.int32, (total, total), 1) < lax.broadcasted_iota(jnp.int32, (total, total), 0)
    slots = dot(earlier.astype(jnp.float32), uses)
    tallies = jnp.sum(uses, axis=0, keepdims=True)
    plan[pl.ds(rows.slots, total), :] = slots.astype(jnp.int32)
    for slot in range(rows.tallies - rows.lists):
        hit = jnp.where(slots == slot, uses * head.astype(jnp.float32), 0.0)
        plan[pl.ds(rows.lists + slot, 1), :] = jnp.sum(hit, axis=0, keepdims=True).astype(jnp.int32)
    plan[pl.ds(rows.tallies, 1), :] = tallies.astype(jnp.int32)
    plan[pl.ds(rows.shared, 1), :] = shared
    plan[pl.ds(rows.spot, 1), :] = jnp.where(lane == 0, position, mine)

    most_odd = jnp.max(jnp.where(odd, tallies, 0.0)).astype(jnp.int32)
    most_even = jnp.max(jnp.where(odd, 0.0, tallies)).astype(jnp.int32)
    chosen = jnp.int32(len(SIZES))
    for index in reversed(range(len(SIZES))):
        fits = (most_odd <= SIZES[index][0]) & (most_even <= SIZES[index][1])
        chosen = jnp.where(fits, index, chosen)
    choice[0] = chosen


def make_plan(size, heads, place, parts):
    total, pairs = size * heads, size * size
    return pl.pallas_call(
        functools.partial(plan_kernel, size, heads),
        out_shape=[
            jax.ShapeDtypeStruct((Rows(total).count, pairs), jnp.int32),
            jax.ShapeDtypeStruct((1,), jnp.int32),
        ],
        in_specs=[SMEM] + [VMEM] * size,
        out_specs=[VMEM, SMEM],
        scratch_shapes=[pltpu.VMEM((total, size * parts[0].shape[2]), jnp.float32)],
        compiler_params=LITTLE,
        name="make_plan",
    )(place, *parts)


def pack_kernel(size, width, row, place, starts, *refs):
    sources, outs, (held, in_sems, out_sems) = refs[:4], refs[-2 - size : -3], refs[-3:]
    position = place[0]
    reads, writes = [], []
    for step in range(1, size):
        start = starts[row, lax.rem(position + step, size)] * width
        columns = pl.ds(pl.multiple_of(start, 128), width)
        reads.append(
            [
                pltpu.make_async_copy(
                    source.at[0, :, columns], held.at[step - 1, index], in_sems.at[step - 1, index]
                )
                for index, source in enumerate(sources)
            ]
        )
        writes.append(pltpu.make_async_copy(held.at[step - 1], outs[step - 1], out_sems.at[step - 1]))
    for read in sum(reads, []):
        read.start()
    for read, write in zip(reads, writes):
        for one in read:
            one.wait()
        write.start()
    for write in writes:
        write.wait()


def pack(size, width, row, place, starts, sources, after):
    tokens = sources[0].shape[1]
    return pl.pallas_call(
        functools.partial(pack_kernel, size, width, row),
        out_shape=[jax.ShapeDtypeStruct((4, tokens, width), jnp.bfloat16)] * (size - 1),
        in_specs=[SMEM] * 2 + [ANY] * (4 + len(after)),
        out_specs=[ANY] * (size - 1),
        scratch_shapes=[
            pltpu.VMEM((size - 1, 4, tokens, width), jnp.bfloat16),
            pltpu.SemaphoreType.DMA((size - 1, 4)),
            pltpu.SemaphoreType.DMA((size - 1,)),
        ],
        compiler_params=PARAMS,
        name="pack",
    )(place, starts, *sources, *after)


def heads_kernel(size, heads, block, spot, uses, *refs):
    own_refs, far_refs = refs[:4], refs[4 : 3 + size]
    out_refs = refs[-4 - size : -4]
    joined, key_flip, key_sum, value_sum = refs[-4:]
    position, first = spot[0], spot[2]
    tokens, features = own_refs[0].shape[1], joined.shape[2]
    length = size * tokens
    blocks = length // block
    local = tokens // block
    chunk = min(length, max(2 * block, 256))
    factor = features**-0.5

    def origin(index):
        return lax.rem(position + size - index // local, size) * local + index % local

    def one_chunk(head, number):
        start = pl.multiple_of(number * chunk, chunk)
        rows = pl.ds(start, chunk)
        query, grad = joined[0, rows, :], joined[3, rows, :]
        scores = dot(joined[1], query, NT)
        prob_grad = dot(joined[2], grad, NT)
        weight_parts, score_parts = [], []
        for part in range(chunk // block):
            row = origin(number * (chunk // block) + part)
            columns = slice(part * block, (part + 1) * block)
            counts = [
                uses[first + head, row * blocks + origin(j)].astype(jnp.float32) for j in range(blocks)
            ]
            terms = []
            for j in range(blocks):
                term = scores[j * block : (j + 1) * block, columns] * (factor * LOG2E)
                terms.append(term + jnp.where(counts[j] > 0, 0.0, -jnp.inf))
            top = functools.reduce(jnp.maximum, terms)
            top = jnp.max(top, axis=0, keepdims=True)
            exps = [jnp.exp2(term - top) for term in terms]
            grads = [prob_grad[j * block : (j + 1) * block, columns] for j in range(blocks)]
            total = sum(count * e for count, e in zip(counts, exps))
            moment = sum(count * (e * g) for count, e, g in zip(counts, exps, grads))
            inverse = 1.0 / jnp.sum(total, axis=0, keepdims=True)
            delta = jnp.sum(moment, axis=0, keepdims=True) * inverse
            probs = [e * (inverse * count) for count, e in zip(counts, exps)]
            weight_parts.append(jnp.concatenate([p.astype(jnp.bfloat16) for p in probs], axis=0))
            score_parts.append(
                jnp.concatenate(
                    [(p * (g - delta)).astype(jnp.bfloat16) for p, g in zip(probs, grads)], axis=0
                )
            )
        weights = jnp.concatenate(weight_parts, axis=1)
        score_grad = jnp.concatenate(score_parts, axis=1)
        key_sum[...] += dot(score_grad, query)
        value_sum[...] += dot(weights, grad)
        flipped = dot(key_flip[...], score_grad)
        return (flipped.T * factor).astype(jnp.bfloat16)

    def one_head(head, carry):
        features_at = columns_of(head, features)
        for index in range(4):
            joined[index, pl.ds(0, tokens), :] = own_refs[index][0, :, features_at]
            for step in range(1, size):
                joined[index, pl.ds(step * tokens, tokens), :] = far_refs[step - 1][index, :, features_at]
        key_flip[...] = joined[1].T
        key_sum[...] = jnp.zeros_like(key_sum)
        value_sum[...] = jnp.zeros_like(value_sum)

        for number in range(length // chunk):
            query_grad = one_chunk(head, number)
            for part in range(max(1, chunk // tokens)):
                step, within = divmod(number * chunk + part * tokens, tokens)
                span = min(chunk, tokens)
                out_refs[step][0, pl.ds(within, span), features_at] = query_grad[part * span : (part + 1) * span]
        for step in range(size):
            rows = pl.ds(step * tokens, tokens)
            out_refs[step][1, :, features_at] = (factor * key_sum[rows, :]).astype(jnp.bfloat16)
            out_refs[step][2, :, features_at] = value_sum[rows, :].astype(jnp.bfloat16)
        return carry

    if heads == 1:
        one_head(0, 0)
    else:
        lax.fori_loop(0, heads, one_head, 0)


def run_heads(size, heads, block, spot, uses, owns, fars, after=()):
    tokens = owns[0].shape[1]
    features = fars[0].shape[2] // heads
    width = heads * features
    length = size * tokens
    own_spec = pl.BlockSpec((1, tokens, width), lambda i, spot: (0, 0, spot[1]))
    far_spec = pl.BlockSpec((4, tokens, width), lambda i, spot: (0, 0, 0))
    out_spec = pl.BlockSpec((3, tokens, width), lambda i, spot: (0, 0, 0))
    return pl.pallas_call(
        functools.partial(heads_kernel, size, heads, block),
        grid_spec=pltpu.PrefetchScalarGridSpec(
            num_scalar_prefetch=1,
            grid=(1,),
            in_specs=[SMEM] + [own_spec] * 4 + [far_spec] * (size - 1) + [ANY] * len(after),
            out_specs=[out_spec] * size,
            scratch_shapes=[
                pltpu.VMEM((4, length, features), jnp.bfloat16),
                pltpu.VMEM((features, length), jnp.bfloat16),
                pltpu.VMEM((length, features), jnp.float32),
                pltpu.VMEM((length, features), jnp.float32),
            ],
        ),
        out_shape=[jax.ShapeDtypeStruct((3, tokens, width), jnp.bfloat16)] * size,
        compiler_params=PARAMS,
        cost_estimate=pl.CostEstimate(
            flops=heads * 10 * length * length * features,
            bytes_accessed=heads * 14 * length * features,
            transcendentals=heads * length * length,
        ),
        name="heads",
    )(spot, uses, *owns, *fars, *after)


def place_kernel(size, groups, width, place, *refs):
    parts, outs = refs[: size * groups], refs[size * groups : -3]
    held, in_sems, out_sems = refs[-3:]
    position = place[0]
    total = outs[0].shape[2]
    reads, writes = [], []
    for step in range(size):
        start = pl.multiple_of(lax.rem(position + step, size) * (total // size), 128)
        reads.append(
            [
                pltpu.make_async_copy(
                    parts[group * size + step],
                    held.at[step, :, :, pl.ds(group * width, width)],
                    in_sems.at[step, group],
                )
                for group in range(groups)
            ]
        )
        writes.append(
            [
                pltpu.make_async_copy(
                    held.at[step, index],
                    out.at[0, :, pl.ds(start, total // size)],
                    out_sems.at[step, index],
                )
                for index, out in enumerate(outs)
            ]
        )
    for read in sum(reads, []):
        read.start()
    for read, write in zip(reads, writes):
        for one in read:
            one.wait()
        for one in write:
            one.start()
    for one in sum(writes, []):
        one.wait()


def put_in_place(size, groups, width, place, parts, shape):
    return pl.pallas_call(
        functools.partial(place_kernel, size, groups, width),
        out_shape=[jax.ShapeDtypeStruct(shape, jnp.bfloat16)] * 3,
        in_specs=[SMEM] + [ANY] * len(parts),
        out_specs=[ANY] * 3,
        scratch_shapes=[
            pltpu.VMEM((size, 3, shape[1], groups * width), jnp.bfloat16),
            pltpu.SemaphoreType.DMA((size, groups)),
            pltpu.SemaphoreType.DMA((size, 3)),
        ],
        compiler_params=PARAMS,
        name="put_in_place",
    )(place, *parts)


def send_group(size, width, row, place, starts, sources, after=()):
    packed = pack(size, width, row, place, starts, sources, after)
    return [shift(packed[step - 1], step) for step in range(1, size)]


def dense_plan(size, heads, groups, block, place, uses, sources):
    features = sources[0].shape[2] // (uses.shape[0] * size)
    width = heads * features
    parts = []
    for group in range(groups):
        starts = jnp.arange(size, dtype=jnp.int32)[None] * groups + group
        spot = jnp.concatenate([place, place * groups + group, jnp.full(1, group * heads, jnp.int32)])
        fars = send_group(size, width, 0, place, starts, sources)
        outs = run_heads(size, heads, block, spot, uses, sources, fars)
        parts.append(outs[0])
        parts += [shift(outs[step], -step) for step in range(1, size)]
    return tuple(put_in_place(size, groups, width, place, parts, sources[0].shape))


class Items:
    def __init__(self, size, total, odd, even):
        self.size, self.total, self.at = size, total, Rows(total)
        self.slots = {step: odd if step % 2 else even for step in range(1, size)}
        self.first, self.count = {}, 0
        for step in range(1, size):
            self.first[step] = self.count
            self.count += self.slots[step]
        self.rows = {step: -(-(self.slots[step] + self.count) // 8) * 8 for step in self.slots}


def item_pack_kernel(items, place, plan, query, grad, *outs):
    size = items.size
    position = place[0]
    features = outs[0].shape[-1]
    for step in range(1, size):
        pair = position * size + lax.rem(position + step, size)
        tally = plan[items.at.tallies, pair]
        for slot in range(items.slots[step]):
            head = jnp.where(slot < tally, plan[items.at.lists + slot, pair], 0)
            columns = columns_of(head, features)
            outs[step - 1][slot, 0] = query[0, :, columns]
            outs[step - 1][slot, 1] = grad[0, :, columns]


def item_pack(items, place, plan, query, grad):
    tokens = query.shape[1]
    features = query.shape[2] // items.total
    return pl.pallas_call(
        functools.partial(item_pack_kernel, items),
        out_shape=[
            jax.ShapeDtypeStruct((items.slots[step], 2, tokens, features), jnp.bfloat16)
            for step in range(1, items.size)
        ],
        in_specs=[SMEM] * 2 + [VMEM] * 2,
        out_specs=[VMEM] * (items.size - 1),
        compiler_params=PARAMS,
        name="item_pack",
    )(place, plan, query, grad)


def each_item(items, position, plan):
    for step in range(1, items.size):
        origin = lax.rem(position + items.size - step, items.size)
        pair = origin * items.size + position
        tally = plan[items.at.tallies, pair]
        for slot in range(items.slots[step]):
            real = slot < tally
            head = jnp.where(real, plan[items.at.lists + slot, pair], 0)
            weight = jnp.where(real, plan[head, pair], 0).astype(jnp.float32)
            yield step, slot, head, weight


def columns_of(head, features):
    if isinstance(head, int):
        return pl.ds(head * features, features)
    return pl.ds(pl.multiple_of(head * features, features), features)


def by_groups(count, one, straight=8):
    straight = math.gcd(count, straight)

    def some(index, carry):
        for part in range(straight):
            one(index * straight + part)
        return carry

    lax.fori_loop(0, count // straight, some, 0)


def cost(blocks, products, side):
    return pl.CostEstimate(
        flops=2 * blocks * products * side**3,
        bytes_accessed=8 * blocks * side * side,
        transcendentals=blocks * side * side,
    )


def products(keys, values, queries, grads):
    factor = keys.shape[1] ** -0.5
    return dot(keys, queries, NT) * (factor * LOG2E), dot(values, grads, NT)


def one_total(scores, prob_grad):
    top = jnp.max(scores, axis=0, keepdims=True)
    exps = jnp.exp2(scores - top)
    total = jnp.sum(exps, axis=0, keepdims=True)
    moment = jnp.sum(exps * prob_grad, axis=0, keepdims=True)
    return top + jnp.log2(total), moment / total


def one_weight(scores, prob_grad, weight, log, delta):
    probs = jnp.exp2(scores - log) * weight
    return probs.astype(jnp.bfloat16), (probs * (prob_grad - delta)).astype(jnp.bfloat16)


def own_totals_kernel(total, query, key, value, grad, out, kept):
    features = query.shape[2] // total

    def one_head(head):
        columns = columns_of(head, features)
        block = [ref[0, :, columns] for ref in (key, value, query, grad)]
        scores, prob_grad = products(*block)
        kept[head, 0], kept[head, 1] = scores, prob_grad
        out[0, pl.ds(head, 1), :], out[1, pl.ds(head, 1), :] = one_total(scores, prob_grad)

    by_groups(total, one_head)


def run_own_totals(total, sources):
    tokens = sources[0].shape[1]
    return pl.pallas_call(
        functools.partial(own_totals_kernel, total),
        out_shape=[
            jax.ShapeDtypeStruct((2, total, tokens), jnp.float32),
            jax.ShapeDtypeStruct((total, 2, tokens, tokens), jnp.float32),
        ],
        in_specs=[VMEM] * 4,
        out_specs=[VMEM] * 2,
        compiler_params=PARAMS,
        cost_estimate=cost(total, 2, tokens),
        name="own_totals",
    )(*sources)


def totals_kernel(items, place, plan, key, value, own, *refs):
    size = items.size
    far_refs, (out, kept, *packets) = refs[: size - 1], refs[size - 1 :]
    position = place[0]
    features = key.shape[2] // items.total
    for step, packet in enumerate(packets, 1):
        pair = position * size + lax.rem(position + step, size)
        tally = plan[items.at.tallies, pair]
        for slot in range(items.slots[step]):
            head = jnp.where(slot < tally, plan[items.at.lists + slot, pair], 0)
            for plane in range(2):
                packet[plane, pl.ds(slot, 1), :] = own[plane, pl.ds(head, 1), :]
    for index, (step, slot, head, _) in enumerate(each_item(items, position, plan)):
        columns = columns_of(head, features)
        far = far_refs[step - 1]
        scores, prob_grad = products(key[0, :, columns], value[0, :, columns], far[slot, 0], far[slot, 1])
        kept[index, 0], kept[index, 1] = scores, prob_grad
        for plane, total in enumerate(one_total(scores, prob_grad)):
            out[plane, pl.ds(index, 1), :] = total
            for back, packet in enumerate(packets, 1):
                packet[plane, pl.ds(items.slots[back] + index, 1), :] = total


def run_totals(items, place, plan, sources, own, fars):
    tokens = sources[0].shape[1]
    rows = [-(-items.count // 8) * 8] + [items.rows[step] for step in range(1, items.size)]
    totals = [jax.ShapeDtypeStruct((2, count, tokens), jnp.float32) for count in rows]
    kept = jax.ShapeDtypeStruct((items.count, 2, tokens, tokens), jnp.float32)
    return pl.pallas_call(
        functools.partial(totals_kernel, items),
        out_shape=[totals[0], kept, *totals[1:]],
        in_specs=[SMEM] * 2 + [VMEM] * (2 + items.size),
        out_specs=[VMEM] * (1 + items.size),
        compiler_params=PARAMS,
        cost_estimate=cost(items.count, 2, tokens),
        name="totals",
    )(place, plan, *sources[1:3], own, *fars)


def far_part(items, position, plan, back, head, origin, gap, slot=None):
    column = lax.rem(position + items.size - back, items.size)
    entry = origin * items.size + column
    weight = plan[head, entry].astype(jnp.float32)
    if gap == 0:
        return weight, back, slot
    row = jnp.minimum(plan[items.at.slots + head, entry], items.slots[gap] - 1)
    return weight, back, items.slots[back] + items.first[gap] + row


def join(rows, totals, logs, means, shares, joined):
    for index, parts in enumerate(rows):
        at = pl.ds(index, 1)
        for part, (weight, back, row) in enumerate(parts):
            log = totals[back][0, pl.ds(row, 1), :]
            logs[part, at, :] = jnp.where(weight > 0, log, -jnp.inf)
            means[part, at, :] = totals[back][1, pl.ds(row, 1), :]
            shares[part, at, :] = jnp.broadcast_to(weight, log.shape)
    count = logs.shape[0]
    top = functools.reduce(jnp.maximum, [logs[part] for part in range(count)])
    weights = [shares[part] * jnp.exp2(logs[part] - top) for part in range(count)]
    total = sum(weights)
    joined[0] = top + jnp.log2(total)
    joined[1] = sum(weight * means[part] for part, weight in enumerate(weights)) / total


def join_scratch(items, count, tokens):
    rows = -(-count // 8) * 8
    part = pltpu.VMEM((items.size, rows, tokens), jnp.float32)
    return [part, part, part, pltpu.VMEM((2, rows, tokens), jnp.float32)]


def items_kernel(items, place, plan, key, kept, *refs):
    size = items.size
    totals, refs = refs[:size], refs[-4 - size :]
    made, item_outs, scratch = refs[0], refs[1:size], refs[size:]
    position = place[0]
    features = key.shape[2] // items.total
    factor = features**-0.5
    arrived = list(each_item(items, position, plan))
    rows = []
    for index, (step, slot, head, weight) in enumerate(arrived):
        origin = lax.rem(position + size - step, size)
        parts = [(weight, 0, index)]
        for back in range(1, size):
            gap = (step - back) % size
            parts.append(far_part(items, position, plan, back, head, origin, gap, slot))
        rows.append(parts)
    join(rows, totals, *scratch)
    joined = scratch[-1]
    for index, (step, slot, head, weight) in enumerate(arrived):
        log, delta = joined[0, pl.ds(index, 1), :], joined[1, pl.ds(index, 1), :]
        log = jnp.where(weight > 0, log, jnp.inf)
        probs, score_grad = one_weight(kept[index, 0], kept[index, 1], weight, log, delta)
        made[index, 0], made[index, 1] = probs, score_grad
        query_term = dot(score_grad, key[0, :, columns_of(head, features)], TN) * factor
        item_outs[step - 1][slot] = query_term.astype(jnp.bfloat16)


def run_items(items, place, plan, sources, kept, totals, after):
    _, tokens, width = sources[0].shape
    features = width // items.total
    outs = [jax.ShapeDtypeStruct(kept.shape, jnp.bfloat16)]
    for step in range(1, items.size):
        outs.append(jax.ShapeDtypeStruct((items.slots[step], tokens, features), jnp.bfloat16))
    return pl.pallas_call(
        functools.partial(items_kernel, items),
        out_shape=outs,
        in_specs=[SMEM] * 2 + [VMEM] * (2 + items.size) + [ANY] * len(after),
        out_specs=[VMEM] * len(outs),
        scratch_shapes=join_scratch(items, items.count, tokens),
        compiler_params=PARAMS,
        cost_estimate=cost(items.count, 5, tokens),
        name="items",
    )(place, plan, sources[1], kept, *totals, *after)


def own_kernel(items, place, plan, query, key, grad, kept, *refs):
    size = items.size
    totals, fars, made = refs[:size], refs[size : 2 * size - 1], refs[2 * size - 1]
    query_out, key_out, value_out = refs[2 * size : 2 * size + 3]
    key_sum, value_sum, *scratch = refs[2 * size + 3 :]
    position = place[0]
    features = query.shape[2] // items.total
    factor = features**-0.5
    rows = []
    for head in range(items.total):
        parts = [(plan[head, position * size + position].astype(jnp.float32), 0, head)]
        for back in range(1, size):
            parts.append(far_part(items, position, plan, back, head, position, size - back))
        rows.append(parts)
    join(rows, totals, *scratch)
    joined = scratch[-1]

    def one_head(head):
        log, delta = joined[0, pl.ds(head, 1), :], joined[1, pl.ds(head, 1), :]
        weight = plan[head, position * size + position].astype(jnp.float32)
        probs, score_grad = one_weight(kept[head, 0], kept[head, 1], weight, log, delta)
        columns = columns_of(head, features)
        key_sum[head] = dot(score_grad, query[0, :, columns])
        value_sum[head] = dot(probs, grad[0, :, columns])
        query_out[head] = dot(score_grad, key[0, :, columns], TN) * factor

    by_groups(items.total, one_head)
    for index, (step, slot, head, weight) in enumerate(each_item(items, position, plan)):
        far = fars[step - 1]
        key_sum[head] += dot(made[index, 1], far[slot, 0])
        value_sum[head] += dot(made[index, 0], far[slot, 1])

    def one_sum(head):
        columns = columns_of(head, features)
        key_out[0, :, columns] = (key_sum[head] * factor).astype(jnp.bfloat16)
        value_out[0, :, columns] = value_sum[head].astype(jnp.bfloat16)

    by_groups(items.total, one_sum)


def run_own(items, place, plan, sources, kept, totals, fars, made):
    _, tokens, width = sources[0].shape
    features = width // items.total
    each = (items.total, tokens, features)
    query, key, _, grad = sources
    return pl.pallas_call(
        functools.partial(own_kernel, items),
        out_shape=[
            jax.ShapeDtypeStruct(each, jnp.float32),
            jax.ShapeDtypeStruct(query.shape, jnp.bfloat16),
            jax.ShapeDtypeStruct(query.shape, jnp.bfloat16),
        ],
        in_specs=[SMEM] * 2 + [VMEM] * (4 + 2 * items.size),
        out_specs=[VMEM] * 3,
        scratch_shapes=[pltpu.VMEM(each, jnp.float32)] * 2
        + join_scratch(items, items.total, tokens),
        compiler_params=PARAMS,
        cost_estimate=cost(items.total + items.count, 5, tokens),
        name="own",
    )(place, plan, query, key, grad, kept, *totals, *fars, made)


def query_kernel(items, place, plan, own_query, *refs):
    size = items.size
    backs, (out, held, sems) = refs[: size - 1], refs[size - 1 :]
    position = place[0]
    features = own_query.shape[2]
    group = math.gcd(items.total, 4)

    def copy(first):
        columns = pl.ds(pl.multiple_of(first * features, 128), group * features)
        return pltpu.make_async_copy(held.at[:, columns], out.at[0, :, columns], sems.at[first // group])

    def some(index, carry):
        for part in range(group):
            head = index * group + part
            total = own_query[head]
            for step in range(1, size):
                entry = position * size + lax.rem(position + step, size)
                used = plan[head, entry] > 0
                slot = jnp.minimum(plan[items.at.slots + head, entry], items.slots[step] - 1)
                total += jnp.where(used, backs[step - 1][slot].astype(jnp.float32), 0.0)
            held[:, columns_of(head, features)] = total.astype(jnp.bfloat16)
        copy(index * group).start()
        return carry

    lax.fori_loop(0, items.total // group, some, 0)
    for first in range(0, items.total, group):
        copy(first).wait()


def query_gradient(items, place, plan, own_query, backs, shape):
    return pl.pallas_call(
        functools.partial(query_kernel, items),
        out_shape=jax.ShapeDtypeStruct(shape, jnp.bfloat16),
        in_specs=[SMEM] * 2 + [VMEM] * items.size,
        out_specs=ANY,
        scratch_shapes=[
            pltpu.VMEM(shape[1:], jnp.bfloat16),
            pltpu.SemaphoreType.DMA((items.total // math.gcd(items.total, 4),)),
        ],
        compiler_params=PARAMS,
        name="query_gradient",
    )(place, plan, own_query, *backs)


def shared_kernel(items, place, plan, *refs):
    size = items.size
    parts, outs, sems = refs[:size], refs[size + 3 : size + 6], refs[-1]
    position = place[0]
    features = parts[0].shape[2]
    copies = []
    for step in range(size):
        columns = columns_of(plan[items.at.shared, lax.rem(position + step, size)], features)
        for index, out in enumerate(outs):
            copies.append(
                pltpu.make_async_copy(
                    parts[step].at[index], out.at[0, :, columns], sems.at[step, index]
                )
            )
    for copy in copies:
        copy.start()
    for copy in copies:
        copy.wait()


def put_shared(items, place, plan, parts, grads):
    first = 2 + len(parts)
    return pl.pallas_call(
        functools.partial(shared_kernel, items),
        out_shape=[jax.ShapeDtypeStruct(grad.shape, jnp.bfloat16) for grad in grads],
        in_specs=[SMEM] * 2 + [VMEM] * len(parts) + [ANY] * 3,
        out_specs=[ANY] * 3,
        scratch_shapes=[pltpu.SemaphoreType.DMA((items.size, 3))],
        input_output_aliases={first + index: index for index in range(3)},
        compiler_params=PARAMS,
        name="put_shared",
    )(place, plan, *parts, *grads)


def items_plan(items, block, place, plan, sources):
    size = items.size
    width = sources[0].shape[2] // items.total
    packed = item_pack(items, place, plan, sources[0], sources[3])
    fars = [shift(packed[step - 1], step) for step in range(1, size)]
    shared_fars = send_group(size, width, items.at.shared, place, plan, sources, packed)
    own_totals, own_kept = run_own_totals(items.total, sources)
    totals, kept, *packets = run_totals(items, place, plan, sources, own_totals, fars)
    packets = [shift(packets[step - 1], step) for step in range(1, size)]
    made, *outs = run_items(items, place, plan, sources, kept, [totals, *packets], shared_fars)
    backs = [shift(outs[step - 1], -step) for step in range(1, size)]
    spot = plan[items.at.spot, :3]
    parts = run_heads(size, 1, block, spot, plan, sources, shared_fars, (made,))
    parts = [parts[0]] + [shift(parts[step], -step) for step in range(1, size)]
    own_query, *light = run_own(items, place, plan, sources, own_kept, [own_totals, *packets], fars, made)
    query_light = query_gradient(items, place, plan, own_query, backs, light[0].shape)
    return tuple(put_shared(items, place, plan, parts, (query_light, *light)))


def shards(query_states, key_states, value_states, out_grad, pattern, counts):
    size = lax.axis_size("seq")
    place = lax.axis_index("seq").astype(jnp.int32).reshape(1)
    heads, blocks, slots = pattern.shape
    block = query_states.shape[1] * size // blocks
    sources = (query_states, key_states, value_states, out_grad)

    def by_heads(*sources):
        uses = count_uses(pattern, counts)
        return dense_plan(size, heads, 1, block, place, uses, sources)

    if size > 4 or size % 2 or blocks != size or heads == 1:
        return by_heads(*sources)
    used = jnp.arange(slots, dtype=jnp.int32) < counts[:, :, None]
    named = jnp.where(used, pattern, size * blocks)
    parts = [named] + [shift(named, step) for step in range(1, size)]
    plan, choice = make_plan(size, heads, place, parts)

    def by_items(odd, even):
        items = Items(size, size * heads, odd, even)
        return lambda *sources: items_plan(items, block, place, plan, sources)

    branches = [by_items(odd, even) for odd, even in SIZES] + [by_heads]
    return lax.switch(choice[0], branches, *sources)


def solution(mesh):
    tokens = P(("groups", "mp", "rep"), "seq", None)
    return jax.shard_map(
        shards,
        mesh=mesh,
        in_specs=(tokens, tokens, tokens, tokens, P("seq", None, None), P("seq", None)),
        out_specs=(tokens, tokens, tokens),
        check_vma=False,
    )
```

```python
import functools
import math

import jax
import jax.numpy as jnp
from jax import lax
from jax.experimental import pallas as pl
from jax.experimental.pallas import tpu as pltpu
from jax.sharding import PartitionSpec as P

LOG2E = math.log2(math.e)
NT = (((1,), (1,)), ((), ()))
NN = (((1,), (0,)), ((), ()))
TN = (((0,), (0,)), ((), ()))
VMEM_LIMIT = 32 * 1024 * 1024
SMEM = pl.BlockSpec(memory_space=pltpu.SMEM)
ANY = pl.BlockSpec(memory_space=pl.ANY)
VMEM = pl.BlockSpec(memory_space=pltpu.VMEM)
PARAMS = pltpu.CompilerParams(vmem_limit_bytes=VMEM_LIMIT)
LITTLE = pltpu.CompilerParams(vmem_limit_bytes=4 * 1024 * 1024)
SIZES = ((3, 2), (3, 3), (4, 3), (4, 4), (5, 5))


def dot(left, right, dims=NN):
    return lax.dot_general(left, right, dims, preferred_element_type=jnp.float32)


def shift(array, step):
    size = lax.axis_size("seq")
    return lax.ppermute(array, "seq", [(j, (j + step) % size) for j in range(size)])


def table_kernel(heads, blocks, slots, pattern, counts, table):
    def one_row(index, carry):
        head, row = index // blocks, index % blocks
        count = counts[head, row]
        named = [jnp.where(slot < count, pattern[head, row, slot], blocks) for slot in range(slots)]
        for column in range(blocks):
            table[head, row * blocks + column] = sum((n == column).astype(jnp.int32) for n in named)
        return carry

    if heads * blocks > 16:
        lax.fori_loop(0, heads * blocks, one_row, 0)
    else:
        for index in range(heads * blocks):
            one_row(index, 0)


def count_uses(pattern, counts):
    heads, blocks, slots = pattern.shape
    return pl.pallas_call(
        functools.partial(table_kernel, heads, blocks, slots),
        out_shape=jax.ShapeDtypeStruct((heads, blocks * blocks), jnp.int32),
        in_specs=[SMEM] * 2,
        out_specs=SMEM,
        name="count_uses",
    )(pattern, counts)


class Rows:
    def __init__(self, total):
        self.slots = total
        self.lists = 2 * total
        self.tallies = self.lists + max(max(pair) for pair in SIZES)
        self.shared = self.tallies + 1
        self.spot = self.shared + 1
        self.count = -(-(self.spot + 1) // 8) * 8


def plan_kernel(size, heads, place, *refs):
    parts, (plan, choice, held) = refs[:size], refs[size:]
    position = place[0]
    total, pairs = size * heads, size * size
    rows = Rows(total)
    count = parts[0].shape[-1]
    for step in range(size):
        for row in range(size):
            named = parts[step][:, row, :].astype(jnp.float32)
            held[pl.ds(step * heads, heads), pl.ds(row * count, count)] = named
    head = lax.broadcasted_iota(jnp.int32, (total, total), 0)
    place_of = lax.broadcasted_iota(jnp.int32, (total, total), 1)
    step = sum((place_of >= heads * k).astype(jnp.int32) for k in range(1, size))
    owner = position - step
    owner += jnp.where(owner < 0, size, 0)
    order = (head == owner * heads + place_of - step * heads).astype(jnp.float32)
    named = dot(order, held[...])
    head = lax.broadcasted_iota(jnp.int32, (total, pairs), 0)
    pair = lax.broadcasted_iota(jnp.int32, (total, pairs), 1)
    table = jnp.zeros((total, pairs), jnp.float32)
    for row in range(size):
        column = (pair - row * size).astype(jnp.float32)
        for slot in range(row * count, (row + 1) * count):
            table += jnp.where(column == named[:, slot : slot + 1], 1.0, 0.0)
    plan[pl.ds(0, total), :] = table.astype(jnp.int32)

    uses = (table > 0).astype(jnp.float32)
    for block in range(size):
        uses = jnp.where(pair == block * (size + 1), 0.0, uses)
    lane = lax.broadcasted_iota(jnp.int32, (1, pairs), 1)
    shared, mine = jnp.zeros((1, pairs), jnp.int32), jnp.zeros((1, 1), jnp.int32)
    odd = functools.reduce(
        jnp.logical_or, [lane == i * size + j for i in range(size) for j in range(size) if (i - j) % 2]
    )
    number = head[:, :1].astype(jnp.float32)
    free = number >= 0
    for index in range(size):
        load = jnp.sum(uses, axis=0, keepdims=True) + jnp.where(odd, 0.0, 0.6)
        load = load * load * load
        score = jnp.sum(uses * (load * load), axis=1, keepdims=True)
        score = jnp.where(free, score, -1.0)
        top = jnp.max(score, axis=0, keepdims=True)
        name = jnp.max(jnp.where(score == top, number, -1.0), axis=0, keepdims=True)
        uses = jnp.where(number == name, 0.0, uses)
        free = free & (number != name)
        shared = jnp.where(lane == index, name.astype(jnp.int32), shared)
        mine = jnp.where(index == position, name.astype(jnp.int32), mine)
    earlier = lax.broadcasted_iota(jnp.int32, (total, total), 1) < lax.broadcasted_iota(jnp.int32, (total, total), 0)
    slots = dot(earlier.astype(jnp.float32), uses)
    tallies = jnp.sum(uses, axis=0, keepdims=True)
    plan[pl.ds(rows.slots, total), :] = slots.astype(jnp.int32)
    for slot in range(rows.tallies - rows.lists):
        hit = jnp.where(slots == slot, uses * head.astype(jnp.float32), 0.0)
        plan[pl.ds(rows.lists + slot, 1), :] = jnp.sum(hit, axis=0, keepdims=True).astype(jnp.int32)
    plan[pl.ds(rows.tallies, 1), :] = tallies.astype(jnp.int32)
    plan[pl.ds(rows.shared, 1), :] = shared
    plan[pl.ds(rows.spot, 1), :] = jnp.where(lane == 0, position, mine)

    most_odd = jnp.max(jnp.where(odd, tallies, 0.0)).astype(jnp.int32)
    most_even = jnp.max(jnp.where(odd, 0.0, tallies)).astype(jnp.int32)
    chosen = jnp.int32(len(SIZES))
    for index in reversed(range(len(SIZES))):
        fits = (most_odd <= SIZES[index][0]) & (most_even <= SIZES[index][1])
        chosen = jnp.where(fits, index, chosen)
    choice[0] = chosen


def make_plan(size, heads, place, parts):
    total, pairs = size * heads, size * size
    return pl.pallas_call(
        functools.partial(plan_kernel, size, heads),
        out_shape=[
            jax.ShapeDtypeStruct((Rows(total).count, pairs), jnp.int32),
            jax.ShapeDtypeStruct((1,), jnp.int32),
        ],
        in_specs=[SMEM] + [VMEM] * size,
        out_specs=[VMEM, SMEM],
        scratch_shapes=[pltpu.VMEM((total, size * parts[0].shape[2]), jnp.float32)],
        compiler_params=LITTLE,
        name="make_plan",
    )(place, *parts)


def pack_kernel(size, width, row, place, starts, *refs):
    sources, outs, (held, in_sems, out_sems) = refs[:4], refs[-2 - size : -3], refs[-3:]
    position = place[0]
    reads, writes = [], []
    for step in range(1, size):
        start = starts[row, lax.rem(position + step, size)] * width
        columns = pl.ds(pl.multiple_of(start, 128), width)
        reads.append(
            [
                pltpu.make_async_copy(
                    source.at[0, :, columns], held.at[step - 1, index], in_sems.at[step - 1, index]
                )
                for index, source in enumerate(sources)
            ]
        )
        writes.append(pltpu.make_async_copy(held.at[step - 1], outs[step - 1], out_sems.at[step - 1]))
    for read in sum(reads, []):
        read.start()
    for read, write in zip(reads, writes):
        for one in read:
            one.wait()
        write.start()
    for write in writes:
        write.wait()


def pack(size, width, row, place, starts, sources, after):
    tokens = sources[0].shape[1]
    return pl.pallas_call(
        functools.partial(pack_kernel, size, width, row),
        out_shape=[jax.ShapeDtypeStruct((4, tokens, width), jnp.bfloat16)] * (size - 1),
        in_specs=[SMEM] * 2 + [ANY] * (4 + len(after)),
        out_specs=[ANY] * (size - 1),
        scratch_shapes=[
            pltpu.VMEM((size - 1, 4, tokens, width), jnp.bfloat16),
            pltpu.SemaphoreType.DMA((size - 1, 4)),
            pltpu.SemaphoreType.DMA((size - 1,)),
        ],
        compiler_params=PARAMS,
        name="pack",
    )(place, starts, *sources, *after)


def heads_kernel(size, heads, block, spot, uses, *refs):
    own_refs, far_refs = refs[:4], refs[4 : 3 + size]
    out_refs = refs[-4 - size : -4]
    joined, key_flip, key_sum, value_sum = refs[-4:]
    position, first = spot[0], spot[2]
    tokens, features = own_refs[0].shape[1], joined.shape[2]
    length = size * tokens
    blocks = length // block
    local = tokens // block
    chunk = min(length, max(2 * block, 256))
    factor = features**-0.5

    def origin(index):
        return lax.rem(position + size - index // local, size) * local + index % local

    def one_chunk(head, number):
        start = pl.multiple_of(number * chunk, chunk)
        rows = pl.ds(start, chunk)
        query, grad = joined[0, rows, :], joined[3, rows, :]
        scores = dot(joined[1], query, NT)
        prob_grad = dot(joined[2], grad, NT)
        weight_parts, score_parts = [], []
        for part in range(chunk // block):
            row = origin(number * (chunk // block) + part)
            columns = slice(part * block, (part + 1) * block)
            counts = [
                uses[first + head, row * blocks + origin(j)].astype(jnp.float32) for j in range(blocks)
            ]
            terms = []
            for j in range(blocks):
                term = scores[j * block : (j + 1) * block, columns] * (factor * LOG2E)
                terms.append(term + jnp.where(counts[j] > 0, 0.0, -jnp.inf))
            top = functools.reduce(jnp.maximum, terms)
            top = jnp.max(top, axis=0, keepdims=True)
            exps = [jnp.exp2(term - top) for term in terms]
            grads = [prob_grad[j * block : (j + 1) * block, columns] for j in range(blocks)]
            total = sum(count * e for count, e in zip(counts, exps))
            moment = sum(count * (e * g) for count, e, g in zip(counts, exps, grads))
            inverse = 1.0 / jnp.sum(total, axis=0, keepdims=True)
            delta = jnp.sum(moment, axis=0, keepdims=True) * inverse
            probs = [e * (inverse * count) for count, e in zip(counts, exps)]
            weight_parts.append(jnp.concatenate([p.astype(jnp.bfloat16) for p in probs], axis=0))
            score_parts.append(
                jnp.concatenate(
                    [(p * (g - delta)).astype(jnp.bfloat16) for p, g in zip(probs, grads)], axis=0
                )
            )
        weights = jnp.concatenate(weight_parts, axis=1)
        score_grad = jnp.concatenate(score_parts, axis=1)
        key_sum[...] += dot(score_grad, query)
        value_sum[...] += dot(weights, grad)
        flipped = dot(key_flip[...], score_grad)
        return (flipped.T * factor).astype(jnp.bfloat16)

    def one_head(head, carry):
        features_at = columns_of(head, features)
        for index in range(4):
            joined[index, pl.ds(0, tokens), :] = own_refs[index][0, :, features_at]
            for step in range(1, size):
                joined[index, pl.ds(step * tokens, tokens), :] = far_refs[step - 1][index, :, features_at]
        key_flip[...] = joined[1].T
        key_sum[...] = jnp.zeros_like(key_sum)
        value_sum[...] = jnp.zeros_like(value_sum)

        for number in range(length // chunk):
            query_grad = one_chunk(head, number)
            for part in range(max(1, chunk // tokens)):
                step, within = divmod(number * chunk + part * tokens, tokens)
                span = min(chunk, tokens)
                out_refs[step][0, pl.ds(within, span), features_at] = query_grad[part * span : (part + 1) * span]
        for step in range(size):
            rows = pl.ds(step * tokens, tokens)
            out_refs[step][1, :, features_at] = (factor * key_sum[rows, :]).astype(jnp.bfloat16)
            out_refs[step][2, :, features_at] = value_sum[rows, :].astype(jnp.bfloat16)
        return carry

    if heads == 1:
        one_head(0, 0)
    else:
        lax.fori_loop(0, heads, one_head, 0)


def run_heads(size, heads, block, spot, uses, owns, fars, after=()):
    tokens = owns[0].shape[1]
    features = fars[0].shape[2] // heads
    width = heads * features
    length = size * tokens
    own_spec = pl.BlockSpec((1, tokens, width), lambda i, spot: (0, 0, spot[1]))
    far_spec = pl.BlockSpec((4, tokens, width), lambda i, spot: (0, 0, 0))
    out_spec = pl.BlockSpec((3, tokens, width), lambda i, spot: (0, 0, 0))
    return pl.pallas_call(
        functools.partial(heads_kernel, size, heads, block),
        grid_spec=pltpu.PrefetchScalarGridSpec(
            num_scalar_prefetch=1,
            grid=(1,),
            in_specs=[SMEM] + [own_spec] * 4 + [far_spec] * (size - 1) + [ANY] * len(after),
            out_specs=[out_spec] * size,
            scratch_shapes=[
                pltpu.VMEM((4, length, features), jnp.bfloat16),
                pltpu.VMEM((features, length), jnp.bfloat16),
                pltpu.VMEM((length, features), jnp.float32),
                pltpu.VMEM((length, features), jnp.float32),
            ],
        ),
        out_shape=[jax.ShapeDtypeStruct((3, tokens, width), jnp.bfloat16)] * size,
        compiler_params=PARAMS,
        cost_estimate=pl.CostEstimate(
            flops=heads * 10 * length * length * features,
            bytes_accessed=heads * 14 * length * features,
            transcendentals=heads * length * length,
        ),
        name="heads",
    )(spot, uses, *owns, *fars, *after)


def place_kernel(size, groups, width, place, *refs):
    parts, outs = refs[: size * groups], refs[size * groups : -3]
    held, in_sems, out_sems = refs[-3:]
    position = place[0]
    total = outs[0].shape[2]
    reads, writes = [], []
    for step in range(size):
        start = pl.multiple_of(lax.rem(position + step, size) * (total // size), 128)
        reads.append(
            [
                pltpu.make_async_copy(
                    parts[group * size + step],
                    held.at[step, :, :, pl.ds(group * width, width)],
                    in_sems.at[step, group],
                )
                for group in range(groups)
            ]
        )
        writes.append(
            [
                pltpu.make_async_copy(
                    held.at[step, index],
                    out.at[0, :, pl.ds(start, total // size)],
                    out_sems.at[step, index],
                )
                for index, out in enumerate(outs)
            ]
        )
    for read in sum(reads, []):
        read.start()
    for read, write in zip(reads, writes):
        for one in read:
            one.wait()
        for one in write:
            one.start()
    for one in sum(writes, []):
        one.wait()


def put_in_place(size, groups, width, place, parts, shape):
    return pl.pallas_call(
        functools.partial(place_kernel, size, groups, width),
        out_shape=[jax.ShapeDtypeStruct(shape, jnp.bfloat16)] * 3,
        in_specs=[SMEM] + [ANY] * len(parts),
        out_specs=[ANY] * 3,
        scratch_shapes=[
            pltpu.VMEM((size, 3, shape[1], groups * width), jnp.bfloat16),
            pltpu.SemaphoreType.DMA((size, groups)),
            pltpu.SemaphoreType.DMA((size, 3)),
        ],
        compiler_params=PARAMS,
        name="put_in_place",
    )(place, *parts)


def send_group(size, width, row, place, starts, sources, after=()):
    packed = pack(size, width, row, place, starts, sources, after)
    return [shift(packed[step - 1], step) for step in range(1, size)]


def dense_plan(size, heads, groups, block, place, uses, sources):
    features = sources[0].shape[2] // (uses.shape[0] * size)
    width = heads * features
    parts = []
    for group in range(groups):
        starts = jnp.arange(size, dtype=jnp.int32)[None] * groups + group
        spot = jnp.concatenate([place, place * groups + group, jnp.full(1, group * heads, jnp.int32)])
        fars = send_group(size, width, 0, place, starts, sources)
        outs = run_heads(size, heads, block, spot, uses, sources, fars)
        parts.append(outs[0])
        parts += [shift(outs[step], -step) for step in range(1, size)]
    return tuple(put_in_place(size, groups, width, place, parts, sources[0].shape))


class Items:
    def __init__(self, size, total, odd, even):
        self.size, self.total, self.at = size, total, Rows(total)
        self.slots = {step: odd if step % 2 else even for step in range(1, size)}
        self.first, self.count = {}, 0
        for step in range(1, size):
            self.first[step] = self.count
            self.count += self.slots[step]
        self.rows = {step: -(-(self.slots[step] + self.count) // 8) * 8 for step in self.slots}


def item_pack_kernel(items, place, plan, query, grad, *outs):
    size = items.size
    position = place[0]
    features = outs[0].shape[-1]
    for step in range(1, size):
        pair = position * size + lax.rem(position + step, size)
        tally = plan[items.at.tallies, pair]
        for slot in range(items.slots[step]):
            head = jnp.where(slot < tally, plan[items.at.lists + slot, pair], 0)
            columns = columns_of(head, features)
            outs[step - 1][slot, 0] = query[0, :, columns]
            outs[step - 1][slot, 1] = grad[0, :, columns]


def item_pack(items, place, plan, query, grad):
    tokens = query.shape[1]
    features = query.shape[2] // items.total
    return pl.pallas_call(
        functools.partial(item_pack_kernel, items),
        out_shape=[
            jax.ShapeDtypeStruct((items.slots[step], 2, tokens, features), jnp.bfloat16)
            for step in range(1, items.size)
        ],
        in_specs=[SMEM] * 2 + [VMEM] * 2,
        out_specs=[VMEM] * (items.size - 1),
        compiler_params=PARAMS,
        name="item_pack",
    )(place, plan, query, grad)


def each_item(items, position, plan):
    for step in range(1, items.size):
        origin = lax.rem(position + items.size - step, items.size)
        pair = origin * items.size + position
        tally = plan[items.at.tallies, pair]
        for slot in range(items.slots[step]):
            real = slot < tally
            head = jnp.where(real, plan[items.at.lists + slot, pair], 0)
            weight = jnp.where(real, plan[head, pair], 0).astype(jnp.float32)
            yield step, slot, head, weight


def columns_of(head, features):
    if isinstance(head, int):
        return pl.ds(head * features, features)
    return pl.ds(pl.multiple_of(head * features, features), features)


def by_groups(count, one, straight=8):
    straight = math.gcd(count, straight)

    def some(index, carry):
        for part in range(straight):
            one(index * straight + part)
        return carry

    lax.fori_loop(0, count // straight, some, 0)


def cost(blocks, products, side):
    return pl.CostEstimate(
        flops=2 * blocks * products * side**3,
        bytes_accessed=8 * blocks * side * side,
        transcendentals=blocks * side * side,
    )


def products(keys, values, queries, grads):
    factor = keys.shape[1] ** -0.5
    return dot(keys, queries, NT) * (factor * LOG2E), dot(values, grads, NT)


def one_total(scores, prob_grad):
    top = jnp.max(scores, axis=0, keepdims=True)
    exps = jnp.exp2(scores - top)
    total = jnp.sum(exps, axis=0, keepdims=True)
    moment = jnp.sum(exps * prob_grad, axis=0, keepdims=True)
    return top + jnp.log2(total), moment / total


def one_weight(scores, prob_grad, weight, log, delta):
    probs = jnp.exp2(scores - log) * weight
    return probs.astype(jnp.bfloat16), (probs * (prob_grad - delta)).astype(jnp.bfloat16)


def own_totals_kernel(total, query, key, value, grad, out, kept):
    features = query.shape[2] // total

    def one_head(head):
        columns = columns_of(head, features)
        block = [ref[0, :, columns] for ref in (key, value, query, grad)]
        scores, prob_grad = products(*block)
        kept[head, 0], kept[head, 1] = scores, prob_grad
        out[0, pl.ds(head, 1), :], out[1, pl.ds(head, 1), :] = one_total(scores, prob_grad)

    by_groups(total, one_head)


def run_own_totals(total, sources):
    tokens = sources[0].shape[1]
    return pl.pallas_call(
        functools.partial(own_totals_kernel, total),
        out_shape=[
            jax.ShapeDtypeStruct((2, total, tokens), jnp.float32),
            jax.ShapeDtypeStruct((total, 2, tokens, tokens), jnp.float32),
        ],
        in_specs=[VMEM] * 4,
        out_specs=[VMEM] * 2,
        compiler_params=PARAMS,
        cost_estimate=cost(total, 2, tokens),
        name="own_totals",
    )(*sources)


def totals_kernel(items, place, plan, key, value, own, *refs):
    size = items.size
    far_refs, (out, kept, *packets) = refs[: size - 1], refs[size - 1 :]
    position = place[0]
    features = key.shape[2] // items.total
    for step, packet in enumerate(packets, 1):
        pair = position * size + lax.rem(position + step, size)
        tally = plan[items.at.tallies, pair]
        for slot in range(items.slots[step]):
            head = jnp.where(slot < tally, plan[items.at.lists + slot, pair], 0)
            for plane in range(2):
                packet[plane, pl.ds(slot, 1), :] = own[plane, pl.ds(head, 1), :]
    for index, (step, slot, head, _) in enumerate(each_item(items, position, plan)):
        columns = columns_of(head, features)
        far = far_refs[step - 1]
        scores, prob_grad = products(key[0, :, columns], value[0, :, columns], far[slot, 0], far[slot, 1])
        kept[index, 0], kept[index, 1] = scores, prob_grad
        for plane, total in enumerate(one_total(scores, prob_grad)):
            out[plane, pl.ds(index, 1), :] = total
            for back, packet in enumerate(packets, 1):
                packet[plane, pl.ds(items.slots[back] + index, 1), :] = total


def run_totals(items, place, plan, sources, own, fars):
    tokens = sources[0].shape[1]
    rows = [-(-items.count // 8) * 8] + [items.rows[step] for step in range(1, items.size)]
    totals = [jax.ShapeDtypeStruct((2, count, tokens), jnp.float32) for count in rows]
    kept = jax.ShapeDtypeStruct((items.count, 2, tokens, tokens), jnp.float32)
    return pl.pallas_call(
        functools.partial(totals_kernel, items),
        out_shape=[totals[0], kept, *totals[1:]],
        in_specs=[SMEM] * 2 + [VMEM] * (2 + items.size),
        out_specs=[VMEM] * (1 + items.size),
        compiler_params=PARAMS,
        cost_estimate=cost(items.count, 2, tokens),
        name="totals",
    )(place, plan, *sources[1:3], own, *fars)


def far_part(items, position, plan, back, head, origin, gap, slot=None):
    column = lax.rem(position + items.size - back, items.size)
    entry = origin * items.size + column
    weight = plan[head, entry].astype(jnp.float32)
    if gap == 0:
        return weight, back, slot
    row = jnp.minimum(plan[items.at.slots + head, entry], items.slots[gap] - 1)
    return weight, back, items.slots[back] + items.first[gap] + row


def join(rows, totals, logs, means, shares, joined):
    for index, parts in enumerate(rows):
        at = pl.ds(index, 1)
        for part, (weight, back, row) in enumerate(parts):
            log = totals[back][0, pl.ds(row, 1), :]
            logs[part, at, :] = jnp.where(weight > 0, log, -jnp.inf)
            means[part, at, :] = totals[back][1, pl.ds(row, 1), :]
            shares[part, at, :] = jnp.broadcast_to(weight, log.shape)
    count = logs.shape[0]
    top = functools.reduce(jnp.maximum, [logs[part] for part in range(count)])
    weights = [shares[part] * jnp.exp2(logs[part] - top) for part in range(count)]
    total = sum(weights)
    joined[0] = top + jnp.log2(total)
    joined[1] = sum(weight * means[part] for part, weight in enumerate(weights)) / total


def join_scratch(items, count, tokens):
    rows = -(-count // 8) * 8
    part = pltpu.VMEM((items.size, rows, tokens), jnp.float32)
    return [part, part, part, pltpu.VMEM((2, rows, tokens), jnp.float32)]


def items_kernel(items, place, plan, key, kept, *refs):
    size = items.size
    totals, refs = refs[:size], refs[-4 - size :]
    made, item_outs, scratch = refs[0], refs[1:size], refs[size:]
    position = place[0]
    features = key.shape[2] // items.total
    factor = features**-0.5
    arrived = list(each_item(items, position, plan))
    rows = []
    for index, (step, slot, head, weight) in enumerate(arrived):
        origin = lax.rem(position + size - step, size)
        parts = [(weight, 0, index)]
        for back in range(1, size):
            gap = (step - back) % size
            parts.append(far_part(items, position, plan, back, head, origin, gap, slot))
        rows.append(parts)
    join(rows, totals, *scratch)
    joined = scratch[-1]
    for index, (step, slot, head, weight) in enumerate(arrived):
        log, delta = joined[0, pl.ds(index, 1), :], joined[1, pl.ds(index, 1), :]
        log = jnp.where(weight > 0, log, jnp.inf)
        probs, score_grad = one_weight(kept[index, 0], kept[index, 1], weight, log, delta)
        made[index, 0], made[index, 1] = probs, score_grad
        query_term = dot(score_grad, key[0, :, columns_of(head, features)], TN) * factor
        item_outs[step - 1][slot] = query_term.astype(jnp.bfloat16)


def run_items(items, place, plan, sources, kept, totals, after):
    _, tokens, width = sources[0].shape
    features = width // items.total
    outs = [jax.ShapeDtypeStruct(kept.shape, jnp.bfloat16)]
    for step in range(1, items.size):
        outs.append(jax.ShapeDtypeStruct((items.slots[step], tokens, features), jnp.bfloat16))
    return pl.pallas_call(
        functools.partial(items_kernel, items),
        out_shape=outs,
        in_specs=[SMEM] * 2 + [VMEM] * (2 + items.size) + [ANY] * len(after),
        out_specs=[VMEM] * len(outs),
        scratch_shapes=join_scratch(items, items.count, tokens),
        compiler_params=PARAMS,
        cost_estimate=cost(items.count, 5, tokens),
        name="items",
    )(place, plan, sources[1], kept, *totals, *after)


def own_kernel(items, place, plan, query, key, grad, kept, *refs):
    size = items.size
    totals, fars, made = refs[:size], refs[size : 2 * size - 1], refs[2 * size - 1]
    query_out, key_out, value_out = refs[2 * size : 2 * size + 3]
    key_sum, value_sum, *scratch = refs[2 * size + 3 :]
    position = place[0]
    features = query.shape[2] // items.total
    factor = features**-0.5
    rows = []
    for head in range(items.total):
        parts = [(plan[head, position * size + position].astype(jnp.float32), 0, head)]
        for back in range(1, size):
            parts.append(far_part(items, position, plan, back, head, position, size - back))
        rows.append(parts)
    join(rows, totals, *scratch)
    joined = scratch[-1]

    def one_head(head):
        log, delta = joined[0, pl.ds(head, 1), :], joined[1, pl.ds(head, 1), :]
        weight = plan[head, position * size + position].astype(jnp.float32)
        probs, score_grad = one_weight(kept[head, 0], kept[head, 1], weight, log, delta)
        columns = columns_of(head, features)
        key_sum[head] = dot(score_grad, query[0, :, columns])
        value_sum[head] = dot(probs, grad[0, :, columns])
        query_out[head] = dot(score_grad, key[0, :, columns], TN) * factor

    by_groups(items.total, one_head)
    for index, (step, slot, head, weight) in enumerate(each_item(items, position, plan)):
        far = fars[step - 1]
        key_sum[head] += dot(made[index, 1], far[slot, 0])
        value_sum[head] += dot(made[index, 0], far[slot, 1])

    def one_sum(head):
        columns = columns_of(head, features)
        key_out[0, :, columns] = (key_sum[head] * factor).astype(jnp.bfloat16)
        value_out[0, :, columns] = value_sum[head].astype(jnp.bfloat16)

    by_groups(items.total, one_sum)


def run_own(items, place, plan, sources, kept, totals, fars, made):
    _, tokens, width = sources[0].shape
    features = width // items.total
    each = (items.total, tokens, features)
    query, key, _, grad = sources
    return pl.pallas_call(
        functools.partial(own_kernel, items),
        out_shape=[
            jax.ShapeDtypeStruct(each, jnp.float32),
            jax.ShapeDtypeStruct(query.shape, jnp.bfloat16),
            jax.ShapeDtypeStruct(query.shape, jnp.bfloat16),
        ],
        in_specs=[SMEM] * 2 + [VMEM] * (4 + 2 * items.size),
        out_specs=[VMEM] * 3,
        scratch_shapes=[pltpu.VMEM(each, jnp.float32)] * 2
        + join_scratch(items, items.total, tokens),
        compiler_params=PARAMS,
        cost_estimate=cost(items.total + items.count, 5, tokens),
        name="own",
    )(place, plan, query, key, grad, kept, *totals, *fars, made)


def query_kernel(items, place, plan, own_query, *refs):
    size = items.size
    backs, light = refs[: size - 1], refs[size - 1 : size + 1]
    out, *light_outs, held, sems, light_sems = refs[size + 1 :]
    writes = [
        pltpu.make_async_copy(source, target, light_sems.at[index])
        for index, (source, target) in enumerate(zip(light, light_outs))
    ]
    for write in writes:
        write.start()
    position = place[0]
    features = own_query.shape[2]
    group = math.gcd(items.total, 4)

    def copy(first):
        columns = pl.ds(pl.multiple_of(first * features, 128), group * features)
        return pltpu.make_async_copy(held.at[:, columns], out.at[0, :, columns], sems.at[first // group])

    def some(index, carry):
        for part in range(group):
            head = index * group + part
            total = own_query[head]
            for step in range(1, size):
                entry = position * size + lax.rem(position + step, size)
                used = plan[head, entry] > 0
                slot = jnp.minimum(plan[items.at.slots + head, entry], items.slots[step] - 1)
                total += jnp.where(used, backs[step - 1][slot].astype(jnp.float32), 0.0)
            held[:, columns_of(head, features)] = total.astype(jnp.bfloat16)
        copy(index * group).start()
        return carry

    lax.fori_loop(0, items.total // group, some, 0)
    for first in range(0, items.total, group):
        copy(first).wait()
    for write in writes:
        write.wait()


def query_gradient(items, place, plan, own_query, backs, light):
    shape = light[0].shape
    return pl.pallas_call(
        functools.partial(query_kernel, items),
        out_shape=[jax.ShapeDtypeStruct(shape, jnp.bfloat16)] * 3,
        in_specs=[SMEM] * 2 + [VMEM] * (items.size + 2),
        out_specs=[ANY] * 3,
        scratch_shapes=[
            pltpu.VMEM(shape[1:], jnp.bfloat16),
            pltpu.SemaphoreType.DMA((items.total // math.gcd(items.total, 4),)),
            pltpu.SemaphoreType.DMA((2,)),
        ],
        compiler_params=PARAMS,
        name="query_gradient",
    )(place, plan, own_query, *backs, *light)


def shared_kernel(items, place, plan, *refs):
    size = items.size
    parts, outs, sems = refs[:size], refs[size + 3 : size + 6], refs[-1]
    position = place[0]
    features = parts[0].shape[2]
    copies = []
    for step in range(size):
        columns = columns_of(plan[items.at.shared, lax.rem(position + step, size)], features)
        for index, out in enumerate(outs):
            copies.append(
                pltpu.make_async_copy(
                    parts[step].at[index], out.at[0, :, columns], sems.at[step, index]
                )
            )
    for copy in copies:
        copy.start()
    for copy in copies:
        copy.wait()


def put_shared(items, place, plan, parts, grads):
    first = 2 + len(parts)
    return pl.pallas_call(
        functools.partial(shared_kernel, items),
        out_shape=[jax.ShapeDtypeStruct(grad.shape, jnp.bfloat16) for grad in grads],
        in_specs=[SMEM] * 2 + [VMEM] * len(parts) + [ANY] * 3,
        out_specs=[ANY] * 3,
        scratch_shapes=[pltpu.SemaphoreType.DMA((items.size, 3))],
        input_output_aliases={first + index: index for index in range(3)},
        compiler_params=PARAMS,
        name="put_shared",
    )(place, plan, *parts, *grads)


def items_plan(items, block, place, plan, sources):
    size = items.size
    width = sources[0].shape[2] // items.total
    packed = item_pack(items, place, plan, sources[0], sources[3])
    fars = [shift(packed[step - 1], step) for step in range(1, size)]
    shared_fars = send_group(size, width, items.at.shared, place, plan, sources, packed)
    own_totals, own_kept = run_own_totals(items.total, sources)
    totals, kept, *packets = run_totals(items, place, plan, sources, own_totals, fars)
    packets = [shift(packets[step - 1], step) for step in range(1, size)]
    made, *outs = run_items(items, place, plan, sources, kept, [totals, *packets], shared_fars)
    backs = [shift(outs[step - 1], -step) for step in range(1, size)]
    spot = plan[items.at.spot, :3]
    parts = run_heads(size, 1, block, spot, plan, sources, shared_fars, (made,))
    parts = [parts[0]] + [shift(parts[step], -step) for step in range(1, size)]
    own_query, *light = run_own(items, place, plan, sources, own_kept, [own_totals, *packets], fars, made)
    grads = query_gradient(items, place, plan, own_query, backs, light)
    return tuple(put_shared(items, place, plan, parts, grads))


def shards(query_states, key_states, value_states, out_grad, pattern, counts):
    size = lax.axis_size("seq")
    place = lax.axis_index("seq").astype(jnp.int32).reshape(1)
    heads, blocks, slots = pattern.shape
    block = query_states.shape[1] * size // blocks
    sources = (query_states, key_states, value_states, out_grad)

    def by_heads(*sources):
        uses = count_uses(pattern, counts)
        return dense_plan(size, heads, 1, block, place, uses, sources)

    if size > 4 or size % 2 or blocks != size or heads == 1:
        return by_heads(*sources)
    used = jnp.arange(slots, dtype=jnp.int32) < counts[:, :, None]
    named = jnp.where(used, pattern, size * blocks)
    parts = [named] + [shift(named, step) for step in range(1, size)]
    plan, choice = make_plan(size, heads, place, parts)

    def by_items(odd, even):
        items = Items(size, size * heads, odd, even)
        return lambda *sources: items_plan(items, block, place, plan, sources)

    branches = [by_items(odd, even) for odd, even in SIZES] + [by_heads]
    return lax.switch(choice[0], branches, *sources)


def solution(mesh):
    tokens = P(("groups", "mp", "rep"), "seq", None)
    return jax.shard_map(
        shards,
        mesh=mesh,
        in_specs=(tokens, tokens, tokens, tokens, P("seq", None, None), P("seq", None)),
        out_specs=(tokens, tokens, tokens),
        check_vma=False,
    )
```
